32 devices in a mesh: frames: 2 (over y), patches: 16 (over z, x, core).
Axes of the slice: x: 2, y: 2, z: 4, core: 2. Of those that a mesh axis runs over, the one named last changes fastest.
Arguments:
- tokens: bfloat16 [18, 1536, 1152], P('frames', 'patches'), may hold values from -6 to 6
- cotangent: bfloat16 [18, 1536, 1152], P('frames', 'patches'), may hold values from -6 to 6
- caption: bfloat16 [4, 120, 1152], replicated, may hold values from -6 to 6
- null_embed: bfloat16 [120, 1152], replicated, may hold values from -6 to 6
- timesteps: int32 [4], replicated, may hold values from 0 to 999
- null_mask: int32 [4], replicated, may hold values from 0 to 1, as said below
- bucket_sizes: int32 [4], replicated, may hold values from 1 to 576, 1536 in all
- patch_mask: int32 [1536], P('patches'), may hold values 0 or 1
- frame_counts: int32 [2], P('frames'), may hold values from 1 to 9, 17 in all
- table: bfloat16 [6, 1152], replicated, may hold values from -3 to 3
- time_proj: bfloat16 [256, 6912], P('patches', 'frames'), may hold values from -0.375 to 0.375
- self_qkv: bfloat16 [1152, 3456], P('patches', 'frames'), may hold values from -0.1875 to 0.1875
- self_out: bfloat16 [1152, 1152], P('patches', 'frames'), may hold values from -0.25 to 0.25
- cross_q: bfloat16 [1152, 1152], P('patches', 'frames'), may hold values from -0.1875 to 0.1875
- cross_kv: bfloat16 [1152, 2304], P('patches', 'frames'), may hold values from -0.1875 to 0.1875
- cross_out: bfloat16 [1152, 1152], P('patches', 'frames'), may hold values from -0.75 to 0.75
- mlp_in: bfloat16 [1152, 4608], P('patches', 'frames'), may hold values from -0.1875 to 0.1875
- mlp_out: bfloat16 [4608, 1152], P('patches', 'frames'), may hold values from -0.09375 to 0.09375
- biases: bfloat16 [7, 1152], replicated, may hold values from -3 to 3
- hidden_bias: bfloat16 [4608], replicated, may hold values from -3 to 3
Outputs:
- block_out: bfloat16 [18, 1536, 1152], P('frames', 'patches')
- input_grad: float32 [18, 1536, 1152], P('frames', 'patches')
- caption_grad: float32 [4, 120, 1152], replicated
- null_grad: float32 [120, 1152], replicated
- table_grad: float32 [6, 1152], replicated
- time_proj_grad: float32 [256, 6912], P('patches', 'frames')
- self_qkv_grad: float32 [1152, 3456], P('patches', 'frames')
- self_out_grad: float32 [1152, 1152], P('patches', 'frames')
- cross_q_grad: float32 [1152, 1152], P('patches', 'frames')
- cross_kv_grad: float32 [1152, 2304], P('patches', 'frames')
- cross_out_grad: float32 [1152, 1152], P('patches', 'frames')
- mlp_in_grad: float32 [1152, 4608], P('patches', 'frames')
- mlp_out_grad: float32 [4608, 1152], P('patches', 'frames')
- biases_grad: float32 [7, 1152], replicated
- hidden_bias_grad: float32 [4608], replicated
The draws below stay inside these ranges and needn't reach their ends.
Inputs may be any that keep to these rules, and one draw needn't show every extreme that they name: `null_mask`: at least one clip and at most 2 clips take the null caption. `frame_counts`: the counts sum to 17; index i of frames holds the frames after those of lower indices. `bucket_sizes`: the sizes sum to 1536; clip c takes the positions after those of lower clips.
All inputs are finite; a program needn't handle non-finite values. No bound on the sum of `patch_mask` or of `frame_counts` on one device may be relied on, other than what follows from the above.
Results may differ from the reference program's by a relative error of at most 0.028.
Values may be sent and summed in bfloat16 or wider, within the bound.
A program may use at most 384 MiB of HBM per device.

```python
import math
import jax
import jax.numpy as jnp
import numpy as np
from jax import lax

D = 1152
HEADS = 16
FF = 4608
CAP = 120
TFREQ = 256
CLIPS = 4
CLIP_FRAMES = 17
FRAMES_DEV = 9
SLOTS = 18
PATCHES = 1536
BUCKET_MOST = 576
N_FRAMES = 2


def draw_null_mask(key, part):
    order = jax.random.permutation(key, CLIPS)
    dropped = jax.random.randint(jax.random.fold_in(key, 7), (), 1, CLIPS // 2 + 1)
    return (order < dropped).astype(jnp.int32)


def with_ends(values, rng, low, largest):
    longest = values.shape.index(max(values.shape))
    spots = []
    for shift in (0, 1):
        where = [jax.random.randint(jax.random.fold_in(rng, axis), (), 0, length) for axis, length in enumerate(values.shape)]
        where[longest] = (where[longest] + shift) % values.shape[longest]
        spots.append(tuple(where))
    return values.at[spots[0]].set(low).at[spots[1]].set(largest)


def block_levels(rng, extent, cuts, low, largest):
    loudness, own = 1.0, jax.random.fold_in(rng, 6)
    for position, parts in cuts:
        steps = jnp.exp(jax.random.uniform(jax.random.fold_in(own, position), (parts,), jnp.float32, low / len(cuts), largest / len(cuts)))
        loudness = loudness * jnp.repeat(steps, extent[position] // parts).reshape([-1 if axis == position else 1 for axis in range(len(extent))])
    return loudness


def split_up(amount, total, reach, lean):
    weights = [(1 << 20) // math.isqrt(grade ** lean) + 1 for grade in range(2, amount + 1)]
    surplus, given = total - reach - (amount - 1), [1] * (amount - 1)
    while surplus > 0:
        movable = [i for i in range(amount - 1) if given[i] < reach]
        pool, left = sum([weights[i] for i in movable]), surplus
        for i in movable:
            addition = min(reach - given[i], max(1, left * weights[i] // pool), surplus)
            given[i] = given[i] + addition
            surplus = surplus - addition
    return np.array([reach] + given)


def uneven_parts(rng, count, total, limit, slope):
    if count == 2:
        one = jax.random.randint(rng, (), max(1, total - limit), min(limit, total - 1) + 1)
        return jnp.stack([one, total - one])
    tallies = jnp.asarray(split_up(count, total, limit, slope), jnp.int32)
    pairs = (count - 1) // 2
    giver, sink = tallies[1:1 + 2 * pairs:2], tallies[2:2 + 2 * pairs:2]
    slack = jnp.minimum(giver - 1, limit - sink)
    passed = jax.random.randint(jax.random.fold_in(rng, 1), (pairs,), 0, 1 << 20) % (slack + 1)
    tallies = tallies.at[1:1 + 2 * pairs:2].set(giver - passed).at[2:2 + 2 * pairs:2].set(sink + passed)
    return tallies[jax.random.permutation(jax.random.fold_in(rng, 2), count)]


def centred(stream_key, dims, spread, limit, shards=(), kind=jnp.bfloat16):
    drawn = spread * jax.random.normal(stream_key, dims, jnp.float32)
    if shards:
        drawn = drawn * block_levels(stream_key, dims, shards, -0.22, 0.18)
    return jnp.clip(drawn, -limit, limit).astype(kind)


def setup_inputs(seed: int = 0) -> dict:
    arg_keys = jax.random.split(jax.random.key(seed), 21)
    return {
        "tokens": centred(arg_keys[0], (SLOTS, PATCHES, D), 1.0, 6.0, ((0, 2), (1, 16))),
        "cotangent": centred(arg_keys[1], (SLOTS, PATCHES, D), 1.0, 6.0, ((0, 2), (1, 16))),
        "caption": centred(arg_keys[2], (CLIPS, CAP, D), 1.0, 6.0),
        "null_embed": centred(arg_keys[3], (CAP, D), 1.0, 6.0),
        "timesteps": with_ends(jax.random.randint(arg_keys[4], (CLIPS,), 0, 1000), jax.random.fold_in(arg_keys[4], 1), 0, 999).astype(jnp.int32),
        "null_mask": draw_null_mask(jax.random.fold_in(arg_keys[20], 71), 0),
        "bucket_sizes": uneven_parts(arg_keys[6], CLIPS, PATCHES, BUCKET_MOST, 0).astype(jnp.int32),
        "patch_mask": with_ends((jax.random.randint(arg_keys[7], (PATCHES,), 0, 4) < 3).astype(jnp.int32), jax.random.fold_in(arg_keys[7], 1), 0, 1),
        "frame_counts": uneven_parts(arg_keys[8], N_FRAMES, CLIP_FRAMES, FRAMES_DEV, 0).astype(jnp.int32),
        "table": centred(arg_keys[9], (6, D), 0.5, 3.0),
        "time_proj": centred(arg_keys[10], (TFREQ, 6 * D), TFREQ ** -0.5, 0.375, ((0, 16), (1, 2))),
        "self_qkv": centred(arg_keys[11], (D, 3 * D), D ** -0.5, 0.1875, ((0, 16), (1, 2))),
        "self_out": centred(arg_keys[12], (D, D), (D // 2) ** -0.5, 0.25, ((0, 16), (1, 2))),
        "cross_q": centred(arg_keys[13], (D, D), D ** -0.5, 0.1875, ((0, 16), (1, 2))),
        "cross_kv": centred(arg_keys[14], (D, 2 * D), D ** -0.5, 0.1875, ((0, 16), (1, 2))),
        "cross_out": centred(arg_keys[15], (D, D), (D // 16) ** -0.5, 0.75, ((0, 16), (1, 2))),
        "mlp_in": centred(arg_keys[16], (D, FF), D ** -0.5, 0.1875, ((0, 16), (1, 2))),
        "mlp_out": centred(arg_keys[17], (FF, D), FF ** -0.5, 0.09375, ((0, 16), (1, 2))),
        "biases": centred(arg_keys[18], (7, D), 0.5, 3.0),
        "hidden_bias": centred(arg_keys[19], (FF,), 0.5, 3.0),
    }


HIGH = lax.Precision.HIGHEST

@jax.custom_vjp
def low(v):
    return lax.optimization_barrier(v.astype(jnp.bfloat16)).astype(jnp.float32)

@jax.custom_vjp
def low_back(v):
    return v

def low_keep(v):
    return (low(v), None)

def low_pass(kept, grad):
    return (grad,)

def back_keep(v):
    return (v, None)

def back_low(kept, grad):
    return (low(grad),)
low.defvjp(low_keep, low_pass)
low_back.defvjp(back_keep, back_low)

def exact_dot(left, right):
    return jnp.dot(left, right, precision=HIGH)

def layer_norm(values):
    mean = lax.optimization_barrier(jnp.mean(values, axis=-1, keepdims=True))
    centered = values - mean
    variance = lax.optimization_barrier(jnp.mean(centered * centered, axis=-1, keepdims=True))
    return centered * lax.rsqrt(variance + 1e-06)

def modulate(values, shift, scale):
    return layer_norm(values) * (1.0 + scale) + shift

def time_features(timesteps, width):
    half = width // 2
    freqs = jnp.exp(-math.log(10000.0) * jnp.arange(half, dtype=jnp.float32) / half)
    angles = timesteps.astype(jnp.float32)[:, None] * freqs[None, :]
    return jnp.concatenate([jnp.cos(angles), jnp.sin(angles)], axis=1)

def token_block(consts, item):
    qkv_weight, out_weight, q_weight, cross_weight_out, in_weight, down_weight, bias_rows, hidden_b, cross_keys, cross_vals, key_mask, key_clip = consts
    slab, mods, clips_here, valid_here = item
    slot_count = slab.shape[0]
    block = slab.shape[1]
    head_dim = D // HEADS
    scale = head_dim ** (-0.5)
    normed = low(modulate(slab, mods[None, :, 0], mods[None, :, 1]))
    qkv_bias = jnp.concatenate([bias_rows[0], jnp.zeros((D,), jnp.float32), bias_rows[1]])
    qkv = low(low_back(exact_dot(normed.reshape(-1, D), qkv_weight) + qkv_bias))
    qkv = qkv.reshape(slot_count, block, 3, HEADS, head_dim)
    queries = qkv[:, :, 0]
    keys = qkv[:, :, 1]
    values = qkv[:, :, 2]
    scores = jnp.einsum('sphd,tphd->phst', queries, keys, precision=HIGH) * scale
    scores = jnp.where(key_mask[None, None], scores, -1000000000.0)
    probs = jax.nn.softmax(scores, axis=-1)
    attn_in = low(low_back(jnp.einsum('phst,tphd->sphd', probs, values, precision=HIGH).reshape(-1, D)))
    attn_out = low_back(exact_dot(attn_in, out_weight) + bias_rows[2])
    resid_a = slab + mods[None, :, 2] * attn_out.reshape(slot_count, block, D)
    cross_in = low(resid_a.reshape(-1, D))
    cross_queries = low(low_back(exact_dot(cross_in, q_weight) + bias_rows[3])).reshape(-1, HEADS, head_dim)
    token_clip = jnp.broadcast_to(clips_here[None, :], (slot_count, block)).reshape(-1)
    same_clip = token_clip[:, None] == key_clip[None, :]
    cross_scores = low_back(jnp.einsum('rhd,khd->rhk', cross_queries, cross_keys, precision=HIGH) * scale)
    cross_scores = jnp.where(same_clip[:, None, :], cross_scores, -1000000000.0)
    cross_probs = low(jax.nn.softmax(cross_scores, axis=-1))
    cross_mix = low(low_back(jnp.einsum('rhk,khd->rhd', cross_probs, cross_vals, precision=HIGH).reshape(-1, D)))
    cross_res = low_back(exact_dot(cross_mix, cross_weight_out) + bias_rows[5])
    resid_c = resid_a + cross_res.reshape(slot_count, block, D)
    normed_m = low(modulate(resid_c, mods[None, :, 3], mods[None, :, 4]))
    pre_act = low_back(exact_dot(normed_m.reshape(-1, D), in_weight) + hidden_b)
    activ = low(jax.nn.gelu(pre_act, approximate=True))
    mlp_res = low_back(exact_dot(activ, down_weight) + bias_rows[6])
    final = resid_c + mods[None, :, 5] * mlp_res.reshape(slot_count, block, D)
    return jnp.where(valid_here[:, :, None], final, 0.0)

def reference(tokens, cotangent, caption, null_embed, timesteps, null_mask, bucket_sizes, patch_mask, frame_counts, table, time_proj, self_qkv, self_out, cross_q, cross_kv, cross_out, mlp_in, mlp_out, biases, hidden_bias):
    slot_count = FRAMES_DEV * N_FRAMES
    counts = frame_counts.astype(jnp.int32)
    starts = jnp.cumsum(counts) - counts
    slot_ids = jnp.arange(slot_count, dtype=jnp.int32)
    owners = slot_ids // FRAMES_DEV
    local_slot = slot_ids % FRAMES_DEV
    slot_valid = local_slot < counts[owners]
    frame_of = starts[owners] + local_slot
    key_mask = slot_valid[None, :] & (jnp.abs(frame_of[:, None] - frame_of[None, :]) <= 1)
    ends = jnp.cumsum(bucket_sizes.astype(jnp.int32))
    patch_ids = jnp.arange(PATCHES, dtype=jnp.int32)
    clip_ids = lax.optimization_barrier(jnp.sum((patch_ids[:, None] >= ends[None, :]).astype(jnp.int32), axis=1))
    onehot = (clip_ids[:, None] == jnp.arange(CLIPS, dtype=jnp.int32)[None, :]).astype(jnp.float32)
    key_clip = jnp.repeat(jnp.arange(CLIPS, dtype=jnp.int32), CAP)
    valid = slot_valid[:, None] & (patch_mask[None, :] == 1)
    block = PATCHES
    while block * slot_count > 4096 and block % 2 == 0:
        block = block // 2
    blocks = PATCHES // block

    def forward(slab_all, captions, null_row, table_f, time_w, qkv_weight, out_weight, q_weight, kv_weight, cross_weight_out, in_weight, down_weight, bias_rows, hidden_b):
        features = low(time_features(timesteps, TFREQ))
        modulation = table_f + exact_dot(features, time_w).reshape(CLIPS, 6, D)
        per_patch = jnp.einsum('pc,ckd->pkd', onehot, modulation, precision=HIGH)
        used = jnp.where(null_mask[:, None, None] == 1, null_row[None], captions).reshape(CLIPS * CAP, D)
        kv_bias = jnp.concatenate([jnp.zeros((D,), jnp.float32), bias_rows[4]])
        cross_kv_val = low(low_back(exact_dot(used, kv_weight) + kv_bias))
        cross_keys = cross_kv_val[:, :D].reshape(CLIPS * CAP, HEADS, D // HEADS)
        cross_vals = cross_kv_val[:, D:].reshape(CLIPS * CAP, HEADS, D // HEADS)
        consts = (qkv_weight, out_weight, q_weight, cross_weight_out, in_weight, down_weight, bias_rows, hidden_b, cross_keys, cross_vals, key_mask, key_clip)
        items = (slab_all.reshape(slot_count, blocks, block, D).transpose(1, 0, 2, 3), per_patch.reshape(blocks, block, 6, D), clip_ids.reshape(blocks, block), valid.reshape(slot_count, blocks, block).transpose(1, 0, 2))
        step = jax.checkpoint(token_block)
        results = lax.map(lambda item: step(consts, item), items)
        return results.transpose(1, 0, 2, 3).reshape(slot_count, PATCHES, D)
    primals = (tokens.astype(jnp.float32), caption.astype(jnp.float32), null_embed.astype(jnp.float32), table.astype(jnp.float32), time_proj.astype(jnp.float32), self_qkv.astype(jnp.float32), self_out.astype(jnp.float32), cross_q.astype(jnp.float32), cross_kv.astype(jnp.float32), cross_out.astype(jnp.float32), mlp_in.astype(jnp.float32), mlp_out.astype(jnp.float32), biases.astype(jnp.float32), hidden_bias.astype(jnp.float32))
    result, pullback = jax.vjp(forward, *primals)
    grads = pullback(cotangent.astype(jnp.float32))
    return (result.astype(jnp.bfloat16), grads[0], grads[1], grads[2], grads[3], grads[4], grads[5], grads[6], grads[7], grads[8], grads[9], grads[10], grads[11], grads[12], grads[13])
```

```python
from functools import partial
import math

import jax
import jax.numpy as jnp
from jax import lax
from jax.experimental import pallas as pl
from jax.experimental.pallas import tpu as pltpu
from jax.sharding import PartitionSpec as P

HEADS = 16
MESH = pl.DeviceIdType.MESH


HIGH = lax.Precision.HIGHEST


def with_halo(shard, sides, width):
    for axis, dim in sides:
        count, length = (lax.axis_size(axis), shard.shape[dim])
        up = [(i, (i + 1) % count) for i in range(count - 1)]
        down = [(j, i) for i, j in up]
        last = lax.slice_in_dim(shard, length - width, length, axis=dim)
        initial = lax.slice_in_dim(shard, 0, width, axis=dim)
        before = lax.ppermute(last, axis, up)
        after = lax.ppermute(initial, axis, down)
        shard = jnp.concatenate([before, shard, after], axis=dim)
    return shard


def layer_norm(values):
    mean = jnp.mean(values, axis=-1, keepdims=True)
    centered = values - mean
    variance = jnp.mean(centered * centered, axis=-1, keepdims=True)
    return centered * lax.rsqrt(variance + 1e-06)


def modulate(values, shift, scale):
    return layer_norm(values) * (1.0 + scale) + shift


def time_features(timesteps, width):
    half = width // 2
    freqs = jnp.exp(-math.log(10000.0) * jnp.arange(half, dtype=jnp.float32) / half)
    angles = timesteps.astype(jnp.float32)[:, None] * freqs[None, :]
    return jnp.concatenate([jnp.cos(angles), jnp.sin(angles)], axis=1)


def gelu_tanh(values):
    return jax.nn.gelu(values, approximate=True)


def forward_dot(left, right):
    return jnp.dot(left, right, preferred_element_type=jnp.float32)


def outer_sum(left, right):
    return jnp.einsum("rd,re->de", left, right, preferred_element_type=jnp.float32)


def times_transposed(grad, weight):
    return jnp.einsum("re,de->rd", grad, weight, preferred_element_type=jnp.float32)


def round_trip(values):
    return lax.optimization_barrier(values.astype(jnp.bfloat16)).astype(jnp.float32)


def gather_forward(shards):
    row_parts = (
        lax.all_gather(shards[0], "patches", axis=0, tiled=True),
        lax.all_gather(shards[1], "patches", axis=0, tiled=True),
        lax.all_gather(shards[2], "patches", axis=0, tiled=True),
        lax.all_gather(shards[3], "patches", axis=0, tiled=True),
        lax.all_gather(shards[4], "patches", axis=0, tiled=True),
        lax.all_gather(shards[5], "patches", axis=0, tiled=True),
        lax.all_gather(shards[6], "patches", axis=0, tiled=True),
        lax.all_gather(shards[7], "patches", axis=0, tiled=True),
    )
    return (
        lax.all_gather(row_parts[0], "frames", axis=1, tiled=True),
        lax.all_gather(row_parts[1], "frames", axis=1, tiled=True),
        lax.all_gather(row_parts[2], "frames", axis=1, tiled=True),
        lax.all_gather(row_parts[3], "frames", axis=1, tiled=True),
        lax.all_gather(row_parts[4], "frames", axis=1, tiled=True),
        lax.all_gather(row_parts[5], "frames", axis=1, tiled=True),
        lax.all_gather(row_parts[6], "frames", axis=1, tiled=True),
        lax.all_gather(row_parts[7], "frames", axis=1, tiled=True),
    )


class Place:
    def __init__(self):
        self.y=lax.axis_index("frames"); p=lax.axis_index("patches")
        self.z=p//4; self.x=lax.rem(p//2,2); self.c=lax.rem(p,2)
    def dev(self,y=None,z=None,x=None,c=None):
        y=self.y if y is None else y; z=self.z if z is None else z
        x=self.x if x is None else x; c=self.c if c is None else c
        return (y,(z*2+x)*2+c)
    def zoff(self,d): return lax.rem(self.z+d,4)

def barrier(pos):
    bar=pltpu.get_barrier_semaphore()
    peers=[pos.dev(z=pos.zoff(d)) for d in (1,2,3)]+[pos.dev(x=1-pos.x),pos.dev(y=1-pos.y),pos.dev(c=1-pos.c)]
    for t in peers: pl.semaphore_signal(bar,inc=1,device_id=t,device_id_type=MESH)
    pl.semaphore_wait(bar,6)

N_AG=9
class Gather:
    def __init__(self,pos,shard,full,send,recv,first):
        self.pos=pos; self.shard=shard; self.full=full; self.send=send; self.recv=recv; self.first=first
    def _rc(self,i,src,dst,dev):
        return pltpu.make_async_remote_copy(src_ref=src,dst_ref=dst,send_sem=self.send.at[i],recv_sem=self.recv.at[i],device_id=dev,device_id_type=MESH)
    def _copies(self):
        p=self.pos; F=self.full; y,z,x,c=p.y,p.z,p.x,p.c
        cs=[]
        mine=F.at[y,z,x,c]
        for d in (1,2,3):
            cs.append(self._rc(d-1,self.shard,mine,p.dev(z=p.zoff(d))))
        line=F.at[y,:,x,c]
        if self.first=="x":
            cs.append(self._rc(3,line,line,p.dev(x=1-x)))
            plane=F.at[y,:,:,c]
            cs.append(self._rc(4,plane,plane,p.dev(y=1-y)))
            got1=F.at[y,:,1-x,c]; got2=F.at[1-y,:,:,c]
        else:
            cs.append(self._rc(3,line,line,p.dev(y=1-y)))
            plane=F.at[:,:,x,c]
            cs.append(self._rc(4,plane,plane,p.dev(x=1-x)))
            got1=F.at[1-y,:,x,c]; got2=F.at[:,:,1-x,c]
        o=p.dev(c=1-c)
        cs.append(self._rc(5,line,line,o)); cs.append(self._rc(6,got1,got1,o)); cs.append(self._rc(7,got2,got2,o))
        return cs
    def start(self):
        self.cs=self._copies()
        p=self.pos
        for i in (0,1,2): self.cs[i].start()
        self.loc=pltpu.make_async_copy(self.shard,self.full.at[p.y,p.z,p.x,p.c],self.send.at[8])
        self.loc.start()
    def step1(self):
        self.loc.wait()
        for i in (0,1,2): self.cs[i].wait_recv()
        self.cs[3].start(); self.cs[5].start()
    def step2(self):
        self.cs[3].wait_recv(); self.cs[4].start(); self.cs[6].start()
    def step3(self):
        self.cs[4].wait_recv(); self.cs[7].start()
    def finish(self):
        for i in (5,6,7): self.cs[i].wait_recv()
        for i in range(8): self.cs[i].wait_send()

N_RS=6
class Scatter:
    def __init__(self,pos,part,out,bufs,send,recv,first):
        self.pos=pos; self.part=part; self.out=out; self.send=send; self.recv=recv; self.first=first
        self.own,self.r1,self.r2,self.r3,self.r4=bufs
    def _rc(self,i,src,dst,dev):
        return pltpu.make_async_remote_copy(src_ref=src,dst_ref=dst,send_sem=self.send.at[i],recv_sem=self.recv.at[i],device_id=dev,device_id_type=MESH)
    def start(self):
        p=self.pos
        self.loc=pltpu.make_async_copy(self.part.at[:,:,:,p.c],self.own,self.send.at[6])
        self.cc=self._rc(0,self.part.at[:,:,:,1-p.c],self.r1,p.dev(c=1-p.c))
        self.loc.start(); self.cc.start()
    def step1(self):
        p=self.pos; own=self.own
        self.loc.wait(); self.cc.wait_recv()
        def body(i,_):
            f,r=i//8,lax.rem(i,8); z,x=r//2,lax.rem(r,2)
            own[f,z,x]=(own[f,z,x].astype(jnp.float32)+self.r1[f,z,x].astype(jnp.float32)).astype(jnp.bfloat16)
            return 0
        lax.fori_loop(0,16,body,0)
        if self.first=="y": self.c1=self._rc(1,own.at[1-p.y],self.r2,p.dev(y=1-p.y))
        else: self.c1=self._rc(1,own.at[:,:,1-p.x],self.r2,p.dev(x=1-p.x))
        self.c1.start()
    def step2(self):
        p=self.pos; own=self.own
        self.c1.wait_recv()
        def body(i,_):
            if self.first=="y": f,z,x=p.y,i//2,lax.rem(i,2); a,b=z,x
            else: f,z,x=i//4,lax.rem(i,4),p.x; a,b=f,z
            own[f,z,x]=(own[f,z,x].astype(jnp.float32)+self.r2[a,b].astype(jnp.float32)).astype(jnp.bfloat16)
            return 0
        lax.fori_loop(0,8,body,0)
        if self.first=="y": self.c2=self._rc(2,own.at[p.y,:,1-p.x],self.r3,p.dev(x=1-p.x))
        else: self.c2=self._rc(2,own.at[1-p.y,:,p.x],self.r3,p.dev(y=1-p.y))
        self.c2.start()
    def step3(self):
        p=self.pos; own=self.own
        self.c2.wait_recv()
        def body(z,_):
            own[p.y,z,p.x]=(own[p.y,z,p.x].astype(jnp.float32)+self.r3[z].astype(jnp.float32)).astype(jnp.bfloat16)
            return 0
        lax.fori_loop(0,4,body,0)
        self.cz=[self._rc(2+d,own.at[p.y,p.zoff(d),p.x],self.r4.at[d-1],p.dev(z=p.zoff(d))) for d in (1,2,3)]
        for c in self.cz: c.start()
    def step4(self):
        p=self.pos
        for c in self.cz: c.wait_recv()
        f32=jnp.float32
        self.out[...]=((self.own[p.y,p.z,p.x].astype(f32)+self.r4[0].astype(f32))+(self.r4[1].astype(f32)+self.r4[2].astype(f32)))
    def finish(self):
        for c in [self.cc,self.c1,self.c2]+self.cz: c.wait_send()
def scatter_bufs(R,C,first):
    bf=jnp.bfloat16
    return [pltpu.VMEM((2,4,2,R,C),bf),pltpu.VMEM((2,4,2,R,C),bf),
      pltpu.VMEM((4,2,R,C) if first=="y" else (2,4,R,C),bf),pltpu.VMEM((4,R,C),bf),pltpu.VMEM((3,R,C),bf)]


def part_of(ref, rows, cols, lead):
    index = [slice(None)] * lead
    index.append(pl.ds(*rows) if rows else slice(None))
    index.append(pl.ds(*cols) if cols else slice(None))
    return ref.at[tuple(index)]


def gather_kernel(units, count, *refs):
    shards, fulls = refs[:count], refs[count : 2 * count]
    send, recv = refs[2 * count :]
    pos = Place()
    barrier(pos)
    work = [
        Gather(
            pos,
            part_of(shards[a], r, c, 0),
            part_of(fulls[a], r, c, 4),
            send.at[k],
            recv.at[k],
            first,
        )
        for k, (a, r, c, first) in enumerate(units)
    ]
    for unit in work:
        unit.start()
    total = len(work)
    for t in range(total + 2):
        if t < total:
            work[t].step1()
        if 0 <= t - 1 < total:
            work[t - 1].step2()
        if 0 <= t - 2 < total:
            work[t - 2].step3()
    for unit in work:
        unit.finish()


def gather_call(shards, units, ident):
    count = len(shards)
    return pl.pallas_call(
        partial(gather_kernel, units, count),
        out_shape=[jax.ShapeDtypeStruct((2, 4, 2, 2) + s.shape, s.dtype) for s in shards],
        in_specs=[pl.BlockSpec(memory_space=pl.ANY)] * count,
        out_specs=[pl.BlockSpec(memory_space=pl.ANY)] * count,
        scratch_shapes=[
            pltpu.SemaphoreType.DMA((len(units), N_AG)),
            pltpu.SemaphoreType.DMA((len(units), 8)),
        ],
        compiler_params=pltpu.CompilerParams(collective_id=ident, has_side_effects=True),
        name="gather",
    )(*shards)


def scatter_kernel(units, count, *refs):
    parts, outs = refs[:count], refs[count : 2 * count]
    rest = refs[2 * count :]
    send, recv = rest[-2:]
    pos = Place()
    barrier(pos)
    work = [
        Scatter(
            pos,
            part_of(parts[a], r, c, 4),
            part_of(outs[a], r, c, 0),
            rest[5 * k : 5 * k + 5],
            send.at[k],
            recv.at[k],
            first,
        )
        for k, (a, r, c, first) in enumerate(units)
    ]
    total = len(work)
    for unit in work:
        unit.start()
    for t in range(total + 3):
        if t < total:
            work[t].step1()
        if 0 <= t - 1 < total:
            work[t - 1].step2()
        if 0 <= t - 2 < total:
            work[t - 2].step3()
        if 0 <= t - 3 < total:
            work[t - 3].step4()
    for unit in work:
        unit.finish()


def scatter_call(parts, units, ident):
    count = len(parts)
    scratch = []
    for a, r, c, first in units:
        rows, cols = parts[a].shape[-2:]
        scratch += scatter_bufs(r[1] if r else rows, c[1] if c else cols, first)
    return pl.pallas_call(
        partial(scatter_kernel, units, count),
        out_shape=[jax.ShapeDtypeStruct(p.shape[-2:], jnp.float32) for p in parts],
        in_specs=[pl.BlockSpec(memory_space=pl.ANY)] * count,
        out_specs=[pl.BlockSpec(memory_space=pltpu.VMEM)] * count,
        scratch_shapes=scratch
        + [
            pltpu.SemaphoreType.DMA((len(units), 7)),
            pltpu.SemaphoreType.DMA((len(units), N_RS)),
        ],
        compiler_params=pltpu.CompilerParams(
            collective_id=ident, has_side_effects=True, vmem_limit_bytes=60 * 2**20
        ),
        name="scatter",
    )(*parts)


GATHER_UNITS = (
    (0, None, (0, 1152), "x"),
    (0, None, (1152, 1152), "y"),
    (1, None, None, "x"),
    (4, None, None, "y"),
    (2, None, (0, 1152), "x"),
    (2, None, (1152, 1152), "y"),
    (3, (0, 144), None, "x"),
    (3, (144, 144), None, "y"),
)


def fast_gather(self_qkv, self_out, cross_q, cross_kv, cross_out, mlp_in, mlp_out):
    first = jnp.concatenate([self_qkv, self_out], axis=1)
    second = jnp.concatenate([cross_q, cross_out], axis=1)
    got = gather_call([first, second, mlp_in, mlp_out, cross_kv], GATHER_UNITS, 0)
    got = [g.reshape(2, -1, g.shape[-1]) for g in got]
    qkv_cols = self_qkv.shape[1]
    q_cols = cross_q.shape[1]

    def whole(array, low, high):
        return jnp.concatenate([array[0, :, low:high], array[1, :, low:high]], axis=1)

    return (
        whole(got[0], 0, qkv_cols),
        whole(got[0], qkv_cols, got[0].shape[-1]),
        whole(got[1], 0, q_cols),
        whole(got[4], 0, cross_kv.shape[1]),
        whole(got[1], q_cols, got[1].shape[-1]),
        whole(got[2], 0, mlp_in.shape[1]),
        whole(got[3], 0, mlp_out.shape[1]),
    )


def blocks_of(grad):
    grad = grad.astype(jnp.bfloat16)
    rows, cols = grad.shape
    return grad.reshape(16, rows // 16, 2, cols // 2).transpose(2, 0, 1, 3).reshape(
        2, 4, 2, 2, rows // 16, cols // 2
    )


def fast_scatter(qkv, out, q, cross_out, mlp_in, mlp_out):
    (in_shard, mlp_out_shard) = scatter_call(
        [blocks_of(mlp_in), blocks_of(mlp_out)],
        (
            (0, None, (0, 1152), "x"),
            (0, None, (1152, 1152), "y"),
            (1, (0, 144), None, "x"),
            (1, (144, 144), None, "y"),
        ),
        1,
    )
    first = jnp.concatenate([blocks_of(qkv), blocks_of(out)], axis=-1)
    second = jnp.concatenate([blocks_of(q), blocks_of(cross_out)], axis=-1)
    first, second = scatter_call(
        [first, second],
        (
            (0, None, (0, 1152), "x"),
            (0, None, (1152, 1152), "y"),
            (1, None, (0, 640), "x"),
            (1, None, (640, 512), "y"),
        ),
        2,
    )
    cut = qkv.shape[1] // 2
    half = q.shape[1] // 2
    return (
        first[:, :cut],
        first[:, cut:],
        second[:, :half],
        second[:, half:],
        in_shard,
        mlp_out_shard,
    )


def self_attend(queries, keys_vals, key_mask, heads):
    frames, patches, width = queries.shape
    head_dim = width // heads
    query_heads = queries.reshape(frames, patches, heads, head_dim)
    key_heads = keys_vals[..., :width].reshape(frames + 2, patches, heads, head_dim)
    value_heads = keys_vals[..., width:].reshape(frames + 2, patches, heads, head_dim)
    scores = jnp.einsum("sphd,tphd->phst", query_heads, key_heads, precision=HIGH) * head_dim ** (
        -0.5
    )
    scores = jnp.where(key_mask[None, None], scores, -1000000000.0)
    probs = jax.nn.softmax(scores, axis=-1)
    mixed = jnp.einsum("phst,tphd->sphd", probs, value_heads, precision=HIGH)
    return mixed.reshape(frames, patches, width)


def body(
    tokens,
    cotangent,
    caption,
    null_embed,
    timesteps,
    null_mask,
    bucket_sizes,
    patch_mask,
    frame_counts,
    table,
    time_proj,
    self_qkv,
    self_out,
    cross_q,
    cross_kv,
    cross_out,
    mlp_in,
    mlp_out,
    biases,
    hidden_bias,
):
    f32 = jnp.float32
    bf16 = jnp.bfloat16
    frames, patches, width = tokens.shape
    heads = HEADS
    head_dim = width // heads
    scale = head_dim ** (-0.5)
    clips = caption.shape[0]
    cap_len = caption.shape[1]
    row_count = frames * patches
    count = frame_counts[0]
    frame_index = lax.axis_index("frames")
    patch_index = lax.axis_index("patches")
    shards = (time_proj, self_qkv, self_out, cross_q, cross_kv, cross_out, mlp_in, mlp_out)
    fast = lax.axis_size("frames") == 2 and lax.axis_size("patches") == 16
    if fast:
        weights = fast_gather(*shards[1:])
    else:
        weights = gather_forward(shards)[1:]
    full_qkv, full_out, full_q, full_kv, full_cross_out, full_in, full_mlp_out = weights
    bias_f = biases.astype(f32)
    bias_hidden = hidden_bias.astype(f32)
    patch_ids = patch_index * patches + jnp.arange(patches, dtype=jnp.int32)
    bucket_ends = jnp.cumsum(bucket_sizes)
    clip_ids = jnp.sum((patch_ids[:, None] >= bucket_ends[None, :]).astype(jnp.int32), axis=1)
    onehot = (clip_ids[:, None] == jnp.arange(clips, dtype=jnp.int32)[None, :]).astype(f32)
    slot_ids = jnp.arange(frames, dtype=jnp.int32)
    valid = (slot_ids < count)[:, None] & (patch_mask[None, :] == 1)
    time_rows, time_cols = time_proj.shape
    features = time_features(timesteps, time_rows * lax.axis_size("patches")).astype(bf16)
    own_features = lax.dynamic_slice_in_dim(features, patch_index * time_rows, time_rows, 1)
    time_part = jnp.zeros((clips, 6 * width), f32)
    time_part = lax.dynamic_update_slice(
        time_part, forward_dot(own_features, time_proj), (0, frame_index * time_cols)
    )
    time_sum = lax.psum(time_part, ("frames", "patches"))
    modulation = table.astype(f32) + time_sum.reshape(clips, 6, width)
    per_patch = jnp.einsum("pc,ckd->pkd", onehot, modulation, precision=HIGH)
    shift_a = per_patch[:, 0]
    scale_a = per_patch[:, 1]
    gate_a = per_patch[:, 2]
    shift_m = per_patch[:, 3]
    scale_m = per_patch[:, 4]
    gate_m = per_patch[:, 5]
    inputs_f = tokens.astype(f32)
    normed_a, modulate_a_vjp = jax.vjp(modulate, inputs_f, shift_a, scale_a)
    normed_r = normed_a.astype(bf16).reshape(row_count, width)
    qkv_bias = jnp.concatenate([bias_f[0], jnp.zeros((width,), f32), bias_f[1]])
    qkv_r = (
        (forward_dot(normed_r, full_qkv) + qkv_bias)
        .astype(bf16)
        .reshape(frames, patches, 3 * width)
    )
    queries_r = qkv_r[..., :width]
    keyval_r = qkv_r[..., width:]
    last_kv = lax.dynamic_index_in_dim(keyval_r, count - 1, 0, keepdims=False)
    edges = jnp.stack([keyval_r[0], last_kv])
    outer_kv = with_halo(edges, (("frames", 0),), 1)
    keys_all = jnp.concatenate([outer_kv[0:1], keyval_r, outer_kv[3:4]], axis=0)
    prev_ok = frame_index > 0
    next_ok = frame_index < lax.axis_size("frames") - 1
    query_slot = slot_ids[:, None]
    key_place = jnp.arange(frames + 2, dtype=jnp.int32)[None, :]
    key_slot = key_place - 1
    slot_keys = (
        (key_place >= 1)
        & (key_place <= frames)
        & (jnp.abs(key_slot - query_slot) <= 1)
        & (key_slot < count)
    )
    prev_keys = (key_place == 0) & (query_slot == 0) & prev_ok
    next_keys = (key_place == frames + 1) & (query_slot == count - 1) & next_ok
    key_mask = slot_keys | prev_keys | next_keys
    attn_in, attend_vjp = jax.vjp(
        partial(self_attend, key_mask=key_mask, heads=heads),
        queries_r.astype(f32),
        keys_all.astype(f32),
    )
    attn_r = attn_in.astype(bf16).reshape(row_count, width)
    attn_out = (forward_dot(attn_r, full_out) + bias_f[2]).reshape(frames, patches, width)
    resid_a = inputs_f + gate_a * attn_out
    captions_used = jnp.where(null_mask[:, None, None] == 1, null_embed[None], caption).reshape(
        clips * cap_len, width
    )
    kv_bias = jnp.concatenate([jnp.zeros((width,), f32), bias_f[4]])
    cross_kv_r = (forward_dot(captions_used, full_kv) + kv_bias).astype(bf16)
    cross_keys = cross_kv_r[:, :width].reshape(clips * cap_len, heads, head_dim)
    cross_vals = cross_kv_r[:, width:].reshape(clips * cap_len, heads, head_dim)
    resid_a_r = resid_a.astype(bf16).reshape(row_count, width)
    cross_queries = (
        (forward_dot(resid_a_r, full_q) + bias_f[3])
        .astype(bf16)
        .reshape(row_count, heads, head_dim)
    )
    token_clip = jnp.broadcast_to(clip_ids[None, :], (frames, patches)).reshape(row_count)
    key_clip = jnp.repeat(jnp.arange(clips, dtype=jnp.int32), cap_len)
    same_clip = token_clip[:, None] == key_clip[None, :]
    scores = (
        jnp.einsum("rhd,khd->rhk", cross_queries, cross_keys, preferred_element_type=f32) * scale
    )
    scores = jnp.where(same_clip[:, None, :], scores, -1000000000.0)
    probs = jax.nn.softmax(scores, axis=-1)
    probs_r = probs.astype(bf16)
    cross_mix = (
        jnp.einsum("rhk,khd->rhd", probs_r, cross_vals, preferred_element_type=f32)
        .astype(bf16)
        .reshape(row_count, width)
    )
    cross_res = forward_dot(cross_mix, full_cross_out) + bias_f[5]
    resid_c = resid_a + cross_res.reshape(frames, patches, width)
    normed_m, modulate_m_vjp = jax.vjp(modulate, resid_c, shift_m, scale_m)
    normed_m_r = normed_m.astype(bf16).reshape(row_count, width)
    pre_act = forward_dot(normed_m_r, full_in) + bias_hidden
    activ, gelu_vjp = jax.vjp(gelu_tanh, pre_act)
    activ_r = activ.astype(bf16)
    mlp_res = (forward_dot(activ_r, full_mlp_out) + bias_f[6]).reshape(frames, patches, width)
    final = resid_c + gate_m * mlp_res
    block_out = jnp.where(valid[:, :, None], final, 0.0).astype(bf16)
    grad_final = jnp.where(valid[:, :, None], cotangent.astype(f32), 0.0)
    grad_gate_m = jnp.sum(grad_final * mlp_res, axis=0)
    grad_mlp_r = (gate_m * grad_final).astype(bf16).reshape(row_count, width)
    bias_mo_grad = jnp.sum(grad_mlp_r.astype(f32), axis=0)
    mlp_out_grad = outer_sum(activ_r, grad_mlp_r)
    grad_act = times_transposed(grad_mlp_r, full_mlp_out)
    grad_pre_r = gelu_vjp(grad_act)[0].astype(bf16)
    bias_hidden_grad = jnp.sum(grad_pre_r.astype(f32), axis=0)
    mlp_in_grad = outer_sum(normed_m_r, grad_pre_r)
    grad_norm_m = times_transposed(grad_pre_r, full_in).reshape(frames, patches, width)
    resid_c_part, grad_shift_m, grad_scale_m = modulate_m_vjp(grad_norm_m)
    grad_resid_c = grad_final + resid_c_part
    grad_cross_r = grad_resid_c.astype(bf16).reshape(row_count, width)
    bias_co_grad = jnp.sum(grad_cross_r.astype(f32), axis=0)
    cross_out_grad = outer_sum(cross_mix, grad_cross_r)
    grad_mix_r = (
        times_transposed(grad_cross_r, full_cross_out)
        .astype(bf16)
        .reshape(row_count, heads, head_dim)
    )
    grad_probs = jnp.einsum("rhd,khd->rhk", grad_mix_r, cross_vals, preferred_element_type=f32)
    grad_vals = jnp.einsum("rhk,rhd->khd", probs_r, grad_mix_r, preferred_element_type=f32)
    grad_scores_r = (
        probs * (grad_probs - jnp.sum(grad_probs * probs, axis=-1, keepdims=True))
    ).astype(bf16)
    grad_cq = (
        jnp.einsum("rhk,khd->rhd", grad_scores_r, cross_keys, preferred_element_type=f32) * scale
    )
    grad_cq_r = grad_cq.astype(bf16).reshape(row_count, width)
    grad_keys = (
        jnp.einsum("rhk,rhd->khd", grad_scores_r, cross_queries, preferred_element_type=f32) * scale
    )
    bias_cq_grad = jnp.sum(grad_cq_r.astype(f32), axis=0)
    cross_q_grad = outer_sum(resid_a_r, grad_cq_r)
    grad_resid_a = grad_resid_c + times_transposed(grad_cq_r, full_q).reshape(
        frames, patches, width
    )
    cross_kv_part = jnp.concatenate(
        [grad_keys.reshape(clips * cap_len, width), grad_vals.reshape(clips * cap_len, width)],
        axis=1,
    )
    grad_gate_a = jnp.sum(grad_resid_a * attn_out, axis=0)
    grad_attn_r = (gate_a * grad_resid_a).astype(bf16).reshape(row_count, width)
    bias_o_grad = jnp.sum(grad_attn_r.astype(f32), axis=0)
    self_out_grad = outer_sum(attn_r, grad_attn_r)
    grad_attn_in = round_trip(times_transposed(grad_attn_r, full_out)).reshape(
        frames, patches, width
    )
    grad_queries, grad_keys_all = attend_vjp(grad_attn_in)
    returns = jnp.stack([grad_keys_all[0], grad_keys_all[frames + 1]])
    back_kv = with_halo(returns.astype(jnp.bfloat16), (("frames", 0),), 1).astype(returns.dtype)
    first_slot = (slot_ids == 0)[:, None, None]
    last_slot = (slot_ids == count - 1)[:, None, None]
    grad_kv = (
        grad_keys_all[1 : frames + 1]
        + jnp.where(first_slot, back_kv[0][None], 0.0)
        + jnp.where(last_slot, back_kv[3][None], 0.0)
    )
    grad_qkv_r = (
        jnp.concatenate([grad_queries, grad_kv], axis=-1).astype(bf16).reshape(row_count, 3 * width)
    )
    bias_q_grad = jnp.sum(grad_qkv_r[:, :width].astype(f32), axis=0)
    bias_v_grad = jnp.sum(grad_qkv_r[:, 2 * width :].astype(f32), axis=0)
    self_qkv_grad = outer_sum(normed_r, grad_qkv_r)
    grad_norm_a = times_transposed(grad_qkv_r, full_qkv).reshape(frames, patches, width)
    input_part, grad_shift_a, grad_scale_a = modulate_a_vjp(grad_norm_a)
    input_grad = grad_resid_a + input_part
    per_patch_grad = jnp.stack(
        [grad_shift_a, grad_scale_a, grad_gate_a, grad_shift_m, grad_scale_m, grad_gate_m], axis=1
    )
    mod_part = jnp.einsum("pc,pkd->ckd", onehot, per_patch_grad, precision=HIGH)
    bias_part = jnp.stack(
        [
            bias_q_grad,
            bias_v_grad,
            bias_o_grad,
            bias_cq_grad,
            jnp.zeros((width,), f32),
            bias_co_grad,
            bias_mo_grad,
        ]
    )
    kv_total, bias_total, hidden_total, mod_total = lax.psum(
        (cross_kv_part, bias_part, bias_hidden_grad, mod_part), ("frames", "patches")
    )
    kv_total_r = kv_total.astype(bf16)
    bias_cv_grad = jnp.sum(kv_total_r[:, width:].astype(f32), axis=0)
    bias_rows_ids = jnp.arange(bias_total.shape[0], dtype=jnp.int32)
    biases_grad = bias_total + jnp.where((bias_rows_ids == 4)[:, None], bias_cv_grad[None, :], 0.0)
    cross_kv_full = outer_sum(captions_used, kv_total_r)
    caption_rows = times_transposed(kv_total_r, full_kv).reshape(clips, cap_len, width)
    dropped = (null_mask == 1)[:, None, None]
    caption_grad = jnp.where(dropped, 0.0, caption_rows)
    null_grad = jnp.sum(jnp.where(dropped, caption_rows, 0.0), axis=0)
    table_grad = jnp.sum(mod_total, axis=0)
    time_full = jnp.dot(features.astype(f32).T, mod_total.reshape(clips, 6 * width), precision=HIGH)
    time_proj_grad = lax.dynamic_slice(
        time_full,
        (patch_index * time_proj.shape[0], frame_index * time_proj.shape[1]),
        time_proj.shape,
    )
    cross_kv_grad = lax.dynamic_slice(
        cross_kv_full,
        (patch_index * cross_kv.shape[0], frame_index * cross_kv.shape[1]),
        cross_kv.shape,
    )
    grads = (self_qkv_grad, self_out_grad, cross_q_grad, cross_out_grad, mlp_in_grad, mlp_out_grad)
    if fast:
        col_sums = fast_scatter(*grads)
    else:
        row_sums = (
            lax.psum_scatter(
                grads[0].astype(jnp.bfloat16), "patches", scatter_dimension=0, tiled=True
            ).astype(jnp.float32),
            lax.psum_scatter(
                grads[1].astype(jnp.bfloat16), "patches", scatter_dimension=0, tiled=True
            ).astype(jnp.float32),
            lax.psum_scatter(
                grads[2].astype(jnp.bfloat16), "patches", scatter_dimension=0, tiled=True
            ).astype(jnp.float32),
            lax.psum_scatter(
                grads[3].astype(jnp.bfloat16), "patches", scatter_dimension=0, tiled=True
            ).astype(jnp.float32),
            lax.psum_scatter(
                grads[4].astype(jnp.bfloat16), "patches", scatter_dimension=0, tiled=True
            ).astype(jnp.float32),
            lax.psum_scatter(
                grads[5].astype(jnp.bfloat16), "patches", scatter_dimension=0, tiled=True
            ).astype(jnp.float32),
        )
        col_sums = (
            lax.psum_scatter(
                row_sums[0].astype(jnp.bfloat16), "frames", scatter_dimension=1, tiled=True
            ).astype(jnp.float32),
            lax.psum_scatter(
                row_sums[1].astype(jnp.bfloat16), "frames", scatter_dimension=1, tiled=True
            ).astype(jnp.float32),
            lax.psum_scatter(
                row_sums[2].astype(jnp.bfloat16), "frames", scatter_dimension=1, tiled=True
            ).astype(jnp.float32),
            lax.psum_scatter(
                row_sums[3].astype(jnp.bfloat16), "frames", scatter_dimension=1, tiled=True
            ).astype(jnp.float32),
            lax.psum_scatter(
                row_sums[4].astype(jnp.bfloat16), "frames", scatter_dimension=1, tiled=True
            ).astype(jnp.float32),
            lax.psum_scatter(
                row_sums[5].astype(jnp.bfloat16), "frames", scatter_dimension=1, tiled=True
            ).astype(jnp.float32),
        )
    qkv_shard, out_shard, q_shard, cross_out_shard, in_shard, mlp_out_shard = col_sums
    return (
        block_out,
        input_grad,
        caption_grad,
        null_grad,
        table_grad,
        time_proj_grad,
        qkv_shard,
        out_shard,
        q_shard,
        cross_kv_grad,
        cross_out_shard,
        in_shard,
        mlp_out_shard,
        biases_grad,
        hidden_total,
    )


def solution(mesh):
    return jax.shard_map(
        body,
        mesh=mesh,
        in_specs=(
            P("frames", "patches", None),
            P("frames", "patches", None),
            P(),
            P(),
            P(),
            P(),
            P(),
            P("patches"),
            P("frames"),
            P(),
            P("patches", "frames"),
            P("patches", "frames"),
            P("patches", "frames"),
            P("patches", "frames"),
            P("patches", "frames"),
            P("patches", "frames"),
            P("patches", "frames"),
            P("patches", "frames"),
            P(),
            P(),
        ),
        out_specs=(
            P("frames", "patches", None),
            P("frames", "patches", None),
            P(),
            P(),
            P(),
            P("patches", "frames"),
            P("patches", "frames"),
            P("patches", "frames"),
            P("patches", "frames"),
            P("patches", "frames"),
            P("patches", "frames"),
            P("patches", "frames"),
            P("patches", "frames"),
            P(),
            P(),
        ),
        check_vma=False,
    )
```

```python
from functools import partial
import math

import jax
import jax.numpy as jnp
from jax import lax
from jax.experimental import pallas as pl
from jax.experimental.pallas import tpu as pltpu
from jax.sharding import PartitionSpec as P

HEADS = 16
MESH = pl.DeviceIdType.MESH


HIGH = lax.Precision.HIGHEST


def with_halo(shard, sides, width):
    for axis, dim in sides:
        count, length = (lax.axis_size(axis), shard.shape[dim])
        up = [(i, (i + 1) % count) for i in range(count - 1)]
        down = [(j, i) for i, j in up]
        last = lax.slice_in_dim(shard, length - width, length, axis=dim)
        initial = lax.slice_in_dim(shard, 0, width, axis=dim)
        before = lax.ppermute(last, axis, up)
        after = lax.ppermute(initial, axis, down)
        shard = jnp.concatenate([before, shard, after], axis=dim)
    return shard


def layer_norm(values):
    mean = jnp.mean(values, axis=-1, keepdims=True)
    centered = values - mean
    variance = jnp.mean(centered * centered, axis=-1, keepdims=True)
    return centered * lax.rsqrt(variance + 1e-06)


def modulate(values, shift, scale):
    return layer_norm(values) * (1.0 + scale) + shift


def time_features(timesteps, width):
    half = width // 2
    freqs = jnp.exp(-math.log(10000.0) * jnp.arange(half, dtype=jnp.float32) / half)
    angles = timesteps.astype(jnp.float32)[:, None] * freqs[None, :]
    return jnp.concatenate([jnp.cos(angles), jnp.sin(angles)], axis=1)


def gelu_tanh(values):
    return jax.nn.gelu(values, approximate=True)


def forward_dot(left, right):
    return jnp.dot(left, right, preferred_element_type=jnp.float32)


def outer_sum(left, right):
    return jnp.einsum("rd,re->de", left, right, preferred_element_type=jnp.float32)


def times_transposed(grad, weight):
    return jnp.einsum("re,de->rd", grad, weight, preferred_element_type=jnp.float32)


def round_trip(values):
    return lax.optimization_barrier(values.astype(jnp.bfloat16)).astype(jnp.float32)


def gather_forward(shards):
    row_parts = (
        lax.all_gather(shards[0], "patches", axis=0, tiled=True),
        lax.all_gather(shards[1], "patches", axis=0, tiled=True),
        lax.all_gather(shards[2], "patches", axis=0, tiled=True),
        lax.all_gather(shards[3], "patches", axis=0, tiled=True),
        lax.all_gather(shards[4], "patches", axis=0, tiled=True),
        lax.all_gather(shards[5], "patches", axis=0, tiled=True),
        lax.all_gather(shards[6], "patches", axis=0, tiled=True),
        lax.all_gather(shards[7], "patches", axis=0, tiled=True),
    )
    return (
        lax.all_gather(row_parts[0], "frames", axis=1, tiled=True),
        lax.all_gather(row_parts[1], "frames", axis=1, tiled=True),
        lax.all_gather(row_parts[2], "frames", axis=1, tiled=True),
        lax.all_gather(row_parts[3], "frames", axis=1, tiled=True),
        lax.all_gather(row_parts[4], "frames", axis=1, tiled=True),
        lax.all_gather(row_parts[5], "frames", axis=1, tiled=True),
        lax.all_gather(row_parts[6], "frames", axis=1, tiled=True),
        lax.all_gather(row_parts[7], "frames", axis=1, tiled=True),
    )


def self_attend(queries, keys_vals, key_mask, heads):
    frames, patches, width = queries.shape
    head_dim = width // heads
    query_heads = queries.reshape(frames, patches, heads, head_dim)
    key_heads = keys_vals[..., :width].reshape(frames + 2, patches, heads, head_dim)
    value_heads = keys_vals[..., width:].reshape(frames + 2, patches, heads, head_dim)
    scores = jnp.einsum("sphd,tphd->phst", query_heads, key_heads, precision=HIGH) * head_dim ** (
        -0.5
    )
    scores = jnp.where(key_mask[None, None], scores, -1000000000.0)
    probs = jax.nn.softmax(scores, axis=-1)
    mixed = jnp.einsum("phst,tphd->sphd", probs, value_heads, precision=HIGH)
    return mixed.reshape(frames, patches, width)


def plain_body(
    tokens,
    cotangent,
    caption,
    null_embed,
    timesteps,
    null_mask,
    bucket_sizes,
    patch_mask,
    frame_counts,
    table,
    time_proj,
    self_qkv,
    self_out,
    cross_q,
    cross_kv,
    cross_out,
    mlp_in,
    mlp_out,
    biases,
    hidden_bias,
):
    f32 = jnp.float32
    bf16 = jnp.bfloat16
    frames, patches, width = tokens.shape
    heads = HEADS
    head_dim = width // heads
    scale = head_dim ** (-0.5)
    clips = caption.shape[0]
    cap_len = caption.shape[1]
    row_count = frames * patches
    count = frame_counts[0]
    frame_index = lax.axis_index("frames")
    patch_index = lax.axis_index("patches")
    shards = (time_proj, self_qkv, self_out, cross_q, cross_kv, cross_out, mlp_in, mlp_out)
    weights = gather_forward(shards)
    full_time, full_qkv, full_out, full_q, full_kv, full_cross_out, full_in, full_mlp_out = weights
    bias_f = biases.astype(f32)
    bias_hidden = hidden_bias.astype(f32)
    patch_ids = patch_index * patches + jnp.arange(patches, dtype=jnp.int32)
    bucket_ends = jnp.cumsum(bucket_sizes)
    clip_ids = jnp.sum((patch_ids[:, None] >= bucket_ends[None, :]).astype(jnp.int32), axis=1)
    onehot = (clip_ids[:, None] == jnp.arange(clips, dtype=jnp.int32)[None, :]).astype(f32)
    slot_ids = jnp.arange(frames, dtype=jnp.int32)
    valid = (slot_ids < count)[:, None] & (patch_mask[None, :] == 1)
    features = time_features(timesteps, full_time.shape[0]).astype(bf16)
    modulation = table.astype(f32) + forward_dot(features, full_time).reshape(clips, 6, width)
    per_patch = jnp.einsum("pc,ckd->pkd", onehot, modulation, precision=HIGH)
    shift_a = per_patch[:, 0]
    scale_a = per_patch[:, 1]
    gate_a = per_patch[:, 2]
    shift_m = per_patch[:, 3]
    scale_m = per_patch[:, 4]
    gate_m = per_patch[:, 5]
    inputs_f = tokens.astype(f32)
    normed_a, modulate_a_vjp = jax.vjp(modulate, inputs_f, shift_a, scale_a)
    normed_r = normed_a.astype(bf16).reshape(row_count, width)
    qkv_bias = jnp.concatenate([bias_f[0], jnp.zeros((width,), f32), bias_f[1]])
    qkv_r = (
        (forward_dot(normed_r, full_qkv) + qkv_bias)
        .astype(bf16)
        .reshape(frames, patches, 3 * width)
    )
    queries_r = qkv_r[..., :width]
    keyval_r = qkv_r[..., width:]
    last_kv = lax.dynamic_index_in_dim(keyval_r, count - 1, 0, keepdims=False)
    edges = jnp.stack([keyval_r[0], last_kv])
    outer_kv = with_halo(edges, (("frames", 0),), 1)
    keys_all = jnp.concatenate([outer_kv[0:1], keyval_r, outer_kv[3:4]], axis=0)
    prev_ok = frame_index > 0
    next_ok = frame_index < lax.axis_size("frames") - 1
    query_slot = slot_ids[:, None]
    key_place = jnp.arange(frames + 2, dtype=jnp.int32)[None, :]
    key_slot = key_place - 1
    slot_keys = (
        (key_place >= 1)
        & (key_place <= frames)
        & (jnp.abs(key_slot - query_slot) <= 1)
        & (key_slot < count)
    )
    prev_keys = (key_place == 0) & (query_slot == 0) & prev_ok
    next_keys = (key_place == frames + 1) & (query_slot == count - 1) & next_ok
    key_mask = slot_keys | prev_keys | next_keys
    attn_in, attend_vjp = jax.vjp(
        partial(self_attend, key_mask=key_mask, heads=heads),
        queries_r.astype(f32),
        keys_all.astype(f32),
    )
    attn_r = attn_in.astype(bf16).reshape(row_count, width)
    attn_out = (forward_dot(attn_r, full_out) + bias_f[2]).reshape(frames, patches, width)
    resid_a = inputs_f + gate_a * attn_out
    captions_used = jnp.where(null_mask[:, None, None] == 1, null_embed[None], caption).reshape(
        clips * cap_len, width
    )
    kv_bias = jnp.concatenate([jnp.zeros((width,), f32), bias_f[4]])
    cross_kv_r = (forward_dot(captions_used, full_kv) + kv_bias).astype(bf16)
    cross_keys = cross_kv_r[:, :width].reshape(clips * cap_len, heads, head_dim)
    cross_vals = cross_kv_r[:, width:].reshape(clips * cap_len, heads, head_dim)
    resid_a_r = resid_a.astype(bf16).reshape(row_count, width)
    cross_queries = (
        (forward_dot(resid_a_r, full_q) + bias_f[3])
        .astype(bf16)
        .reshape(row_count, heads, head_dim)
    )
    token_clip = jnp.broadcast_to(clip_ids[None, :], (frames, patches)).reshape(row_count)
    key_clip = jnp.repeat(jnp.arange(clips, dtype=jnp.int32), cap_len)
    same_clip = token_clip[:, None] == key_clip[None, :]
    scores = (
        jnp.einsum("rhd,khd->rhk", cross_queries, cross_keys, preferred_element_type=f32) * scale
    )
    scores = jnp.where(same_clip[:, None, :], scores, -1000000000.0)
    probs = jax.nn.softmax(scores, axis=-1)
    probs_r = probs.astype(bf16)
    cross_mix = (
        jnp.einsum("rhk,khd->rhd", probs_r, cross_vals, preferred_element_type=f32)
        .astype(bf16)
        .reshape(row_count, width)
    )
    cross_res = forward_dot(cross_mix, full_cross_out) + bias_f[5]
    resid_c = resid_a + cross_res.reshape(frames, patches, width)
    normed_m, modulate_m_vjp = jax.vjp(modulate, resid_c, shift_m, scale_m)
    normed_m_r = normed_m.astype(bf16).reshape(row_count, width)
    pre_act = forward_dot(normed_m_r, full_in) + bias_hidden
    activ, gelu_vjp = jax.vjp(gelu_tanh, pre_act)
    activ_r = activ.astype(bf16)
    mlp_res = (forward_dot(activ_r, full_mlp_out) + bias_f[6]).reshape(frames, patches, width)
    final = resid_c + gate_m * mlp_res
    block_out = jnp.where(valid[:, :, None], final, 0.0).astype(bf16)
    grad_final = jnp.where(valid[:, :, None], cotangent.astype(f32), 0.0)
    grad_gate_m = jnp.sum(grad_final * mlp_res, axis=0)
    grad_mlp_r = (gate_m * grad_final).astype(bf16).reshape(row_count, width)
    bias_mo_grad = jnp.sum(grad_mlp_r.astype(f32), axis=0)
    mlp_out_grad = outer_sum(activ_r, grad_mlp_r)
    grad_act = times_transposed(grad_mlp_r, full_mlp_out)
    grad_pre_r = gelu_vjp(grad_act)[0].astype(bf16)
    bias_hidden_grad = jnp.sum(grad_pre_r.astype(f32), axis=0)
    mlp_in_grad = outer_sum(normed_m_r, grad_pre_r)
    grad_norm_m = times_transposed(grad_pre_r, full_in).reshape(frames, patches, width)
    resid_c_part, grad_shift_m, grad_scale_m = modulate_m_vjp(grad_norm_m)
    grad_resid_c = grad_final + resid_c_part
    grad_cross_r = grad_resid_c.astype(bf16).reshape(row_count, width)
    bias_co_grad = jnp.sum(grad_cross_r.astype(f32), axis=0)
    cross_out_grad = outer_sum(cross_mix, grad_cross_r)
    grad_mix_r = (
        times_transposed(grad_cross_r, full_cross_out)
        .astype(bf16)
        .reshape(row_count, heads, head_dim)
    )
    grad_probs = jnp.einsum("rhd,khd->rhk", grad_mix_r, cross_vals, preferred_element_type=f32)
    grad_vals = jnp.einsum("rhk,rhd->khd", probs_r, grad_mix_r, preferred_element_type=f32)
    grad_scores_r = (
        probs * (grad_probs - jnp.sum(grad_probs * probs, axis=-1, keepdims=True))
    ).astype(bf16)
    grad_cq = (
        jnp.einsum("rhk,khd->rhd", grad_scores_r, cross_keys, preferred_element_type=f32) * scale
    )
    grad_cq_r = grad_cq.astype(bf16).reshape(row_count, width)
    grad_keys = (
        jnp.einsum("rhk,rhd->khd", grad_scores_r, cross_queries, preferred_element_type=f32) * scale
    )
    bias_cq_grad = jnp.sum(grad_cq_r.astype(f32), axis=0)
    cross_q_grad = outer_sum(resid_a_r, grad_cq_r)
    grad_resid_a = grad_resid_c + times_transposed(grad_cq_r, full_q).reshape(
        frames, patches, width
    )
    cross_kv_part = jnp.concatenate(
        [grad_keys.reshape(clips * cap_len, width), grad_vals.reshape(clips * cap_len, width)],
        axis=1,
    )
    grad_gate_a = jnp.sum(grad_resid_a * attn_out, axis=0)
    grad_attn_r = (gate_a * grad_resid_a).astype(bf16).reshape(row_count, width)
    bias_o_grad = jnp.sum(grad_attn_r.astype(f32), axis=0)
    self_out_grad = outer_sum(attn_r, grad_attn_r)
    grad_attn_in = round_trip(times_transposed(grad_attn_r, full_out)).reshape(
        frames, patches, width
    )
    grad_queries, grad_keys_all = attend_vjp(grad_attn_in)
    returns = jnp.stack([grad_keys_all[0], grad_keys_all[frames + 1]])
    back_kv = with_halo(returns.astype(jnp.bfloat16), (("frames", 0),), 1).astype(returns.dtype)
    first_slot = (slot_ids == 0)[:, None, None]
    last_slot = (slot_ids == count - 1)[:, None, None]
    grad_kv = (
        grad_keys_all[1 : frames + 1]
        + jnp.where(first_slot, back_kv[0][None], 0.0)
        + jnp.where(last_slot, back_kv[3][None], 0.0)
    )
    grad_qkv_r = (
        jnp.concatenate([grad_queries, grad_kv], axis=-1).astype(bf16).reshape(row_count, 3 * width)
    )
    bias_q_grad = jnp.sum(grad_qkv_r[:, :width].astype(f32), axis=0)
    bias_v_grad = jnp.sum(grad_qkv_r[:, 2 * width :].astype(f32), axis=0)
    self_qkv_grad = outer_sum(normed_r, grad_qkv_r)
    grad_norm_a = times_transposed(grad_qkv_r, full_qkv).reshape(frames, patches, width)
    input_part, grad_shift_a, grad_scale_a = modulate_a_vjp(grad_norm_a)
    input_grad = grad_resid_a + input_part
    per_patch_grad = jnp.stack(
        [grad_shift_a, grad_scale_a, grad_gate_a, grad_shift_m, grad_scale_m, grad_gate_m], axis=1
    )
    mod_part = jnp.einsum("pc,pkd->ckd", onehot, per_patch_grad, precision=HIGH)
    bias_part = jnp.stack(
        [
            bias_q_grad,
            bias_v_grad,
            bias_o_grad,
            bias_cq_grad,
            jnp.zeros((width,), f32),
            bias_co_grad,
            bias_mo_grad,
        ]
    )
    kv_total, bias_total, hidden_total, mod_total = lax.psum(
        (cross_kv_part, bias_part, bias_hidden_grad, mod_part), ("frames", "patches")
    )
    kv_total_r = kv_total.astype(bf16)
    bias_cv_grad = jnp.sum(kv_total_r[:, width:].astype(f32), axis=0)
    bias_rows_ids = jnp.arange(bias_total.shape[0], dtype=jnp.int32)
    biases_grad = bias_total + jnp.where((bias_rows_ids == 4)[:, None], bias_cv_grad[None, :], 0.0)
    cross_kv_full = outer_sum(captions_used, kv_total_r)
    caption_rows = times_transposed(kv_total_r, full_kv).reshape(clips, cap_len, width)
    dropped = (null_mask == 1)[:, None, None]
    caption_grad = jnp.where(dropped, 0.0, caption_rows)
    null_grad = jnp.sum(jnp.where(dropped, caption_rows, 0.0), axis=0)
    table_grad = jnp.sum(mod_total, axis=0)
    time_full = jnp.dot(features.astype(f32).T, mod_total.reshape(clips, 6 * width), precision=HIGH)
    time_proj_grad = lax.dynamic_slice(
        time_full,
        (patch_index * time_proj.shape[0], frame_index * time_proj.shape[1]),
        time_proj.shape,
    )
    cross_kv_grad = lax.dynamic_slice(
        cross_kv_full,
        (patch_index * cross_kv.shape[0], frame_index * cross_kv.shape[1]),
        cross_kv.shape,
    )
    grads = (self_qkv_grad, self_out_grad, cross_q_grad, cross_out_grad, mlp_in_grad, mlp_out_grad)
    row_sums = (
        lax.psum_scatter(
            grads[0].astype(jnp.bfloat16), "patches", scatter_dimension=0, tiled=True
        ).astype(jnp.float32),
        lax.psum_scatter(
            grads[1].astype(jnp.bfloat16), "patches", scatter_dimension=0, tiled=True
        ).astype(jnp.float32),
        lax.psum_scatter(
            grads[2].astype(jnp.bfloat16), "patches", scatter_dimension=0, tiled=True
        ).astype(jnp.float32),
        lax.psum_scatter(
            grads[3].astype(jnp.bfloat16), "patches", scatter_dimension=0, tiled=True
        ).astype(jnp.float32),
        lax.psum_scatter(
            grads[4].astype(jnp.bfloat16), "patches", scatter_dimension=0, tiled=True
        ).astype(jnp.float32),
        lax.psum_scatter(
            grads[5].astype(jnp.bfloat16), "patches", scatter_dimension=0, tiled=True
        ).astype(jnp.float32),
    )
    col_sums = (
        lax.psum_scatter(
            row_sums[0].astype(jnp.bfloat16), "frames", scatter_dimension=1, tiled=True
        ).astype(jnp.float32),
        lax.psum_scatter(
            row_sums[1].astype(jnp.bfloat16), "frames", scatter_dimension=1, tiled=True
        ).astype(jnp.float32),
        lax.psum_scatter(
            row_sums[2].astype(jnp.bfloat16), "frames", scatter_dimension=1, tiled=True
        ).astype(jnp.float32),
        lax.psum_scatter(
            row_sums[3].astype(jnp.bfloat16), "frames", scatter_dimension=1, tiled=True
        ).astype(jnp.float32),
        lax.psum_scatter(
            row_sums[4].astype(jnp.bfloat16), "frames", scatter_dimension=1, tiled=True
        ).astype(jnp.float32),
        lax.psum_scatter(
            row_sums[5].astype(jnp.bfloat16), "frames", scatter_dimension=1, tiled=True
        ).astype(jnp.float32),
    )
    qkv_shard, out_shard, q_shard, cross_out_shard, in_shard, mlp_out_shard = col_sums
    return (
        block_out,
        input_grad,
        caption_grad,
        null_grad,
        table_grad,
        time_proj_grad,
        qkv_shard,
        out_shard,
        q_shard,
        cross_kv_grad,
        cross_out_shard,
        in_shard,
        mlp_out_shard,
        biases_grad,
        hidden_total,
    )


BF = jnp.bfloat16
F32 = jnp.float32
VMEM_LIMIT = 60 * 2**20
NEG = -1e30
IN_VMEM = pl.BlockSpec(memory_space=pltpu.VMEM)
IN_ANY = pl.BlockSpec(memory_space=pl.ANY)
IN_SMEM = pl.BlockSpec(memory_space=pltpu.SMEM)
GELU_C = math.sqrt(2.0 / math.pi)


def dot(a, b):
    return jnp.dot(a, b, preferred_element_type=F32)


def dot_nt(a, b):
    return lax.dot_general(a, b, (((1,), (1,)), ((), ())), preferred_element_type=F32)


def dot_tn(a, b):
    return lax.dot_general(a, b, (((0,), (0,)), ((), ())), preferred_element_type=F32)


def gelu_parts(v):
    square = v * v
    inner = GELU_C * (v + 0.044715 * (v * square))
    t = jnp.tanh(inner)
    half = 0.5 * (1.0 + t)
    act = v * half
    slope = half + (0.5 * GELU_C) * v * (1.0 - t * t) * (1.0 + (3 * 0.044715) * square)
    return act, slope


def normalise(v):
    mean = jnp.mean(v, axis=-1, keepdims=True)
    cen = v - mean
    var = jnp.mean(cen * cen, axis=-1, keepdims=True)
    rstd = lax.rsqrt(var + 1e-06)
    return cen * rstd, rstd


def normalise_back(xhat, rstd, g, scale):
    h = g * (1.0 + scale)
    a = jnp.mean(h, axis=-1, keepdims=True)
    b = jnp.mean(h * xhat, axis=-1, keepdims=True)
    return rstd * (h - a - xhat * b)


def rows_at(start, size):
    return pl.ds(pl.multiple_of(start, 16), size)


def each(count, fn):
    def step(i, carry):
        fn(i)
        return carry

    lax.fori_loop(0, count, step, 0)


def norm_body(x_ref, mods_ref, out_ref, patches):
    def frame(s):
        r = rows_at(s * patches, patches)
        xhat, _ = normalise(x_ref[r, :].astype(F32))
        out_ref[r, :] = (xhat * (1.0 + mods_ref[1]) + mods_ref[0]).astype(BF)

    each(x_ref.shape[0] // patches, frame)


def key_ok(t, per, patches, j, count, y):
    rows = per * patches
    row = lax.broadcasted_iota(jnp.int32, (rows, 128), 0)
    slot = jnp.zeros((rows, 128), jnp.int32)
    for i in range(1, per):
        slot = slot + (row >= i * patches).astype(jnp.int32)
    key = slot + (t * per + j - 1)
    low = (key >= 0) | (y > 0)
    high = (key < count) | ((key == count) & (y < 1))
    return low & high


def spread(p, et_ref):
    hi = p.astype(BF)
    lo = (p - hi.astype(F32)).astype(BF)
    return dot(jnp.concatenate([hi, lo], axis=1), et_ref[...])


def attend_tile(t, per, patches, count, y, scale, q_ref, kvx_ref, e_ref, et_ref, probs_ref, attn_ref):
    rows = per * patches
    width = q_ref.shape[1]
    r = rows_at(t * rows, rows)
    q = q_ref[r, :].astype(F32)
    scores = []
    for j in range(3):
        kr = rows_at(t * rows + j * patches, rows)
        s = dot((q * kvx_ref[kr, :width].astype(F32)).astype(BF), e_ref[...]) * scale
        scores.append(jnp.where(key_ok(t, per, patches, j, count, y), s, NEG))
    top = jnp.maximum(jnp.maximum(scores[0], scores[1]), scores[2])
    ex = [jnp.exp(s - top) for s in scores]
    inv = 1.0 / (ex[0] + ex[1] + ex[2])
    total = None
    for j in range(3):
        p = ex[j] * inv
        probs_ref[j, r, :] = p
        kr = rows_at(t * rows + j * patches, rows)
        term = spread(p, et_ref) * kvx_ref[kr, width:].astype(F32)
        total = term if total is None else total + term
    attn_ref[r, :] = total.astype(BF)


def attend_tile_back(t, per, patches, scale, q_ref, kvx_ref, e_ref, et_ref, probs_ref, go_ref, gq_ref, gkv_ref):
    rows = per * patches
    width = q_ref.shape[1]
    r = rows_at(t * rows, rows)
    q = q_ref[r, :].astype(F32)
    go = go_ref[r, :].astype(F32)
    dps, ps = [], []
    for j in range(3):
        kr = rows_at(t * rows + j * patches, rows)
        dps.append(dot((go * kvx_ref[kr, width:].astype(F32)).astype(BF), e_ref[...]))
        ps.append(probs_ref[j, r, :])
    mean = dps[0] * ps[0] + dps[1] * ps[1] + dps[2] * ps[2]
    gq = None
    for j in range(3):
        kr = rows_at(t * rows + j * patches, rows)
        ds = spread(ps[j] * (dps[j] - mean) * scale, et_ref)
        term = ds * kvx_ref[kr, :width].astype(F32)
        gq = term if gq is None else gq + term
        gkv_ref[kr, :width] += ds * q
        gkv_ref[kr, width:] += spread(ps[j], et_ref) * go
    gq_ref[r, :] = gq.astype(BF)


def head_window(h, head_dim, width):
    return min(h * head_dim // 128 * 128, width - 256)


def head_lanes(h, head_dim, width):
    lane = lax.broadcasted_iota(jnp.int32, (1, 256), 1) + head_window(h, head_dim, width)
    return (lane >= h * head_dim) & (lane < (h + 1) * head_dim)


def cross_head(h, heads, tiles, q_ref, keys_ref, vals_ref, cmask_ref, lse_ref, mix_ref):
    width = q_ref.shape[1]
    head_dim = width // heads
    scale = head_dim ** (-0.5)
    w = head_window(h, head_dim, width)
    keep = head_lanes(h, head_dim, width)
    kw = jnp.where(keep, keys_ref[:, w : w + 256], 0)
    vw = jnp.where(keep, vals_ref[:, w : w + 256], 0)
    rows = q_ref.shape[0] // tiles
    for i in range(tiles):
        r = slice(i * rows, (i + 1) * rows)
        s = dot_nt(q_ref[r, w : w + 256], kw) * scale + cmask_ref[...]
        top = jnp.max(s, axis=-1, keepdims=True)
        ex = jnp.exp(s - top)
        total = jnp.sum(ex, axis=-1, keepdims=True)
        p = (ex * (1.0 / total)).astype(BF)
        lse_ref[r, h : h + 1] = top + jnp.log(total)
        mix_ref[r, w : w + 256] += dot(p, vw)


def cross_head_back(h, heads, tiles, q_ref, keys_ref, vals_ref, cmask_ref, lse_ref, gmix_ref, gq_ref, gkv_ref, p_buf, ds_buf):
    width = q_ref.shape[1]
    head_dim = width // heads
    scale = head_dim ** (-0.5)
    w = head_window(h, head_dim, width)
    keep = head_lanes(h, head_dim, width)
    kw = jnp.where(keep, keys_ref[:, w : w + 256], 0)
    vw = jnp.where(keep, vals_ref[:, w : w + 256], 0)
    rows = q_ref.shape[0] // tiles
    for i in range(tiles):
        r = slice(i * rows, (i + 1) * rows)
        s = dot_nt(q_ref[r, w : w + 256], kw) * scale + cmask_ref[...]
        p = jnp.exp(s - lse_ref[r, h : h + 1])
        dp = dot_nt(gmix_ref[r, w : w + 256], vw)
        ds = (p * (dp - jnp.sum(dp * p, axis=-1, keepdims=True))).astype(BF)
        p_buf[r, :] = p.astype(BF)
        ds_buf[r, :] = ds
        gq_ref[r, w : w + 256] += dot(ds, kw)
    gk = dot_tn(ds_buf[...], q_ref[:, w : w + 256]) * scale
    gv = dot_tn(p_buf[...], gmix_ref[:, w : w + 256])
    gkv_ref[0, :, w : w + 256] += jnp.where(keep, gk, 0.0)
    gkv_ref[1, :, w : w + 256] += jnp.where(keep, gv, 0.0)


class Place:
    def __init__(self):
        self.y=lax.axis_index("frames"); p=lax.axis_index("patches")
        self.z=p//4; self.x=lax.rem(p//2,2); self.c=lax.rem(p,2)
    def dev(self,y=None,z=None,x=None,c=None):
        y=self.y if y is None else y; z=self.z if z is None else z
        x=self.x if x is None else x; c=self.c if c is None else c
        return (y,(z*2+x)*2+c)
    def zoff(self,d): return lax.rem(self.z+d,4)

def barrier(pos):
    bar=pltpu.get_barrier_semaphore()
    peers=[pos.dev(z=pos.zoff(d)) for d in (1,2,3)]+[pos.dev(x=1-pos.x),pos.dev(y=1-pos.y),pos.dev(c=1-pos.c)]
    for t in peers: pl.semaphore_signal(bar,inc=1,device_id=t,device_id_type=MESH)
    pl.semaphore_wait(bar,6)

N_AG=9
class Gather:
    def __init__(self,pos,shard,full,send,recv,first):
        self.pos=pos; self.shard=shard; self.full=full; self.send=send; self.recv=recv; self.first=first
    def _rc(self,i,src,dst,dev):
        return pltpu.make_async_remote_copy(src_ref=src,dst_ref=dst,send_sem=self.send.at[i],recv_sem=self.recv.at[i],device_id=dev,device_id_type=MESH)
    def _copies(self):
        p=self.pos; F=self.full; y,z,x,c=p.y,p.z,p.x,p.c
        cs=[]
        mine=F.at[y,z,x,c]
        for d in (1,2,3):
            cs.append(self._rc(d-1,self.shard,mine,p.dev(z=p.zoff(d))))
        line=F.at[y,:,x,c]
        if self.first=="x":
            cs.append(self._rc(3,line,line,p.dev(x=1-x)))
            plane=F.at[y,:,:,c]
            cs.append(self._rc(4,plane,plane,p.dev(y=1-y)))
            got1=F.at[y,:,1-x,c]; got2=F.at[1-y,:,:,c]
        else:
            cs.append(self._rc(3,line,line,p.dev(y=1-y)))
            plane=F.at[:,:,x,c]
            cs.append(self._rc(4,plane,plane,p.dev(x=1-x)))
            got1=F.at[1-y,:,x,c]; got2=F.at[:,:,1-x,c]
        o=p.dev(c=1-c)
        cs.append(self._rc(5,line,line,o)); cs.append(self._rc(6,got1,got1,o)); cs.append(self._rc(7,got2,got2,o))
        return cs
    def start(self):
        self.cs=self._copies()
        p=self.pos
        for i in (0,1,2): self.cs[i].start()
        self.loc=pltpu.make_async_copy(self.shard,self.full.at[p.y,p.z,p.x,p.c],self.send.at[8])
        self.loc.start()
    def step1(self):
        self.loc.wait()
        for i in (0,1,2): self.cs[i].wait_recv()
        self.cs[3].start(); self.cs[5].start()
    def step2(self):
        self.cs[3].wait_recv(); self.cs[4].start(); self.cs[6].start()
    def step3(self):
        self.cs[4].wait_recv(); self.cs[7].start()
    def finish(self):
        for i in (5,6,7): self.cs[i].wait_recv()
        for i in range(8): self.cs[i].wait_send()

N_RS=6
class Scatter:
    def __init__(self,pos,part,out,bufs,send,recv,first):
        self.pos=pos; self.part=part; self.out=out; self.send=send; self.recv=recv; self.first=first
        self.own,self.r1,self.r2,self.r3,self.r4=bufs
    def _rc(self,i,src,dst,dev):
        return pltpu.make_async_remote_copy(src_ref=src,dst_ref=dst,send_sem=self.send.at[i],recv_sem=self.recv.at[i],device_id=dev,device_id_type=MESH)
    def start(self):
        p=self.pos
        self.loc=pltpu.make_async_copy(self.part.at[:,:,:,p.c],self.own,self.send.at[6])
        self.cc=self._rc(0,self.part.at[:,:,:,1-p.c],self.r1,p.dev(c=1-p.c))
        self.loc.start(); self.cc.start()
    def step1(self):
        p=self.pos; own=self.own
        self.loc.wait(); self.cc.wait_recv()
        def body(i,_):
            f,r=i//8,lax.rem(i,8); z,x=r//2,lax.rem(r,2)
            own[f,z,x]=(own[f,z,x].astype(jnp.float32)+self.r1[f,z,x].astype(jnp.float32)).astype(jnp.bfloat16)
            return 0
        lax.fori_loop(0,16,body,0)
        if self.first=="y": self.c1=self._rc(1,own.at[1-p.y],self.r2,p.dev(y=1-p.y))
        else: self.c1=self._rc(1,own.at[:,:,1-p.x],self.r2,p.dev(x=1-p.x))
        self.c1.start()
    def step2(self):
        p=self.pos; own=self.own
        self.c1.wait_recv()
        def body(i,_):
            if self.first=="y": f,z,x=p.y,i//2,lax.rem(i,2); a,b=z,x
            else: f,z,x=i//4,lax.rem(i,4),p.x; a,b=f,z
            own[f,z,x]=(own[f,z,x].astype(jnp.float32)+self.r2[a,b].astype(jnp.float32)).astype(jnp.bfloat16)
            return 0
        lax.fori_loop(0,8,body,0)
        if self.first=="y": self.c2=self._rc(2,own.at[p.y,:,1-p.x],self.r3,p.dev(x=1-p.x))
        else: self.c2=self._rc(2,own.at[1-p.y,:,p.x],self.r3,p.dev(y=1-p.y))
        self.c2.start()
    def step3(self):
        p=self.pos; own=self.own
        self.c2.wait_recv()
        def body(z,_):
            own[p.y,z,p.x]=(own[p.y,z,p.x].astype(jnp.float32)+self.r3[z].astype(jnp.float32)).astype(jnp.bfloat16)
            return 0
        lax.fori_loop(0,4,body,0)
        self.cz=[self._rc(2+d,own.at[p.y,p.zoff(d),p.x],self.r4.at[d-1],p.dev(z=p.zoff(d))) for d in (1,2,3)]
        for c in self.cz: c.start()
    def step4(self):
        p=self.pos
        for c in self.cz: c.wait_recv()
        f32=jnp.float32
        self.out[...]=((self.own[p.y,p.z,p.x].astype(f32)+self.r4[0].astype(f32))+(self.r4[1].astype(f32)+self.r4[2].astype(f32)))
    def finish(self):
        for c in [self.cc,self.c1,self.c2]+self.cz: c.wait_send()
def scatter_bufs(R,C,first):
    bf=jnp.bfloat16
    return [pltpu.VMEM((2,4,2,R,C),bf),pltpu.VMEM((2,4,2,R,C),bf),
      pltpu.VMEM((4,2,R,C) if first=="y" else (2,4,R,C),bf),pltpu.VMEM((4,R,C),bf),pltpu.VMEM((3,R,C),bf)]


def part_of(ref, rows, cols, lead):
    index = [slice(None)] * lead
    index.append(pl.ds(*rows) if rows else slice(None))
    index.append(pl.ds(*cols) if cols else slice(None))
    return ref.at[tuple(index)]


def gather_kernel(units, count, *refs):
    shards, fulls = refs[:count], refs[count : 2 * count]
    send, recv = refs[2 * count :]
    pos = Place()
    barrier(pos)
    work = [
        Gather(
            pos,
            part_of(shards[a], r, c, 0),
            part_of(fulls[a], r, c, 4),
            send.at[k],
            recv.at[k],
            first,
        )
        for k, (a, r, c, first) in enumerate(units)
    ]
    for unit in work:
        unit.start()
    total = len(work)
    for t in range(total + 2):
        if t < total:
            work[t].step1()
        if 0 <= t - 1 < total:
            work[t - 1].step2()
        if 0 <= t - 2 < total:
            work[t - 2].step3()
    for unit in work:
        unit.finish()


def gather_call(shards, units, ident):
    count = len(shards)
    return pl.pallas_call(
        partial(gather_kernel, units, count),
        out_shape=[jax.ShapeDtypeStruct((2, 4, 2, 2) + s.shape, s.dtype) for s in shards],
        in_specs=[pl.BlockSpec(memory_space=pl.ANY)] * count,
        out_specs=[pl.BlockSpec(memory_space=pl.ANY)] * count,
        scratch_shapes=[
            pltpu.SemaphoreType.DMA((len(units), N_AG)),
            pltpu.SemaphoreType.DMA((len(units), 8)),
        ],
        compiler_params=pltpu.CompilerParams(collective_id=ident, has_side_effects=True),
        name="gather",
    )(*shards)


def scatter_kernel(units, count, *refs):
    parts, outs = refs[:count], refs[count : 2 * count]
    rest = refs[2 * count :]
    send, recv = rest[-2:]
    pos = Place()
    barrier(pos)
    work = [
        Scatter(
            pos,
            part_of(parts[a], r, c, 4),
            part_of(outs[a], r, c, 0),
            rest[5 * k : 5 * k + 5],
            send.at[k],
            recv.at[k],
            first,
        )
        for k, (a, r, c, first) in enumerate(units)
    ]
    total = len(work)
    for unit in work:
        unit.start()
    for t in range(total + 3):
        if t < total:
            work[t].step1()
        if 0 <= t - 1 < total:
            work[t - 1].step2()
        if 0 <= t - 2 < total:
            work[t - 2].step3()
        if 0 <= t - 3 < total:
            work[t - 3].step4()
    for unit in work:
        unit.finish()


def scatter_call(parts, units, ident):
    count = len(parts)
    scratch = []
    for a, r, c, first in units:
        rows, cols = parts[a].shape[-2:]
        scratch += scatter_bufs(r[1] if r else rows, c[1] if c else cols, first)
    return pl.pallas_call(
        partial(scatter_kernel, units, count),
        out_shape=[jax.ShapeDtypeStruct(p.shape[-2:], jnp.float32) for p in parts],
        in_specs=[pl.BlockSpec(memory_space=pl.ANY)] * count,
        out_specs=[pl.BlockSpec(memory_space=pltpu.VMEM)] * count,
        scratch_shapes=scratch
        + [
            pltpu.SemaphoreType.DMA((len(units), 7)),
            pltpu.SemaphoreType.DMA((len(units), N_RS)),
        ],
        compiler_params=pltpu.CompilerParams(
            collective_id=ident, has_side_effects=True, vmem_limit_bytes=60 * 2**20
        ),
        name="scatter",
    )(*parts)


def attend_kernel(
    patches, heads, nm_ref, x_ref, mods_ref, w1_ref, w2_ref, qb_ref, ob_ref, e_ref, et_ref, info_ref,
    wqkv_ref, wo_ref, q_ref, kvx_ref, probs_ref, attn_ref, ao_ref, resid_ref, residb_ref,
    w1_buf, w2_buf, wqkv_buf, wo_buf, halo_out, halo_in, sems, send, recv,
):
    pos = Place()
    rows, width = x_ref.shape
    frames = rows // patches
    count, y = info_ref[0], info_ref[1]
    loads = (
        pltpu.make_async_copy(w1_ref, w1_buf, sems.at[0]),
        pltpu.make_async_copy(w2_ref, w2_buf, sems.at[1]),
    )
    for c in loads:
        c.start()
    pair_barrier(pos)
    cut = 3 * width // 2
    half = width // 2
    loads[0].wait()
    for f in range(2):
        wqkv_buf[:, f * cut : (f + 1) * cut] = w1_buf[f, :, :cut]
    loads[1].wait()
    for f in range(2):
        wo_buf[:, f * half : (f + 1) * half] = w2_buf[f, :, :half]
    keep = (
        pltpu.make_async_copy(wqkv_buf, wqkv_ref, sems.at[2]),
        pltpu.make_async_copy(wo_buf, wo_ref, sems.at[3]),
    )
    for c in keep:
        c.start()
    zero = jnp.zeros((patches, 2 * width), BF)
    kvx_ref[0:patches, :] = zero
    kvx_ref[(frames + 1) * patches :, :] = zero
    own = slice(patches, (frames + 1) * patches)
    for third in (1, 2, 0):
        cols = slice(third * width, (third + 1) * width)
        got = (dot(nm_ref[...], wqkv_buf[:, cols]) + qb_ref[:, cols]).astype(BF)
        if third == 0:
            q_ref[...] = got
        else:
            kvx_ref[own, (third - 1) * width : third * width] = got
        if third == 2:
            copy = halo_send(pos, frames, patches, count, y, kvx_ref, halo_out, halo_in, send, recv)
    copy.wait()
    place = jnp.where(y == 0, count, -1) + 1

    def settle(s):
        r = rows_at(s * patches, patches)
        hit = jnp.full((patches, 2 * width), (s == place).astype(F32), F32)
        kvx_ref[r, :] = jnp.where(hit > 0.5, halo_in[...].astype(F32), kvx_ref[r, :].astype(F32)).astype(BF)

    each(frames + 2, settle)
    scale = (width // heads) ** (-0.5)
    each(
        frames // 3,
        lambda t: attend_tile(t, 3, patches, count, y, scale, q_ref, kvx_ref, e_ref, et_ref, probs_ref, attn_ref),
    )
    resid_ref[...] = dot(attn_ref[...], wo_buf[...]) + ob_ref[...]

    def frame(s):
        r = rows_at(s * patches, patches)
        ao = resid_ref[r, :]
        ao_ref[r, :] = ao.astype(BF)
        resid = x_ref[r, :].astype(F32) + mods_ref[2] * ao
        resid_ref[r, :] = resid
        residb_ref[r, :] = resid.astype(BF)

    each(frames, frame)
    for c in keep:
        c.wait()


def pair_barrier(pos):
    bar = pltpu.get_barrier_semaphore()
    pl.semaphore_signal(bar, inc=1, device_id=pos.dev(y=1 - pos.y), device_id_type=MESH)
    pl.semaphore_wait(bar, 1)


def pick_slot(frames, patches, slot, src_ref, dst_ref):
    dst_ref[...] = jnp.zeros(dst_ref.shape, dst_ref.dtype)

    def step(s):
        r = rows_at(s * patches, patches)
        hit = jnp.full(dst_ref.shape, (s == slot).astype(F32), F32)
        dst_ref[...] = jnp.where(hit > 0.5, src_ref[r, :].astype(F32), dst_ref[...].astype(F32)).astype(dst_ref.dtype)

    each(frames, step)


def halo_send(pos, frames, patches, count, y, kvx_ref, halo_out, halo_in, send, recv):
    pick_slot(frames + 2, patches, jnp.where(y == 0, count - 1, 0) + 1, kvx_ref, halo_out)
    copy = pltpu.make_async_remote_copy(
        src_ref=halo_out, dst_ref=halo_in, send_sem=send, recv_sem=recv,
        device_id=pos.dev(y=1 - pos.y), device_id_type=MESH,
    )
    copy.start()
    return copy


def attend_call(patches, heads, nm, x, mods, w1, w2, qb, ob, e, et, info, ident):
    rows, width = x.shape
    frames = rows // patches
    ext = (frames + 2) * patches
    S = jax.ShapeDtypeStruct
    return pl.pallas_call(
        partial(attend_kernel, patches, heads),
        out_shape=[
            S((width, 3 * width), BF), S((width, width), BF), S((rows, width), BF), S((ext, 2 * width), BF),
            S((3, rows, 128), F32), S((rows, width), BF), S((rows, width), BF), S((rows, width), F32), S((rows, width), BF),
        ],
        in_specs=[IN_VMEM] * 3 + [IN_ANY] * 2 + [IN_VMEM] * 4 + [IN_SMEM],
        out_specs=[IN_ANY] * 2 + [IN_VMEM] * 7,
        scratch_shapes=[
            pltpu.VMEM(w1.shape, BF), pltpu.VMEM(w2.shape, BF), pltpu.VMEM((width, 3 * width), BF), pltpu.VMEM((width, width), BF),
            pltpu.VMEM((patches, 2 * width), BF), pltpu.VMEM((patches, 2 * width), BF),
            pltpu.SemaphoreType.DMA((4,)), pltpu.SemaphoreType.DMA, pltpu.SemaphoreType.DMA,
        ],
        compiler_params=pltpu.CompilerParams(collective_id=ident, has_side_effects=True, vmem_limit_bytes=VMEM_LIMIT),
        name="attend",
    )(nm, x, mods, w1, w2, qb, ob, e, et, info)


def norm_call(patches, x, mods):
    return pl.pallas_call(
        lambda x_ref, m_ref, o_ref: norm_body(x_ref, m_ref, o_ref, patches),
        out_shape=jax.ShapeDtypeStruct(x.shape, BF), in_specs=[IN_VMEM] * 2, out_specs=IN_VMEM, name="norm",
    )(x, mods)


def cross_kernel(
    patches, heads, resid_ref, residb_ref, mods_ref, used_ref, cm_ref, w2_ref, w3_ref, kv_ref, b3_ref, b4_ref, b5_ref,
    wq_ref, wco_ref, q_ref, keys_ref, vals_ref, lse_ref, mixb_ref, rc_ref, nm_ref,
    w2_buf, w3_buf, kv_buf, wq_buf, wco_buf, mix_buf, cmask, sems,
):
    rows, width = resid_ref.shape
    frames = rows // patches
    half = width // 2
    loads = (
        pltpu.make_async_copy(kv_ref, kv_buf, sems.at[0]),
        pltpu.make_async_copy(w2_ref, w2_buf, sems.at[1]),
        pltpu.make_async_copy(w3_ref, w3_buf, sems.at[4]),
    )
    for c in loads:
        c.start()
    for i in range(3):
        cmask[i * patches : (i + 1) * patches, :] = cm_ref[...]
    mix_buf[...] = jnp.zeros(mix_buf.shape, F32)
    loads[0].wait()
    keys_ref[...] = dot(used_ref[...], kv_buf[0]).astype(BF)
    vals_ref[...] = (dot(used_ref[...], kv_buf[1]) + b4_ref[...]).astype(BF)
    loads[1].wait()
    loads[2].wait()
    for f in range(2):
        wq_buf[:, f * half : (f + 1) * half] = w2_buf[f]
        wco_buf[:, f * half : (f + 1) * half] = w3_buf[f]
    keep = (
        pltpu.make_async_copy(wq_buf, wq_ref, sems.at[2]),
        pltpu.make_async_copy(wco_buf, wco_ref, sems.at[3]),
    )
    for c in keep:
        c.start()
    q_ref[...] = (dot(residb_ref[...], wq_buf[...]) + b3_ref[...]).astype(BF)
    for h in range(heads):
        cross_head(h, heads, rows // cmask.shape[0], q_ref, keys_ref, vals_ref, cmask, lse_ref, mix_buf)
    mixb_ref[...] = mix_buf[...].astype(BF)
    rc_ref[...] = dot(mixb_ref[...], wco_buf[...]) + b5_ref[...]

    def frame(s):
        r = rows_at(s * patches, patches)
        rc = rc_ref[r, :] + resid_ref[r, :]
        rc_ref[r, :] = rc
        xhat, _ = normalise(rc)
        nm_ref[r, :] = (xhat * (1.0 + mods_ref[4]) + mods_ref[3]).astype(BF)

    each(frames, frame)
    for c in keep:
        c.wait()


def cross_call(patches, heads, resid, residb, mods, used, cm, w2, w3, kv, b3, b4, b5):
    rows, width = resid.shape
    caps = used.shape[0]
    S = jax.ShapeDtypeStruct
    return pl.pallas_call(
        partial(cross_kernel, patches, heads),
        out_shape=[
            S((width, width), BF), S((width, width), BF), S((rows, width), BF), S((caps, width), BF), S((caps, width), BF),
            S((rows, 128), F32), S((rows, width), BF), S((rows, width), F32), S((rows, width), BF),
        ],
        in_specs=[IN_VMEM] * 5 + [IN_ANY] * 3 + [IN_VMEM] * 3,
        out_specs=[IN_ANY] * 2 + [IN_VMEM] * 7,
        scratch_shapes=[
            pltpu.VMEM(w2.shape, BF), pltpu.VMEM(w3.shape, BF), pltpu.VMEM(kv.shape, BF), pltpu.VMEM((width, width), BF), pltpu.VMEM((width, width), BF),
            pltpu.VMEM((rows, width), F32), pltpu.VMEM((3 * patches, caps), F32), pltpu.SemaphoreType.DMA((5,)),
        ],
        compiler_params=pltpu.CompilerParams(vmem_limit_bytes=VMEM_LIMIT),
        name="cross",
    )(resid, residb, mods, used, cm, w2, w3, kv, b3, b4, b5)


def mlp_kernel(
    chunk, patches, nm_ref, cot_ref, valid_ref, rc_ref, mods_ref, hb_ref, b6_ref, win_ref, wout_ref,
    out_ref, grc_ref, hsum_ref, bsum_ref, gp_ref, dwin_ref, dwout_ref,
    gm_ref, res_ref, win_b, wout_h, wout_b, act_b, gpre_b, din_s, dout_s, in_sem, out_sem,
):
    rows, width = nm_ref.shape
    frames = rows // patches
    half = wout_ref.shape[2]
    per = win_ref.shape[2] // chunk
    total = 2 * per

    def loads(j, slot):
        f, u = j // per, lax.rem(j, per)
        cols = pl.ds(pl.multiple_of(u * chunk, 128), chunk)
        rws = pl.ds(pl.multiple_of(j * chunk, 128), chunk)
        return (
            pltpu.make_async_copy(win_ref.at[f, :, cols], win_b.at[slot], in_sem.at[slot, 0]),
            pltpu.make_async_copy(wout_ref.at[:, rws], wout_h.at[slot], in_sem.at[slot, 1]),
        )

    def stores(j, slot):
        f, u = j // per, lax.rem(j, per)
        cols = pl.ds(pl.multiple_of(u * chunk, 128), chunk)
        rws = pl.ds(pl.multiple_of(j * chunk, 128), chunk)
        return (
            pltpu.make_async_copy(din_s.at[slot], dwin_ref.at[f, :, cols], out_sem.at[slot, 0]),
            pltpu.make_async_copy(dout_s.at[slot], dwout_ref.at[:, rws], out_sem.at[slot, 1]),
        )

    for c in loads(0, 0):
        c.start()
    bsum_ref[...] = jnp.zeros(bsum_ref.shape, F32)
    gp_ref[...] = jnp.zeros(gp_ref.shape, F32)

    def prepare(s):
        r = rows_at(s * patches, patches)
        gf = jnp.where(valid_ref[r, :] > 0.5, cot_ref[r, :].astype(F32), 0.0)
        gm = (mods_ref[5] * gf).astype(BF)
        gm_ref[r, :] = gm
        bsum_ref[0:1, :] += jnp.sum(gm.astype(F32), axis=0, keepdims=True)

    each(frames, prepare)

    def step(j, carry):
        slot = lax.rem(j, 2)
        for c in loads(j, slot):
            c.wait()

        @pl.when(j + 1 < total)
        def _():
            for c in loads(j + 1, 1 - slot):
                c.start()

        @pl.when(j >= 2)
        def _():
            for c in stores(j - 2, slot):
                c.wait()

        wout_b[...] = jnp.concatenate([wout_h[slot, 0], wout_h[slot, 1]], axis=1)
        pre = dot(nm_ref[...], win_b[slot]) + hb_ref[pl.ds(j, 1), :]
        act, slope = gelu_parts(pre)
        act_b[...] = act.astype(BF)
        gpre = (dot_nt(gm_ref[...], wout_b[...]) * slope).astype(BF)
        gpre_b[...] = gpre
        hsum_ref[pl.ds(j, 1), :] = jnp.sum(gpre.astype(F32), axis=0, keepdims=True)
        part = dot(act_b[...], wout_b[...])
        back = dot_nt(gpre_b[...], win_b[slot])

        @pl.when(j == 0)
        def _():
            res_ref[...] = part
            grc_ref[...] = back

        @pl.when(j > 0)
        def _():
            res_ref[...] += part
            grc_ref[...] += back

        din_s[slot] = dot_tn(nm_ref[...], gpre_b[...]).astype(BF)
        d = dot_tn(act_b[...], gm_ref[...]).astype(BF)
        dout_s[slot, 0] = d[:, :half]
        dout_s[slot, 1] = d[:, half:]
        for c in stores(j, slot):
            c.start()
        return carry

    lax.fori_loop(0, total, step, 0)

    def finish(s):
        r = rows_at(s * patches, patches)
        ok = valid_ref[r, :] > 0.5
        rc = rc_ref[r, :]
        res = res_ref[r, :] + b6_ref[...]
        gf = jnp.where(ok, cot_ref[r, :].astype(F32), 0.0)
        out_ref[r, :] = jnp.where(ok, rc + mods_ref[5] * res, 0.0).astype(BF)
        xhat, rstd = normalise(rc)
        g = grc_ref[r, :]
        gp_ref[0] += g
        gp_ref[1] += g * xhat
        gp_ref[2] += gf * res
        grc_ref[r, :] = gf + normalise_back(xhat, rstd, g, mods_ref[4])

    each(frames, finish)
    for back in (2, 1):
        for c in stores(total - back, (total - back) % 2):
            c.wait()


def mlp_call(patches, nm, cot, valid, rc, mods, hb, b6, win, wout):
    rows, width = nm.shape
    chunk = 768
    total = 2 * win.shape[2] // chunk
    half = wout.shape[2]
    S = jax.ShapeDtypeStruct
    return pl.pallas_call(
        partial(mlp_kernel, chunk, patches),
        out_shape=[
            S((rows, width), BF), S((rows, width), F32), S((total, chunk), F32), S((8, width), F32), S((3, patches, width), F32),
            S(win.shape, BF), S(wout.shape, BF),
        ],
        in_specs=[IN_VMEM] * 7 + [IN_ANY] * 2,
        out_specs=[IN_VMEM] * 5 + [IN_ANY] * 2,
        scratch_shapes=[
            pltpu.VMEM((rows, width), BF), pltpu.VMEM((rows, width), F32),
            pltpu.VMEM((2, width, chunk), BF), pltpu.VMEM((2, 2, chunk, half), BF), pltpu.VMEM((chunk, width), BF),
            pltpu.VMEM((rows, chunk), BF), pltpu.VMEM((rows, chunk), BF),
            pltpu.VMEM((2, width, chunk), BF), pltpu.VMEM((2, 2, chunk, half), BF),
            pltpu.SemaphoreType.DMA((2, 2)), pltpu.SemaphoreType.DMA((2, 2)),
        ],
        compiler_params=pltpu.CompilerParams(vmem_limit_bytes=VMEM_LIMIT),
        name="mlp",
    )(nm, cot, valid, rc, mods, hb.reshape(total, chunk), b6, win, wout)


def cross_back_kernel(
    patches, heads, grc_ref, mixb_ref, q_ref, keys_ref, vals_ref, lse_ref, cm_ref, residb_ref, attn_ref, ao_ref, gate_ref,
    wco_ref, wq_ref, wo_ref,
    gra_ref, gai_ref, gkvb_ref, bsum_ref, gp_ref, dwo_ref, dwq_ref, dwco_ref,
    w_buf, gcb, gmix, gq, gkv, p_buf, ds_buf, cmask, dw_s, sems, out_sem,
):
    rows, width = grc_ref.shape
    frames = rows // patches
    half = width // 2
    scale = (width // heads) ** (-0.5)
    loads = [pltpu.make_async_copy(src, w_buf, sems.at[i]) for i, src in enumerate((wco_ref, wq_ref, wo_ref))]
    outs = [pltpu.make_async_copy(dw_s.at[i % 2], dst, out_sem.at[i]) for i, dst in enumerate((dwco_ref, dwq_ref, dwo_ref))]
    loads[0].start()
    for i in range(3):
        cmask[i * patches : (i + 1) * patches, :] = cm_ref[...]
    bsum_ref[...] = jnp.zeros(bsum_ref.shape, F32)
    gp_ref[...] = jnp.zeros(gp_ref.shape, F32)
    gkv[...] = jnp.zeros(gkv.shape, F32)
    gq[...] = jnp.zeros(gq.shape, F32)

    def first(s):
        r = rows_at(s * patches, patches)
        g = grc_ref[r, :].astype(BF)
        gcb[r, :] = g
        bsum_ref[0:1, :] += jnp.sum(g.astype(F32), axis=0, keepdims=True)

    each(frames, first)
    loads[0].wait()
    gmix[...] = dot_nt(gcb[...], w_buf[...]).astype(BF)
    loads[1].start()

    def weight_grad(k, left, right):
        d = dot_tn(left, right).astype(BF)
        for f in range(2):
            dw_s[k % 2, f] = d[:, f * half : (f + 1) * half]
        outs[k].start()

    weight_grad(0, mixb_ref[...], gcb[...])
    for h in range(heads):
        cross_head_back(
            h, heads, rows // cmask.shape[0], q_ref, keys_ref, vals_ref, cmask, lse_ref, gmix, gq, gkv, p_buf, ds_buf
        )
    gkvb_ref[...] = gkv[...].astype(BF)

    def second(s):
        r = rows_at(s * patches, patches)
        g = (gq[r, :] * scale).astype(BF)
        gcb[r, :] = g
        bsum_ref[1:2, :] += jnp.sum(g.astype(F32), axis=0, keepdims=True)

    each(frames, second)
    weight_grad(1, residb_ref[...], gcb[...])
    loads[1].wait()
    gra_ref[...] = dot_nt(gcb[...], w_buf[...])
    loads[2].start()

    def third(s):
        r = rows_at(s * patches, patches)
        gra = gra_ref[r, :] + grc_ref[r, :]
        gra_ref[r, :] = gra
        gp_ref[...] += gra * ao_ref[r, :].astype(F32)
        g = (gate_ref[...] * gra).astype(BF)
        gmix[r, :] = g
        bsum_ref[2:3, :] += jnp.sum(g.astype(F32), axis=0, keepdims=True)

    each(frames, third)
    loads[2].wait()
    gai_ref[...] = dot_nt(gmix[...], w_buf[...]).astype(BF)
    outs[0].wait()
    weight_grad(2, attn_ref[...], gmix[...])
    outs[1].wait()
    outs[2].wait()


def cross_back_call(patches, heads, grc, mixb, q, keys, vals, lse, cm, residb, attn, ao, gate, wco, wq, wo):
    rows, width = grc.shape
    caps = keys.shape[0]
    S = jax.ShapeDtypeStruct
    return pl.pallas_call(
        partial(cross_back_kernel, patches, heads),
        out_shape=[
            S((rows, width), F32), S((rows, width), BF), S((2, caps, width), BF), S((8, width), F32), S((patches, width), F32),
        ]
        + [S((2, width, width // 2), BF)] * 3,
        in_specs=[IN_VMEM] * 11 + [IN_ANY] * 3,
        out_specs=[IN_VMEM] * 5 + [IN_ANY] * 3,
        scratch_shapes=[
            pltpu.VMEM((width, width), BF), pltpu.VMEM((rows, width), BF), pltpu.VMEM((rows, width), BF),
            pltpu.VMEM((rows, width), F32), pltpu.VMEM((2, caps, width), F32),
            pltpu.VMEM((rows, caps), BF), pltpu.VMEM((rows, caps), BF), pltpu.VMEM((3 * patches, caps), F32),
            pltpu.VMEM((2, 2, width, width // 2), BF),
            pltpu.SemaphoreType.DMA((3,)), pltpu.SemaphoreType.DMA((3,)),
        ],
        compiler_params=pltpu.CompilerParams(vmem_limit_bytes=VMEM_LIMIT),
        name="cross_back",
    )(grc, mixb, q, keys, vals, lse, cm, residb, attn, ao, gate, wco, wq, wo)


def attend_back_kernel(
    patches, heads, gai_ref, q_ref, kvx_ref, probs_ref, e_ref, et_ref, info_ref, nm_ref, x_ref, scale_ref, gra_ref, wqkv_ref,
    ig_ref, bsum_ref, gp_ref, dw_ref,
    w_buf, gqb, gkb, gvb, gkv, halo_out, halo_in, dw_s, sems, send, recv,
):
    pos = Place()
    rows, width = x_ref.shape
    frames = rows // patches
    half = width // 2
    count, y = info_ref[0], info_ref[1]
    load = pltpu.make_async_copy(wqkv_ref, w_buf, sems.at[0])
    load.start()
    pair_barrier(pos)
    gkv[...] = jnp.zeros(gkv.shape, F32)
    scale = (width // heads) ** (-0.5)
    each(
        frames // 3,
        lambda t: attend_tile_back(t, 3, patches, scale, q_ref, kvx_ref, e_ref, et_ref, probs_ref, gai_ref, gqb, gkv),
    )
    place = jnp.where(y == 0, count, -1) + 1
    pick_slot(frames + 2, patches, place, gkv, halo_out)
    copy = pltpu.make_async_remote_copy(
        src_ref=halo_out, dst_ref=halo_in, send_sem=send, recv_sem=recv,
        device_id=pos.dev(y=1 - pos.y), device_id_type=MESH,
    )
    copy.start()
    bsum_ref[...] = jnp.zeros(bsum_ref.shape, F32)
    gp_ref[...] = jnp.zeros(gp_ref.shape, F32)
    dw_s[:, :width] = dot_tn(nm_ref[...], gqb[...]).astype(BF)
    load.wait()
    ig_ref[...] = dot_nt(gqb[...], w_buf[:, :width])
    copy.wait()
    mine = jnp.where(y == 0, count - 1, 0) + 1

    def settle(s):
        r = rows_at((s + 1) * patches, patches)
        o = rows_at(s * patches, patches)
        shape = (patches, 2 * width)
        drop = jnp.full(shape, (s + 1 == place).astype(F32), F32)
        add = jnp.full(shape, (s + 1 == mine).astype(F32), F32)
        g = jnp.where(drop > 0.5, 0.0, gkv[r, :]) + jnp.where(add > 0.5, halo_in[...].astype(F32), 0.0)
        g = g.astype(BF)
        gkb[o, :] = g[:, :width]
        gvb[o, :] = g[:, width:]
        bsum_ref[0:1, :] += jnp.sum(gqb[o, :].astype(F32), axis=0, keepdims=True)
        bsum_ref[1:2, :] += jnp.sum(g[:, width:].astype(F32), axis=0, keepdims=True)

    each(frames, settle)
    late = pltpu.make_async_copy(gra_ref, gkv.at[pl.ds(0, rows), pl.ds(0, width)], sems.at[2])
    late.start()
    dw_s[:, width:] = dot_tn(nm_ref[...], gkb[:, :half]).astype(BF)
    out = [pltpu.make_async_copy(dw_s, dw_ref.at[f], sems.at[1]) for f in range(2)]
    out[0].start()
    ig_ref[...] += dot_nt(gkb[...], w_buf[:, width : 2 * width])
    ig_ref[...] += dot_nt(gvb[...], w_buf[:, 2 * width :])
    out[0].wait()
    dw_s[:, :half] = dot_tn(nm_ref[...], gkb[:, half:]).astype(BF)
    dw_s[:, half:] = dot_tn(nm_ref[...], gvb[...]).astype(BF)
    out[1].start()
    late.wait()

    def finish(s):
        r = rows_at(s * patches, patches)
        xhat, rstd = normalise(x_ref[r, :].astype(F32))
        g = ig_ref[r, :]
        gp_ref[0] += g
        gp_ref[1] += g * xhat
        ig_ref[r, :] = gkv[r, :width] + normalise_back(xhat, rstd, g, scale_ref[...])

    each(frames, finish)
    out[1].wait()


def attend_back_call(patches, heads, gai, q, kvx, probs, e, et, info, nm, x, scale, gra, wqkv, ident):
    cols = 3 * x.shape[1] // 2
    rows, width = x.shape
    S = jax.ShapeDtypeStruct
    return pl.pallas_call(
        partial(attend_back_kernel, patches, heads),
        out_shape=[S((rows, width), F32), S((8, width), F32), S((2, patches, width), F32), S((2, width, cols), BF)],
        in_specs=[IN_VMEM] * 6 + [IN_SMEM] + [IN_VMEM] * 3 + [IN_ANY] * 2,
        out_specs=[IN_VMEM] * 3 + [IN_ANY],
        scratch_shapes=[
            pltpu.VMEM(wqkv.shape, BF), pltpu.VMEM((rows, width), BF), pltpu.VMEM((rows, width), BF), pltpu.VMEM((rows, width), BF),
            pltpu.VMEM(kvx.shape, F32), pltpu.VMEM((patches, 2 * width), BF), pltpu.VMEM((patches, 2 * width), BF),
            pltpu.VMEM((width, cols), BF),
            pltpu.SemaphoreType.DMA((3,)), pltpu.SemaphoreType.DMA, pltpu.SemaphoreType.DMA,
        ],
        compiler_params=pltpu.CompilerParams(collective_id=ident, has_side_effects=True, vmem_limit_bytes=VMEM_LIMIT),
        name="attend_back",
    )(gai, q, kvx, probs, e, et, info, nm, x, scale, gra, wqkv)


UNITS_ALL = (
    (0, None, (0, 896), "x"),
    (0, None, (896, 832), "y"),
    (1, None, None, "x"),
    (2, None, None, "y"),
    (3, None, None, "x"),
    (4, None, None, "y"),
    (5, None, (0, 1152), "x"),
    (5, None, (1152, 1152), "y"),
    (6, (0, 144), None, "x"),
    (6, (144, 144), None, "y"),
)


def fast_body(
    tokens, cotangent, caption, null_embed, timesteps, null_mask, bucket_sizes, patch_mask, frame_counts, table, time_proj,
    self_qkv, self_out, cross_q, cross_kv, cross_out, mlp_in, mlp_out, biases, hidden_bias,
):
    frames, patches, width = tokens.shape
    heads = HEADS
    head_dim = width // heads
    clips, cap_len, _ = caption.shape
    cap_pad = -(-cap_len // 128) * 128
    rows = frames * patches
    count = frame_counts[0]
    frame_index = lax.axis_index("frames")
    patch_index = lax.axis_index("patches")
    bias_f = biases.astype(F32)
    patch_ids = patch_index * patches + jnp.arange(patches, dtype=jnp.int32)
    bucket_ends = jnp.cumsum(bucket_sizes)
    clip_ids = jnp.sum((patch_ids[:, None] >= bucket_ends[None, :]).astype(jnp.int32), axis=1)
    onehot = (clip_ids[:, None] == jnp.arange(clips, dtype=jnp.int32)[None, :]).astype(F32)
    valid = (jnp.arange(frames, dtype=jnp.int32) < count)[:, None] & (patch_mask[None, :] == 1)
    valid = valid.reshape(rows, 1).astype(F32)
    time_rows, time_cols = time_proj.shape
    features = time_features(timesteps, time_rows * lax.axis_size("patches")).astype(BF)
    own_features = lax.dynamic_slice_in_dim(features, patch_index * time_rows, time_rows, 1)
    time_part = lax.dynamic_update_slice(
        jnp.zeros((clips, 6 * width), F32), forward_dot(own_features, time_proj), (0, frame_index * time_cols)
    )
    time_sum = lax.psum(time_part, ("frames", "patches"))
    modulation = table.astype(F32) + time_sum.reshape(clips, 6, width)
    mods = jnp.einsum("pc,ckd->kpd", onehot, modulation, precision=HIGH)
    used = jnp.where(null_mask[:, None, None] == 1, null_embed[None], caption)
    used = jnp.pad(used, ((0, 0), (0, cap_pad - cap_len), (0, 0))).reshape(clips * cap_pad, width)
    key_ids = jnp.arange(clips * cap_pad, dtype=jnp.int32)
    open_key = (clip_ids[:, None] == (key_ids // cap_pad)[None, :]) & (key_ids % cap_pad < cap_len)[None, :]
    cmask = jnp.where(open_key, 0.0, NEG)
    lanes = jnp.arange(width, dtype=jnp.int32)[:, None] // head_dim
    e = (lanes == jnp.arange(128, dtype=jnp.int32)[None, :]).astype(BF)
    et = jnp.concatenate([e.T, e.T], axis=0)
    info = jnp.stack([count, frame_index]).astype(jnp.int32)
    qkv_bias = jnp.concatenate([bias_f[0], jnp.zeros((width,), F32), bias_f[1]])[None]

    got = gather_call([self_qkv, self_out, cross_q, cross_out, cross_kv, mlp_in, mlp_out], UNITS_ALL, 0)
    w_qkv, w_out, w_q, w_co, w_kv, w_in, w_mo = [g.reshape(2, -1, g.shape[-1]) for g in got]
    x = tokens.reshape(rows, width)
    cot = cotangent.reshape(rows, width)
    nm_a = norm_call(patches, x, mods)
    wqkv, wo, q, kvx, probs, attn, ao, resid, residb = attend_call(
        patches, heads, nm_a, x, mods, w_qkv, w_out, qkv_bias, bias_f[2:3], e, et, info, 3
    )
    wq, wco, cq, keys, vals, lse, mixb, rc, nm_m = cross_call(
        patches, heads, resid, residb, mods, used, cmask, w_q, w_co, w_kv, bias_f[3:4], bias_f[4:5], bias_f[5:6]
    )
    block_out, grc, hsum, bsum_m, gp_m, dw_in, dw_mo = mlp_call(
        patches, nm_m, cot, valid, rc, mods, hidden_bias.astype(F32), bias_f[6:7], w_in, w_mo
    )
    gra, gai, gkv, bsum_c, gp_g, dwo, dwq, dwco = cross_back_call(
        patches, heads, grc, mixb, cq, keys, vals, lse, cmask, residb, attn, ao, mods[2], wco, wq, wo
    )
    input_grad, bsum_a, gp_a, dwqkv = attend_back_call(
        patches, heads, gai, q, kvx, probs, e, et, info, nm_a, x, mods[1], gra, wqkv, 4
    )
    per_patch = jnp.stack([gp_a[0], gp_a[1], gp_g, gp_m[0], gp_m[1], gp_m[2]], axis=1)
    mod_part = jnp.einsum("pc,pkd->ckd", onehot, per_patch, precision=HIGH)
    bias_part = jnp.stack(
        [bsum_a[0], bsum_a[1], bsum_c[2], bsum_c[1], jnp.zeros((width,), F32), bsum_c[0], bsum_m[0]]
    )
    kv_total, bias_total, hidden_total, mod_total = lax.psum(
        (gkv.astype(F32), bias_part, hsum.reshape(-1), mod_part), ("frames", "patches")
    )
    kv_low = kv_total.astype(BF)
    bias_cv = jnp.sum(kv_low[1].astype(F32), axis=0)
    biases_grad = bias_total.at[4].add(bias_cv)
    own_used = lax.dynamic_slice_in_dim(used, patch_index * cross_kv.shape[0], cross_kv.shape[0], 1)
    cross_kv_grad = outer_sum(own_used, kv_low[frame_index])
    caption_rows = times_transposed(kv_low[0], w_kv[0]) + times_transposed(kv_low[1], w_kv[1])
    caption_rows = caption_rows.reshape(clips, cap_pad, width)[:, :cap_len]
    dropped = (null_mask == 1)[:, None, None]
    caption_grad = jnp.where(dropped, 0.0, caption_rows)
    null_grad = jnp.sum(jnp.where(dropped, caption_rows, 0.0), axis=0)
    table_grad = jnp.sum(mod_total, axis=0)
    own_mod = lax.dynamic_slice_in_dim(mod_total.reshape(clips, 6 * width), frame_index * time_cols, time_cols, 1)
    time_proj_grad = jnp.dot(own_features.astype(F32).T, own_mod, precision=HIGH)

    def blocks(part, shard):
        return part.reshape((2, 4, 2, 2) + shard.shape)

    in_shard, mo_shard = scatter_call(
        [blocks(dw_in, mlp_in), blocks(dw_mo, mlp_out)],
        (
            (0, None, (0, 1152), "x"),
            (0, None, (1152, 1152), "y"),
            (1, (0, 144), None, "x"),
            (1, (144, 144), None, "y"),
        ),
        1,
    )
    out_shard, q_shard, co_shard, qkv_shard = scatter_call(
        [blocks(dwo, self_out), blocks(dwq, cross_q), blocks(dwco, cross_out), blocks(dwqkv, self_qkv)],
        (
            (0, None, None, "x"),
            (1, None, None, "y"),
            (2, None, None, "x"),
            (3, None, (0, 896), "y"),
            (3, None, (896, 832), "x"),
        ),
        2,
    )
    return (
        block_out.reshape(tokens.shape),
        input_grad.reshape(tokens.shape),
        caption_grad,
        null_grad,
        table_grad,
        time_proj_grad,
        qkv_shard,
        out_shard,
        q_shard,
        cross_kv_grad,
        co_shard,
        in_shard,
        mo_shard,
        biases_grad,
        hidden_total,
    )


def body(*args):
    if lax.axis_size("frames") == 2 and lax.axis_size("patches") == 16:
        return fast_body(*args)
    return plain_body(*args)


def solution(mesh):
    return jax.shard_map(
        body,
        mesh=mesh,
        in_specs=(
            P("frames", "patches", None),
            P("frames", "patches", None),
            P(),
            P(),
            P(),
            P(),
            P(),
            P("patches"),
            P("frames"),
            P(),
            P("patches", "frames"),
            P("patches", "frames"),
            P("patches", "frames"),
            P("patches", "frames"),
            P("patches", "frames"),
            P("patches", "frames"),
            P("patches", "frames"),
            P("patches", "frames"),
            P(),
            P(),
        ),
        out_specs=(
            P("frames", "patches", None),
            P("frames", "patches", None),
            P(),
            P(),
            P(),
            P("patches", "frames"),
            P("patches", "frames"),
            P("patches", "frames"),
            P("patches", "frames"),
            P("patches", "frames"),
            P("patches", "frames"),
            P("patches", "frames"),
            P("patches", "frames"),
            P(),
            P(),
        ),
        check_vma=False,
    )
```

```python
from functools import partial
import math

import jax
import jax.numpy as jnp
from jax import lax
from jax.experimental import pallas as pl
from jax.experimental.pallas import tpu as pltpu
from jax.sharding import PartitionSpec as P

HEADS = 16
MESH = pl.DeviceIdType.MESH


HIGH = lax.Precision.HIGHEST


def with_halo(shard, sides, width):
    for axis, dim in sides:
        count, length = (lax.axis_size(axis), shard.shape[dim])
        up = [(i, (i + 1) % count) for i in range(count - 1)]
        down = [(j, i) for i, j in up]
        last = lax.slice_in_dim(shard, length - width, length, axis=dim)
        initial = lax.slice_in_dim(shard, 0, width, axis=dim)
        before = lax.ppermute(last, axis, up)
        after = lax.ppermute(initial, axis, down)
        shard = jnp.concatenate([before, shard, after], axis=dim)
    return shard


def layer_norm(values):
    mean = jnp.mean(values, axis=-1, keepdims=True)
    centered = values - mean
    variance = jnp.mean(centered * centered, axis=-1, keepdims=True)
    return centered * lax.rsqrt(variance + 1e-06)


def modulate(values, shift, scale):
    return layer_norm(values) * (1.0 + scale) + shift


def time_features(timesteps, width):
    half = width // 2
    freqs = jnp.exp(-math.log(10000.0) * jnp.arange(half, dtype=jnp.float32) / half)
    angles = timesteps.astype(jnp.float32)[:, None] * freqs[None, :]
    return jnp.concatenate([jnp.cos(angles), jnp.sin(angles)], axis=1)


def gelu_tanh(values):
    return jax.nn.gelu(values, approximate=True)


def forward_dot(left, right):
    return jnp.dot(left, right, preferred_element_type=jnp.float32)


def outer_sum(left, right):
    return jnp.einsum("rd,re->de", left, right, preferred_element_type=jnp.float32)


def times_transposed(grad, weight):
    return jnp.einsum("re,de->rd", grad, weight, preferred_element_type=jnp.float32)


def round_trip(values):
    return lax.optimization_barrier(values.astype(jnp.bfloat16)).astype(jnp.float32)


def gather_forward(shards):
    row_parts = (
        lax.all_gather(shards[0], "patches", axis=0, tiled=True),
        lax.all_gather(shards[1], "patches", axis=0, tiled=True),
        lax.all_gather(shards[2], "patches", axis=0, tiled=True),
        lax.all_gather(shards[3], "patches", axis=0, tiled=True),
        lax.all_gather(shards[4], "patches", axis=0, tiled=True),
        lax.all_gather(shards[5], "patches", axis=0, tiled=True),
        lax.all_gather(shards[6], "patches", axis=0, tiled=True),
        lax.all_gather(shards[7], "patches", axis=0, tiled=True),
    )
    return (
        lax.all_gather(row_parts[0], "frames", axis=1, tiled=True),
        lax.all_gather(row_parts[1], "frames", axis=1, tiled=True),
        lax.all_gather(row_parts[2], "frames", axis=1, tiled=True),
        lax.all_gather(row_parts[3], "frames", axis=1, tiled=True),
        lax.all_gather(row_parts[4], "frames", axis=1, tiled=True),
        lax.all_gather(row_parts[5], "frames", axis=1, tiled=True),
        lax.all_gather(row_parts[6], "frames", axis=1, tiled=True),
        lax.all_gather(row_parts[7], "frames", axis=1, tiled=True),
    )


def self_attend(queries, keys_vals, key_mask, heads):
    frames, patches, width = queries.shape
    head_dim = width // heads
    query_heads = queries.reshape(frames, patches, heads, head_dim)
    key_heads = keys_vals[..., :width].reshape(frames + 2, patches, heads, head_dim)
    value_heads = keys_vals[..., width:].reshape(frames + 2, patches, heads, head_dim)
    scores = jnp.einsum("sphd,tphd->phst", query_heads, key_heads, precision=HIGH) * head_dim ** (
        -0.5
    )
    scores = jnp.where(key_mask[None, None], scores, -1000000000.0)
    probs = jax.nn.softmax(scores, axis=-1)
    mixed = jnp.einsum("phst,tphd->sphd", probs, value_heads, precision=HIGH)
    return mixed.reshape(frames, patches, width)


def plain_body(
    tokens,
    cotangent,
    caption,
    null_embed,
    timesteps,
    null_mask,
    bucket_sizes,
    patch_mask,
    frame_counts,
    table,
    time_proj,
    self_qkv,
    self_out,
    cross_q,
    cross_kv,
    cross_out,
    mlp_in,
    mlp_out,
    biases,
    hidden_bias,
):
    f32 = jnp.float32
    bf16 = jnp.bfloat16
    frames, patches, width = tokens.shape
    heads = HEADS
    head_dim = width // heads
    scale = head_dim ** (-0.5)
    clips = caption.shape[0]
    cap_len = caption.shape[1]
    row_count = frames * patches
    count = frame_counts[0]
    frame_index = lax.axis_index("frames")
    patch_index = lax.axis_index("patches")
    shards = (time_proj, self_qkv, self_out, cross_q, cross_kv, cross_out, mlp_in, mlp_out)
    weights = gather_forward(shards)
    full_time, full_qkv, full_out, full_q, full_kv, full_cross_out, full_in, full_mlp_out = weights
    bias_f = biases.astype(f32)
    bias_hidden = hidden_bias.astype(f32)
    patch_ids = patch_index * patches + jnp.arange(patches, dtype=jnp.int32)
    bucket_ends = jnp.cumsum(bucket_sizes)
    clip_ids = jnp.sum((patch_ids[:, None] >= bucket_ends[None, :]).astype(jnp.int32), axis=1)
    onehot = (clip_ids[:, None] == jnp.arange(clips, dtype=jnp.int32)[None, :]).astype(f32)
    slot_ids = jnp.arange(frames, dtype=jnp.int32)
    valid = (slot_ids < count)[:, None] & (patch_mask[None, :] == 1)
    features = time_features(timesteps, full_time.shape[0]).astype(bf16)
    modulation = table.astype(f32) + forward_dot(features, full_time).reshape(clips, 6, width)
    per_patch = jnp.einsum("pc,ckd->pkd", onehot, modulation, precision=HIGH)
    shift_a = per_patch[:, 0]
    scale_a = per_patch[:, 1]
    gate_a = per_patch[:, 2]
    shift_m = per_patch[:, 3]
    scale_m = per_patch[:, 4]
    gate_m = per_patch[:, 5]
    inputs_f = tokens.astype(f32)
    normed_a, modulate_a_vjp = jax.vjp(modulate, inputs_f, shift_a, scale_a)
    normed_r = normed_a.astype(bf16).reshape(row_count, width)
    qkv_bias = jnp.concatenate([bias_f[0], jnp.zeros((width,), f32), bias_f[1]])
    qkv_r = (
        (forward_dot(normed_r, full_qkv) + qkv_bias)
        .astype(bf16)
        .reshape(frames, patches, 3 * width)
    )
    queries_r = qkv_r[..., :width]
    keyval_r = qkv_r[..., width:]
    last_kv = lax.dynamic_index_in_dim(keyval_r, count - 1, 0, keepdims=False)
    edges = jnp.stack([keyval_r[0], last_kv])
    outer_kv = with_halo(edges, (("frames", 0),), 1)
    keys_all = jnp.concatenate([outer_kv[0:1], keyval_r, outer_kv[3:4]], axis=0)
    prev_ok = frame_index > 0
    next_ok = frame_index < lax.axis_size("frames") - 1
    query_slot = slot_ids[:, None]
    key_place = jnp.arange(frames + 2, dtype=jnp.int32)[None, :]
    key_slot = key_place - 1
    slot_keys = (
        (key_place >= 1)
        & (key_place <= frames)
        & (jnp.abs(key_slot - query_slot) <= 1)
        & (key_slot < count)
    )
    prev_keys = (key_place == 0) & (query_slot == 0) & prev_ok
    next_keys = (key_place == frames + 1) & (query_slot == count - 1) & next_ok
    key_mask = slot_keys | prev_keys | next_keys
    attn_in, attend_vjp = jax.vjp(
        partial(self_attend, key_mask=key_mask, heads=heads),
        queries_r.astype(f32),
        keys_all.astype(f32),
    )
    attn_r = attn_in.astype(bf16).reshape(row_count, width)
    attn_out = (forward_dot(attn_r, full_out) + bias_f[2]).reshape(frames, patches, width)
    resid_a = inputs_f + gate_a * attn_out
    captions_used = jnp.where(null_mask[:, None, None] == 1, null_embed[None], caption).reshape(
        clips * cap_len, width
    )
    kv_bias = jnp.concatenate([jnp.zeros((width,), f32), bias_f[4]])
    cross_kv_r = (forward_dot(captions_used, full_kv) + kv_bias).astype(bf16)
    cross_keys = cross_kv_r[:, :width].reshape(clips * cap_len, heads, head_dim)
    cross_vals = cross_kv_r[:, width:].reshape(clips * cap_len, heads, head_dim)
    resid_a_r = resid_a.astype(bf16).reshape(row_count, width)
    cross_queries = (
        (forward_dot(resid_a_r, full_q) + bias_f[3])
        .astype(bf16)
        .reshape(row_count, heads, head_dim)
    )
    token_clip = jnp.broadcast_to(clip_ids[None, :], (frames, patches)).reshape(row_count)
    key_clip = jnp.repeat(jnp.arange(clips, dtype=jnp.int32), cap_len)
    same_clip = token_clip[:, None] == key_clip[None, :]
    scores = (
        jnp.einsum("rhd,khd->rhk", cross_queries, cross_keys, preferred_element_type=f32) * scale
    )
    scores = jnp.where(same_clip[:, None, :], scores, -1000000000.0)
    probs = jax.nn.softmax(scores, axis=-1)
    probs_r = probs.astype(bf16)
    cross_mix = (
        jnp.einsum("rhk,khd->rhd", probs_r, cross_vals, preferred_element_type=f32)
        .astype(bf16)
        .reshape(row_count, width)
    )
    cross_res = forward_dot(cross_mix, full_cross_out) + bias_f[5]
    resid_c = resid_a + cross_res.reshape(frames, patches, width)
    normed_m, modulate_m_vjp = jax.vjp(modulate, resid_c, shift_m, scale_m)
    normed_m_r = normed_m.astype(bf16).reshape(row_count, width)
    pre_act = forward_dot(normed_m_r, full_in) + bias_hidden
    activ, gelu_vjp = jax.vjp(gelu_tanh, pre_act)
    activ_r = activ.astype(bf16)
    mlp_res = (forward_dot(activ_r, full_mlp_out) + bias_f[6]).reshape(frames, patches, width)
    final = resid_c + gate_m * mlp_res
    block_out = jnp.where(valid[:, :, None], final, 0.0).astype(bf16)
    grad_final = jnp.where(valid[:, :, None], cotangent.astype(f32), 0.0)
    grad_gate_m = jnp.sum(grad_final * mlp_res, axis=0)
    grad_mlp_r = (gate_m * grad_final).astype(bf16).reshape(row_count, width)
    bias_mo_grad = jnp.sum(grad_mlp_r.astype(f32), axis=0)
    mlp_out_grad = outer_sum(activ_r, grad_mlp_r)
    grad_act = times_transposed(grad_mlp_r, full_mlp_out)
    grad_pre_r = gelu_vjp(grad_act)[0].astype(bf16)
    bias_hidden_grad = jnp.sum(grad_pre_r.astype(f32), axis=0)
    mlp_in_grad = outer_sum(normed_m_r, grad_pre_r)
    grad_norm_m = times_transposed(grad_pre_r, full_in).reshape(frames, patches, width)
    resid_c_part, grad_shift_m, grad_scale_m = modulate_m_vjp(grad_norm_m)
    grad_resid_c = grad_final + resid_c_part
    grad_cross_r = grad_resid_c.astype(bf16).reshape(row_count, width)
    bias_co_grad = jnp.sum(grad_cross_r.astype(f32), axis=0)
    cross_out_grad = outer_sum(cross_mix, grad_cross_r)
    grad_mix_r = (
        times_transposed(grad_cross_r, full_cross_out)
        .astype(bf16)
        .reshape(row_count, heads, head_dim)
    )
    grad_probs = jnp.einsum("rhd,khd->rhk", grad_mix_r, cross_vals, preferred_element_type=f32)
    grad_vals = jnp.einsum("rhk,rhd->khd", probs_r, grad_mix_r, preferred_element_type=f32)
    grad_scores_r = (
        probs * (grad_probs - jnp.sum(grad_probs * probs, axis=-1, keepdims=True))
    ).astype(bf16)
    grad_cq = (
        jnp.einsum("rhk,khd->rhd", grad_scores_r, cross_keys, preferred_element_type=f32) * scale
    )
    grad_cq_r = grad_cq.astype(bf16).reshape(row_count, width)
    grad_keys = (
        jnp.einsum("rhk,rhd->khd", grad_scores_r, cross_queries, preferred_element_type=f32) * scale
    )
    bias_cq_grad = jnp.sum(grad_cq_r.astype(f32), axis=0)
    cross_q_grad = outer_sum(resid_a_r, grad_cq_r)
    grad_resid_a = grad_resid_c + times_transposed(grad_cq_r, full_q).reshape(
        frames, patches, width
    )
    cross_kv_part = jnp.concatenate(
        [grad_keys.reshape(clips * cap_len, width), grad_vals.reshape(clips * cap_len, width)],
        axis=1,
    )
    grad_gate_a = jnp.sum(grad_resid_a * attn_out, axis=0)
    grad_attn_r = (gate_a * grad_resid_a).astype(bf16).reshape(row_count, width)
    bias_o_grad = jnp.sum(grad_attn_r.astype(f32), axis=0)
    self_out_grad = outer_sum(attn_r, grad_attn_r)
    grad_attn_in = round_trip(times_transposed(grad_attn_r, full_out)).reshape(
        frames, patches, width
    )
    grad_queries, grad_keys_all = attend_vjp(grad_attn_in)
    returns = jnp.stack([grad_keys_all[0], grad_keys_all[frames + 1]])
    back_kv = with_halo(returns.astype(jnp.bfloat16), (("frames", 0),), 1).astype(returns.dtype)
    first_slot = (slot_ids == 0)[:, None, None]
    last_slot = (slot_ids == count - 1)[:, None, None]
    grad_kv = (
        grad_keys_all[1 : frames + 1]
        + jnp.where(first_slot, back_kv[0][None], 0.0)
        + jnp.where(last_slot, back_kv[3][None], 0.0)
    )
    grad_qkv_r = (
        jnp.concatenate([grad_queries, grad_kv], axis=-1).astype(bf16).reshape(row_count, 3 * width)
    )
    bias_q_grad = jnp.sum(grad_qkv_r[:, :width].astype(f32), axis=0)
    bias_v_grad = jnp.sum(grad_qkv_r[:, 2 * width :].astype(f32), axis=0)
    self_qkv_grad = outer_sum(normed_r, grad_qkv_r)
    grad_norm_a = times_transposed(grad_qkv_r, full_qkv).reshape(frames, patches, width)
    input_part, grad_shift_a, grad_scale_a = modulate_a_vjp(grad_norm_a)
    input_grad = grad_resid_a + input_part
    per_patch_grad = jnp.stack(
        [grad_shift_a, grad_scale_a, grad_gate_a, grad_shift_m, grad_scale_m, grad_gate_m], axis=1
    )
    mod_part = jnp.einsum("pc,pkd->ckd", onehot, per_patch_grad, precision=HIGH)
    bias_part = jnp.stack(
        [
            bias_q_grad,
            bias_v_grad,
            bias_o_grad,
            bias_cq_grad,
            jnp.zeros((width,), f32),
            bias_co_grad,
            bias_mo_grad,
        ]
    )
    kv_total, bias_total, hidden_total, mod_total = lax.psum(
        (cross_kv_part, bias_part, bias_hidden_grad, mod_part), ("frames", "patches")
    )
    kv_total_r = kv_total.astype(bf16)
    bias_cv_grad = jnp.sum(kv_total_r[:, width:].astype(f32), axis=0)
    bias_rows_ids = jnp.arange(bias_total.shape[0], dtype=jnp.int32)
    biases_grad = bias_total + jnp.where((bias_rows_ids == 4)[:, None], bias_cv_grad[None, :], 0.0)
    cross_kv_full = outer_sum(captions_used, kv_total_r)
    caption_rows = times_transposed(kv_total_r, full_kv).reshape(clips, cap_len, width)
    dropped = (null_mask == 1)[:, None, None]
    caption_grad = jnp.where(dropped, 0.0, caption_rows)
    null_grad = jnp.sum(jnp.where(dropped, caption_rows, 0.0), axis=0)
    table_grad = jnp.sum(mod_total, axis=0)
    time_full = jnp.dot(features.astype(f32).T, mod_total.reshape(clips, 6 * width), precision=HIGH)
    time_proj_grad = lax.dynamic_slice(
        time_full,
        (patch_index * time_proj.shape[0], frame_index * time_proj.shape[1]),
        time_proj.shape,
    )
    cross_kv_grad = lax.dynamic_slice(
        cross_kv_full,
        (patch_index * cross_kv.shape[0], frame_index * cross_kv.shape[1]),
        cross_kv.shape,
    )
    grads = (self_qkv_grad, self_out_grad, cross_q_grad, cross_out_grad, mlp_in_grad, mlp_out_grad)
    row_sums = (
        lax.psum_scatter(
            grads[0].astype(jnp.bfloat16), "patches", scatter_dimension=0, tiled=True
        ).astype(jnp.float32),
        lax.psum_scatter(
            grads[1].astype(jnp.bfloat16), "patches", scatter_dimension=0, tiled=True
        ).astype(jnp.float32),
        lax.psum_scatter(
            grads[2].astype(jnp.bfloat16), "patches", scatter_dimension=0, tiled=True
        ).astype(jnp.float32),
        lax.psum_scatter(
            grads[3].astype(jnp.bfloat16), "patches", scatter_dimension=0, tiled=True
        ).astype(jnp.float32),
        lax.psum_scatter(
            grads[4].astype(jnp.bfloat16), "patches", scatter_dimension=0, tiled=True
        ).astype(jnp.float32),
        lax.psum_scatter(
            grads[5].astype(jnp.bfloat16), "patches", scatter_dimension=0, tiled=True
        ).astype(jnp.float32),
    )
    col_sums = (
        lax.psum_scatter(
            row_sums[0].astype(jnp.bfloat16), "frames", scatter_dimension=1, tiled=True
        ).astype(jnp.float32),
        lax.psum_scatter(
            row_sums[1].astype(jnp.bfloat16), "frames", scatter_dimension=1, tiled=True
        ).astype(jnp.float32),
        lax.psum_scatter(
            row_sums[2].astype(jnp.bfloat16), "frames", scatter_dimension=1, tiled=True
        ).astype(jnp.float32),
        lax.psum_scatter(
            row_sums[3].astype(jnp.bfloat16), "frames", scatter_dimension=1, tiled=True
        ).astype(jnp.float32),
        lax.psum_scatter(
            row_sums[4].astype(jnp.bfloat16), "frames", scatter_dimension=1, tiled=True
        ).astype(jnp.float32),
        lax.psum_scatter(
            row_sums[5].astype(jnp.bfloat16), "frames", scatter_dimension=1, tiled=True
        ).astype(jnp.float32),
    )
    qkv_shard, out_shard, q_shard, cross_out_shard, in_shard, mlp_out_shard = col_sums
    return (
        block_out,
        input_grad,
        caption_grad,
        null_grad,
        table_grad,
        time_proj_grad,
        qkv_shard,
        out_shard,
        q_shard,
        cross_kv_grad,
        cross_out_shard,
        in_shard,
        mlp_out_shard,
        biases_grad,
        hidden_total,
    )


BF = jnp.bfloat16
F32 = jnp.float32
VMEM_LIMIT = 60 * 2**20
NEG = -1e30
IN_VMEM = pl.BlockSpec(memory_space=pltpu.VMEM)
IN_ANY = pl.BlockSpec(memory_space=pl.ANY)
IN_SMEM = pl.BlockSpec(memory_space=pltpu.SMEM)
GELU_C = math.sqrt(2.0 / math.pi)


def dot(a, b):
    return jnp.dot(a, b, preferred_element_type=F32)


def dot_nt(a, b):
    return lax.dot_general(a, b, (((1,), (1,)), ((), ())), preferred_element_type=F32)


def dot_tn(a, b):
    return lax.dot_general(a, b, (((0,), (0,)), ((), ())), preferred_element_type=F32)


def gelu_parts(v):
    square = v * v
    inner = GELU_C * (v + 0.044715 * (v * square))
    t = jnp.tanh(inner)
    half = 0.5 * (1.0 + t)
    act = v * half
    slope = half + (0.5 * GELU_C) * v * (1.0 - t * t) * (1.0 + (3 * 0.044715) * square)
    return act, slope


def normalise(v):
    mean = jnp.mean(v, axis=-1, keepdims=True)
    cen = v - mean
    var = jnp.mean(cen * cen, axis=-1, keepdims=True)
    rstd = lax.rsqrt(var + 1e-06)
    return cen * rstd, rstd


def normalise_back(xhat, rstd, g, scale):
    h = g * (1.0 + scale)
    a = jnp.mean(h, axis=-1, keepdims=True)
    b = jnp.mean(h * xhat, axis=-1, keepdims=True)
    return rstd * (h - a - xhat * b)


def rows_at(start, size):
    return pl.ds(pl.multiple_of(start, 16), size)


def each(count, fn):
    def step(i, carry):
        fn(i)
        return carry

    lax.fori_loop(0, count, step, 0)


def norm_body(x_ref, mods_ref, out_ref, patches):
    def frame(s):
        r = rows_at(s * patches, patches)
        xhat, _ = normalise(x_ref[r, :].astype(F32))
        out_ref[r, :] = (xhat * (1.0 + mods_ref[1]) + mods_ref[0]).astype(BF)

    each(x_ref.shape[0] // patches, frame)


def key_ok(t, per, patches, j, count, y):
    rows = per * patches
    row = lax.broadcasted_iota(jnp.int32, (rows, 128), 0)
    slot = jnp.zeros((rows, 128), jnp.int32)
    for i in range(1, per):
        slot = slot + (row >= i * patches).astype(jnp.int32)
    key = slot + (t * per + j - 1)
    low = (key >= 0) | (y > 0)
    high = (key < count) | ((key == count) & (y < 1))
    return low & high


def spread(p, et_ref):
    hi = p.astype(BF)
    lo = (p - hi.astype(F32)).astype(BF)
    return dot(jnp.concatenate([hi, lo], axis=1), et_ref[...])


def attend_tile(t, per, patches, count, y, scale, q_ref, kvx_ref, e_ref, et_ref, probs_ref, attn_ref):
    rows = per * patches
    width = q_ref.shape[1]
    r = rows_at(t * rows, rows)
    q = q_ref[r, :].astype(F32)
    scores = []
    for j in range(3):
        kr = rows_at(t * rows + j * patches, rows)
        s = dot((q * kvx_ref[kr, :width].astype(F32)).astype(BF), e_ref[...]) * scale
        scores.append(jnp.where(key_ok(t, per, patches, j, count, y), s, NEG))
    top = jnp.maximum(jnp.maximum(scores[0], scores[1]), scores[2])
    ex = [jnp.exp(s - top) for s in scores]
    inv = 1.0 / (ex[0] + ex[1] + ex[2])
    total = None
    for j in range(3):
        p = ex[j] * inv
        probs_ref[j, r, :] = p
        kr = rows_at(t * rows + j * patches, rows)
        term = spread(p, et_ref) * kvx_ref[kr, width:].astype(F32)
        total = term if total is None else total + term
    attn_ref[r, :] = total.astype(BF)


def attend_tile_back(t, per, patches, scale, q_ref, kvx_ref, e_ref, et_ref, probs_ref, go_ref, gq_ref, gkv_ref):
    rows = per * patches
    width = q_ref.shape[1]
    r = rows_at(t * rows, rows)
    q = q_ref[r, :].astype(F32)
    go = go_ref[r, :].astype(F32)
    dps, ps = [], []
    for j in range(3):
        kr = rows_at(t * rows + j * patches, rows)
        dps.append(dot((go * kvx_ref[kr, width:].astype(F32)).astype(BF), e_ref[...]))
        ps.append(probs_ref[j, r, :])
    mean = dps[0] * ps[0] + dps[1] * ps[1] + dps[2] * ps[2]
    gq = None
    for j in range(3):
        kr = rows_at(t * rows + j * patches, rows)
        ds = spread(ps[j] * (dps[j] - mean) * scale, et_ref)
        term = ds * kvx_ref[kr, :width].astype(F32)
        gq = term if gq is None else gq + term
        gkv_ref[kr, :width] += ds * q
        gkv_ref[kr, width:] += spread(ps[j], et_ref) * go
    gq_ref[r, :] = gq.astype(BF)


def head_window(h, head_dim, width):
    return min(h * head_dim // 128 * 128, width - 256)


def head_lanes(h, head_dim, width):
    lane = lax.broadcasted_iota(jnp.int32, (1, 256), 1) + head_window(h, head_dim, width)
    return (lane >= h * head_dim) & (lane < (h + 1) * head_dim)


def cross_head(h, heads, tiles, q_ref, keys_ref, vals_ref, cmask_ref, lse_ref, mix_ref):
    width = q_ref.shape[1]
    head_dim = width // heads
    scale = head_dim ** (-0.5)
    w = head_window(h, head_dim, width)
    keep = head_lanes(h, head_dim, width)
    kw = jnp.where(keep, keys_ref[:, w : w + 256], 0)
    vw = jnp.where(keep, vals_ref[:, w : w + 256], 0)
    rows = q_ref.shape[0] // tiles
    for i in range(tiles):
        r = slice(i * rows, (i + 1) * rows)
        s = dot_nt(q_ref[r, w : w + 256], kw) * scale + cmask_ref[...]
        top = jnp.max(s, axis=-1, keepdims=True)
        ex = jnp.exp(s - top)
        total = jnp.sum(ex, axis=-1, keepdims=True)
        p = (ex * (1.0 / total)).astype(BF)
        lse_ref[r, h : h + 1] = top + jnp.log(total)
        mix_ref[r, w : w + 256] += dot(p, vw)


def cross_head_back(h, heads, tiles, q_ref, keys_ref, vals_ref, cmask_ref, lse_ref, gmix_ref, gq_ref, gkv_ref, p_buf, ds_buf):
    width = q_ref.shape[1]
    head_dim = width // heads
    scale = head_dim ** (-0.5)
    w = head_window(h, head_dim, width)
    keep = head_lanes(h, head_dim, width)
    kw = jnp.where(keep, keys_ref[:, w : w + 256], 0)
    vw = jnp.where(keep, vals_ref[:, w : w + 256], 0)
    rows = q_ref.shape[0] // tiles
    for i in range(tiles):
        r = slice(i * rows, (i + 1) * rows)
        s = dot_nt(q_ref[r, w : w + 256], kw) * scale + cmask_ref[...]
        p = jnp.exp(s - lse_ref[r, h : h + 1])
        dp = dot_nt(gmix_ref[r, w : w + 256], vw)
        ds = (p * (dp - jnp.sum(dp * p, axis=-1, keepdims=True))).astype(BF)
        p_buf[r, :] = p.astype(BF)
        ds_buf[r, :] = ds
        gq_ref[r, w : w + 256] += dot(ds, kw)
    gk = dot_tn(ds_buf[...], q_ref[:, w : w + 256]) * scale
    gv = dot_tn(p_buf[...], gmix_ref[:, w : w + 256])
    gkv_ref[0, :, w : w + 256] += jnp.where(keep, gk, 0.0)
    gkv_ref[1, :, w : w + 256] += jnp.where(keep, gv, 0.0)


class Place:
    def __init__(self):
        self.y = lax.axis_index("frames")
        p = lax.axis_index("patches")
        self.z = p // 4
        self.x = lax.rem(p // 2, 2)
        self.c = lax.rem(p, 2)

    def dev(self, y=None, z=None, x=None, c=None):
        y = self.y if y is None else y
        z = self.z if z is None else z
        x = self.x if x is None else x
        c = self.c if c is None else c
        return (y, (z * 2 + x) * 2 + c)

    def zoff(self, d):
        return lax.rem(self.z + d, 4)


def barrier(pos):
    bar = pltpu.get_barrier_semaphore()
    peers = [pos.dev(z=pos.zoff(d)) for d in (1, 2, 3)]
    peers += [pos.dev(x=1 - pos.x), pos.dev(y=1 - pos.y), pos.dev(c=1 - pos.c)]
    for t in peers:
        pl.semaphore_signal(bar, inc=1, device_id=t, device_id_type=MESH)
    pl.semaphore_wait(bar, 6)


def remote(src, dst, send, recv, i, dev):
    return pltpu.make_async_remote_copy(
        src_ref=src, dst_ref=dst, send_sem=send.at[i], recv_sem=recv.at[i], device_id=dev, device_id_type=MESH
    )


def part_of(ref, rows, cols, lead):
    index = [slice(None)] * lead
    index.append(pl.ds(*rows) if rows else slice(None))
    index.append(pl.ds(*cols) if cols else slice(None))
    return ref.at[tuple(index)]


class Ticker:
    def __init__(self, process):
        self.process = process

    def __call__(self, steps=1):
        for _ in range(steps):
            next(self.process, None)

    def drain(self):
        for _ in self.process:
            pass


N_AG = 11


class Gather:
    def __init__(self, pos, shard, full, send, recv, order):
        y, z, x, c = pos.y, pos.z, pos.x, pos.c
        self.order = order
        mine = full.at[y, z, x, c]
        self.local = pltpu.make_async_copy(shard, mine, send.at[8])
        rc = lambda i, ref, dev, src=None: remote(ref if src is None else src, ref, send, recv, i, dev)
        xd, yd, cd = pos.dev(x=1 - x), pos.dev(y=1 - y), pos.dev(c=1 - c)
        zd = [pos.dev(z=pos.zoff(d)) for d in (1, 2, 3)]
        if order == "zxy":
            line, plane, got1, got2 = full.at[y, :, x, c], full.at[y, :, :, c], full.at[y, :, 1 - x, c], full.at[1 - y, :, :, c]
            self.stages = [[rc(d, mine, zd[d], shard) for d in range(3)], [rc(3, line, xd)], [rc(4, plane, yd)]]
        elif order == "zyx":
            line, plane, got1, got2 = full.at[y, :, x, c], full.at[:, :, x, c], full.at[1 - y, :, x, c], full.at[:, :, 1 - x, c]
            self.stages = [[rc(d, mine, zd[d], shard) for d in range(3)], [rc(3, line, yd)], [rc(4, plane, xd)]]
        else:
            line, plane = full.at[y, z, :, c], full.at[:, z, :, c]
            self.stages = [[rc(3, mine, xd, shard)], [rc(4, line, yd)], [rc(d, plane, zd[d]) for d in range(3)]]
            got1, got2 = full.at[1 - y, z, :, c], None
        self.core = [[rc(5, line, cd)], [rc(6, got1, cd)]]
        if got2 is not None:
            self.core.append([rc(7, got2, cd)])
        else:
            self.core.append([rc((7, 9, 10)[d], full.at[:, pos.zoff(d + 1), :, c], cd) for d in range(3)])

    def start(self):
        for k in self.stages[0]:
            k.start()
        self.local.start()

    def step1(self):
        self.local.wait()
        for k in self.stages[0]:
            k.wait_recv()
        for k in self.stages[1]:
            k.start()
        for k in self.core[0]:
            k.start()

    def step2(self):
        for k in self.stages[1]:
            k.wait_recv()
        for k in self.stages[2]:
            k.start()
        for k in self.core[1]:
            k.start()

    def step3(self):
        for k in self.stages[2]:
            k.wait_recv()
        for k in self.core[2]:
            k.start()

    def finish(self):
        for stage in self.core:
            for k in stage:
                k.wait()
        for stage in self.stages:
            for k in stage:
                k.wait_send()


    def head1(self):
        self.start()

    def head2(self):
        if self.order == "xyz":
            self.step1()

    def head_finish(self):
        if self.order == "xyz":
            for k in self.stages[1]:
                k.wait_recv()
            for k in self.core[0]:
                k.wait()
            for k in self.stages[0] + self.stages[1]:
                k.wait_send()
        else:
            self.local.wait()
            for k in self.stages[0]:
                k.wait()

    def tail1(self):
        if self.order == "xyz":
            for k in self.stages[2]:
                k.start()
            for k in self.core[1]:
                k.start()
        else:
            for k in self.stages[1]:
                k.start()
            for k in self.core[0]:
                k.start()

    def tail2(self):
        if self.order != "xyz":
            self.step2()

    def tail3(self):
        self.step3()

    def tail_finish(self):
        if self.order == "xyz":
            for stage in self.core[1:]:
                for k in stage:
                    k.wait()
            for k in self.stages[2]:
                k.wait_send()
        else:
            for stage in self.core:
                for k in stage:
                    k.wait()
            for k in self.stages[1] + self.stages[2]:
                k.wait_send()


def gather_process(units, heads=()):
    for u in units:
        u.start()
    yield
    total = len(units)
    for t in range(total + 2):
        if t < total:
            units[t].step1()
            if t == total - 2 or total == 1:
                for u in heads:
                    u.head1()
            yield
        elif t == total:
            for u in heads:
                u.head2()
        if 0 <= t - 1 < total:
            units[t - 1].step2()
            yield
        if 0 <= t - 2 < total:
            units[t - 2].step3()
            yield
    for u in units:
        u.finish()
    for u in heads:
        u.head_finish()


def head_tail_process(heads, tails, lags):
    for u in heads:
        u.head1()
    total = len(tails)
    for t in range(total + lags[1]):
        if t == 0:
            for u in tails:
                if u.order == "zxy":
                    u.tail1()
        elif t < total and tails[t].order != "zxy":
            tails[t].tail1()
        if t == 1:
            for u in heads:
                u.head2()
        if 0 <= t - lags[0] < total:
            tails[t - lags[0]].tail2()
        if 0 <= t - lags[1] < total:
            tails[t - lags[1]].tail3()
        yield
    for u in tails:
        u.tail_finish()
    for u in heads:
        u.head_finish()


def tail_process(units, lags=(2, 4)):
    total = len(units)
    for t in range(total + lags[1]):
        if t < total:
            units[t].tail1()
        if 0 <= t - lags[0] < total:
            units[t - lags[0]].tail2()
        if 0 <= t - lags[1] < total:
            units[t - lags[1]].tail3()
        yield
    for u in units:
        u.tail_finish()


def both_processes(*processes):
    live = list(processes)
    while live:
        left = []
        for p in live:
            try:
                next(p)
                left.append(p)
            except StopIteration:
                pass
        live = left
        if live:
            yield


def after(first, second):
    yield from first
    yield from second


def gather_units(pos, units, shards, fulls, send, recv):
    return [
        Gather(pos, part_of(shards[a], r, c, 0), part_of(fulls[a], r, c, 4), send.at[k], recv.at[k], order)
        for k, (a, r, c, order) in enumerate(units)
    ]


def gather_shapes(shards):
    return [jax.ShapeDtypeStruct((2, 4, 2, 2) + s.shape, s.dtype) for s in shards]


def gather_sems(units):
    return [pltpu.SemaphoreType.DMA((len(units), N_AG)), pltpu.SemaphoreType.DMA((len(units), N_AG))]


N_RS = 8


def add_into(dst, src, count, index_dst, index_src):
    def step(i, carry):
        d, s = index_dst(i), index_src(i)
        dst[d] = dst[d] + src[s]
        return carry

    lax.fori_loop(0, count, step, 0)


def half_shape(size, order):
    return ((4, 2) if order == "yxz" else (2, 4)) + size


class ScatterHead:
    def __init__(self, pos, part, r1, r2, keep, own, other, send, recv, order):
        self.own, self.other = own, other
        y, x, c = pos.y, pos.x, pos.c
        self.cc = remote(part.at[:, :, :, 1 - c], r1, send, recv, 0, pos.dev(c=1 - c))
        self.loads = (
            pltpu.make_async_copy(part.at[:, :, :, c], own, send.at[2]),
            pltpu.make_async_copy(r1, other, send.at[3]),
        )
        if order == "yxz":
            self.c1 = remote(own.at[1 - y], r2, send, recv, 1, pos.dev(y=1 - y))
            self.store = pltpu.make_async_copy(own.at[y], keep, send.at[4])
        else:
            self.c1 = remote(own.at[:, :, 1 - x], r2, send, recv, 1, pos.dev(x=1 - x))
            self.store = pltpu.make_async_copy(own.at[:, :, x], keep, send.at[4])

    def send(self):
        self.cc.start()

    def load(self):
        self.cc.wait_recv()
        for k in self.loads:
            k.start()

    def step1(self):
        for k in self.loads:
            k.wait()
        at = lambda i: (i // 8, lax.rem(i // 2, 4), lax.rem(i, 2))
        add_into(self.own, self.other, 16, at, at)
        self.c1.start()
        self.store.start()

    def step2(self):
        self.c1.wait()
        self.store.wait()

    def finish(self):
        self.cc.wait_send()


class ScatterTail:
    def __init__(self, pos, keep, r2, out, h, g, r3, r4, send, recv, order):
        self.pos, self.out, self.order = pos, out, order
        self.h, self.g, self.r3, self.r4 = h, g, r3, r4
        y, x = pos.y, pos.x
        self.loads = (pltpu.make_async_copy(keep, h, send.at[4]), pltpu.make_async_copy(r2, g, send.at[5]))
        if order == "yxz":
            self.c2 = remote(h.at[:, 1 - x], r3, send, recv, 0, pos.dev(x=1 - x))
        else:
            self.c2 = remote(h.at[1 - y], r3, send, recv, 0, pos.dev(y=1 - y))
        self.cz = [remote(r3.at[pos.zoff(d)], r4.at[d - 1], send, recv, d, pos.dev(z=pos.zoff(d))) for d in (1, 2, 3)]

    def load(self):
        for k in self.loads:
            k.start()

    def step1(self):
        for k in self.loads:
            k.wait()
        if self.order == "yxz":
            at = lambda i: (i // 2, lax.rem(i, 2))
        else:
            at = lambda i: (i // 4, lax.rem(i, 4))
        add_into(self.h, self.g, 8, at, at)
        self.c2.start()

    def step2(self):
        y, x = self.pos.y, self.pos.x
        self.c2.wait()
        add_into(self.r3, self.h, 4, lambda i: (i,), (lambda i: (i, x)) if self.order == "yxz" else (lambda i: (y, i)))
        for k in self.cz:
            k.start()

    def step3(self):
        for k in self.cz:
            k.wait()
        f = lambda v: v.astype(F32)
        total = (f(self.r3[self.pos.z]) + f(self.r4[0])) + (f(self.r4[1]) + f(self.r4[2]))
        self.out[...] = total.astype(self.out.dtype)


def scatter_head_process(units, deep=3, ahead=3):
    lags = (1, deep)
    total = len(units)
    for u in units[:ahead]:
        u.send()
    yield
    for t in range(total + lags[1]):
        if t + ahead < total:
            units[t + ahead].send()
        for lag, step in ((lags[1], "step2"), (lags[0], "step1"), (0, "load")):
            if 0 <= t - lag < total:
                getattr(units[t - lag], step)()
        yield
    for u in units:
        u.finish()


def scatter_tail_process(units, deep=3, more=3):
    lags = (1, deep, deep + more)
    total = len(units)
    for t in range(total + lags[2]):
        for lag, step in ((lags[2], "step3"), (lags[1], "step2"), (lags[0], "step1"), (0, "load")):
            if 0 <= t - lag < total:
                getattr(units[t - lag], step)()
        yield


class Slots:
    def __init__(self):
        self.scratch, self.at, self.turn = [], {}, {}

    def take(self, kind, shape, most, want):
        key = (kind, shape)
        if key not in self.at:
            n = min(most, want)
            self.at[key] = (len(self.scratch), n)
            self.turn[key] = 0
            self.scratch += [pltpu.VMEM(shape, BF)] * n
        base, n = self.at[key]
        k = self.turn[key]
        self.turn[key] = k + 1
        return base + k % n


class ScatterPlan:
    def __init__(self, shapes, units, deep=3, others=1):
        self.units, self.deep, self.others = units, deep, others
        self.sizes = [(r[1] if r else shapes[a][0], c[1] if c else shapes[a][1]) for a, r, c, *_ in units]
        self.halves = [jax.ShapeDtypeStruct(half_shape(s, u[3]), BF) for s, u in zip(self.sizes, units)]
        self.r1_shapes = [jax.ShapeDtypeStruct((2, 4, 2) + s, BF) for s in self.sizes]
        self.n = len(units)

    def head_scratch(self):
        slots = Slots()
        kinds = [(2, 4, 2) + s for s in self.sizes]
        self.own_at = [slots.take("own", k, self.deep, kinds.count(k)) for k in kinds]
        self.other_at = [slots.take("other", k, self.others, kinds.count(k)) for k in kinds]
        return slots.scratch + [pltpu.SemaphoreType.DMA((self.n, 5)), pltpu.SemaphoreType.DMA((self.n, 2))]

    def head_bind(self, pos, parts, r1s, r2s, keeps, refs):
        send, recv = refs[-2:]
        return [
            ScatterHead(
                pos, part_of(parts[u[0]], u[1], u[2], 4), r1s[k], r2s[k], keeps[k], refs[self.own_at[k]], refs[self.other_at[k]],
                send.at[k], recv.at[k], u[3],
            )
            for k, u in enumerate(self.units)
        ]

    def tail_scratch(self):
        slots = Slots()
        kinds = [h.shape for h in self.halves]
        self.h_at = [slots.take("h", k, self.deep, kinds.count(k)) for k in kinds]
        self.g_at = [slots.take("g", k, self.others, kinds.count(k)) for k in kinds]
        self.landing = len(slots.scratch)
        scratch = slots.scratch
        for s in self.sizes:
            scratch += [pltpu.VMEM((4,) + s, BF), pltpu.VMEM((3,) + s, BF)]
        return scratch + [pltpu.SemaphoreType.DMA((self.n, 6)), pltpu.SemaphoreType.DMA((self.n, 4))]

    def tail_bind(self, pos, keeps, r2s, outs, refs):
        send, recv = refs[-2:]
        made = []
        for k, (a, r, c, order, base) in enumerate(self.units):
            o = (r[0] - base, r[1]) if r else None
            at = self.landing + 2 * k
            made.append(
                ScatterTail(
                    pos, keeps[k], r2s[k], part_of(outs[a], o, c, 0), refs[self.h_at[k]], refs[self.g_at[k]], refs[at], refs[at + 1],
                    send.at[k], recv.at[k], order,
                )
            )
        return made


def take(refs, *counts):
    out, at = [], 0
    for n in counts:
        out.append(refs[at : at + n])
        at += n
    return out + [refs[at:]]


def sum_process(pos, acc, land, zland, send, recv):
    copies = [remote(acc, zland.at[pos.z], send, recv, 2 + d, pos.dev(z=pos.zoff(d))) for d in (1, 2, 3)]
    zland[pos.z] = acc[...]
    for copy in copies:
        copy.start()
    yield
    for copy in copies:
        copy.wait()
    acc[...] = (zland[0] + zland[1]) + (zland[2] + zland[3])
    for i, dev in enumerate((pos.dev(c=1 - pos.c), pos.dev(x=1 - pos.x), pos.dev(y=1 - pos.y))):
        if land[i] is None:
            continue
        copy = remote(acc, land[i], send, recv, i, dev)
        copy.start()
        yield
        copy.wait()
        acc[...] += land[i][...]


def attend_kernel(
    patches, heads, units, n, hunits, hn, nm_ref, x_ref, gate_ref, w1_ref, w2_ref, qb_ref, ob_ref, e_ref, et_ref, info_ref, *refs
):
    shards, _, hshards, outs, fulls, hfulls, refs = take(refs, n, n, hn, 9, n, hn)
    wqkv_ref, wo_ref, q_ref, kvx_ref, probs_ref, attn_ref, ao_ref, resid_ref, residb_ref = outs
    w1_buf, w2_buf, wqkv_buf, wo_buf, halo_out, halo_in, sems, send, recv, g_send, g_recv, h_send, h_recv = refs
    pos = Place()
    rows, width = x_ref.shape
    frames = rows // patches
    count, y = info_ref[0], info_ref[1]
    loads = (
        pltpu.make_async_copy(w1_ref, w1_buf, sems.at[0]),
        pltpu.make_async_copy(w2_ref, w2_buf, sems.at[1]),
    )
    for c in loads:
        c.start()
    barrier(pos)
    tick = Ticker(
        head_tail_process(
            gather_units(pos, hunits, hshards, hfulls, h_send, h_recv), gather_units(pos, units, shards, fulls, g_send, g_recv), (2, 4)
        )
    )
    tick()
    cut = 3 * width // 2
    half = width // 2
    loads[0].wait()
    for f in range(2):
        wqkv_buf[:, f * cut : (f + 1) * cut] = w1_buf[f, :, :cut]
    loads[1].wait()
    for f in range(2):
        wo_buf[:, f * half : (f + 1) * half] = w2_buf[f, :, :half]
    keep = (
        pltpu.make_async_copy(wqkv_buf, wqkv_ref, sems.at[2]),
        pltpu.make_async_copy(wo_buf, wo_ref, sems.at[3]),
    )
    for c in keep:
        c.start()
    zero = jnp.zeros((patches, 2 * width), BF)
    kvx_ref[0:patches, :] = zero
    kvx_ref[(frames + 1) * patches :, :] = zero
    own = slice(patches, (frames + 1) * patches)
    for third in (1, 2, 0):
        cols = slice(third * width, (third + 1) * width)
        got = (dot(nm_ref[...], wqkv_buf[:, cols]) + qb_ref[:, cols]).astype(BF)
        if third == 0:
            q_ref[...] = got
        else:
            kvx_ref[own, (third - 1) * width : third * width] = got
        if third == 2:
            copy = halo_send(pos, frames, patches, count, y, kvx_ref, halo_out, halo_in, send, recv)
    tick()
    copy.wait()
    place = jnp.where(y == 0, count, -1) + 1

    def settle(s):
        r = rows_at(s * patches, patches)
        hit = jnp.full((patches, 2 * width), (s == place).astype(F32), F32)
        kvx_ref[r, :] = jnp.where(hit > 0.5, halo_in[...].astype(F32), kvx_ref[r, :].astype(F32)).astype(BF)

    each(frames + 2, settle)
    tick()
    scale = (width // heads) ** (-0.5)
    for t in range(frames // 3):
        attend_tile(t, 3, patches, count, y, scale, q_ref, kvx_ref, e_ref, et_ref, probs_ref, attn_ref)
        tick()
    resid_ref[...] = dot(attn_ref[...], wo_buf[...]) + ob_ref[...]
    tick()

    def frame(s):
        r = rows_at(s * patches, patches)
        ao = resid_ref[r, :]
        ao_ref[r, :] = ao.astype(BF)
        resid = x_ref[r, :].astype(F32) + gate_ref[...] * ao
        resid_ref[r, :] = resid
        residb_ref[r, :] = resid.astype(BF)

    each(frames, frame)
    for c in keep:
        c.wait()
    tick.drain()


def pick_slot(frames, patches, slot, src_ref, dst_ref):
    dst_ref[...] = jnp.zeros(dst_ref.shape, dst_ref.dtype)

    def step(s):
        r = rows_at(s * patches, patches)
        hit = jnp.full(dst_ref.shape, (s == slot).astype(F32), F32)
        dst_ref[...] = jnp.where(hit > 0.5, src_ref[r, :].astype(F32), dst_ref[...].astype(F32)).astype(dst_ref.dtype)

    each(frames, step)


def halo_send(pos, frames, patches, count, y, kvx_ref, halo_out, halo_in, send, recv):
    pick_slot(frames + 2, patches, jnp.where(y == 0, count - 1, 0) + 1, kvx_ref, halo_out)
    copy = pltpu.make_async_remote_copy(
        src_ref=halo_out, dst_ref=halo_in, send_sem=send, recv_sem=recv,
        device_id=pos.dev(y=1 - pos.y), device_id_type=MESH,
    )
    copy.start()
    return copy


def attend_call(patches, heads, nm, x, gate, w1, w2, qb, ob, e, et, info, shards, fulls, units, hshards, hunits, ident):
    rows, width = x.shape
    frames = rows // patches
    ext = (frames + 2) * patches
    S = jax.ShapeDtypeStruct
    n, hn = len(shards), len(hshards)
    out = pl.pallas_call(
        partial(attend_kernel, patches, heads, units, n, hunits, hn),
        out_shape=[
            S((width, 3 * width), BF), S((width, width), BF), S((rows, width), BF), S((ext, 2 * width), BF),
            S((3, rows, 128), F32), S((rows, width), BF), S((rows, width), BF), S((rows, width), F32), S((rows, width), BF),
        ]
        + gather_shapes(shards)
        + gather_shapes(hshards),
        in_specs=[IN_VMEM] * 3 + [IN_ANY] * 2 + [IN_VMEM] * 4 + [IN_SMEM] + [IN_ANY] * (2 * n + hn),
        out_specs=[IN_ANY] * 2 + [IN_VMEM] * 7 + [IN_ANY] * (n + hn),
        input_output_aliases={10 + n + i: 9 + i for i in range(n)},
        scratch_shapes=[
            pltpu.VMEM(w1.shape, BF), pltpu.VMEM(w2.shape, BF), pltpu.VMEM((width, 3 * width), BF), pltpu.VMEM((width, width), BF),
            pltpu.VMEM((patches, 2 * width), BF), pltpu.VMEM((patches, 2 * width), BF),
            pltpu.SemaphoreType.DMA((4,)), pltpu.SemaphoreType.DMA, pltpu.SemaphoreType.DMA,
        ]
        + gather_sems(units)
        + gather_sems(hunits),
        compiler_params=pltpu.CompilerParams(collective_id=ident, has_side_effects=True, vmem_limit_bytes=VMEM_LIMIT),
        name="attend",
    )(nm, x, gate, w1, w2, qb, ob, e, et, info, *shards, *fulls, *hshards)
    return out[:9], [g.reshape(2, -1, g.shape[-1]) for g in out[9 : 9 + n]], out[9 + n :]


def clip_rows(one_ref, rows):
    total = None
    for c, row in enumerate(rows):
        term = one_ref[:, c : c + 1] * row
        total = term if total is None else total + term
    return total


def open_kernel(patches, units, count, hunits, hcount, x_ref, part_ref, table_ref, one_ref, *refs):
    shards, hshards, (nm_ref, scale_ref, gate_ref, mods_ref), fulls, hfulls, refs = take(refs, count, hcount, 4, count, hcount)
    shift_ref, acc, land_c, land_x, zland, both, g_send, g_recv, h_send, h_recv, s_send, s_recv = refs
    pos = Place()
    width = x_ref.shape[1]
    clips = one_ref.shape[1]
    barrier(pos)
    heads = gather_units(pos, hunits, hshards, hfulls, h_send, h_recv)
    tick = Ticker(gather_process(gather_units(pos, units, shards, fulls, g_send, g_recv), heads))
    acc[...] = part_ref[...]
    small = Ticker(sum_process(pos, acc, (land_c, land_x, None), zland, s_send, s_recv))
    small()
    small()
    tick()
    small.drain()
    both[pos.y] = acc[...]
    swap = remote(acc, both.at[pos.y], s_send, s_recv, 2, pos.dev(y=1 - pos.y))
    swap.start()
    swap.wait()
    for k in range(6):
        f, u = k // 3, k % 3
        rows = [
            both[f, c : c + 1, u * width : (u + 1) * width] + table_ref[k : k + 1, :] for c in range(clips)
        ]
        (shift_ref, scale_ref, gate_ref, mods_ref.at[0], mods_ref.at[1], mods_ref.at[2])[k][...] = clip_rows(one_ref, rows)
        if k % 2:
            tick()

    def frame(s):
        r = rows_at(s * patches, patches)
        xhat, _ = normalise(x_ref[r, :].astype(F32))
        nm_ref[r, :] = (xhat * (1.0 + scale_ref[...]) + shift_ref[...]).astype(BF)

    each(x_ref.shape[0] // patches, frame)
    tick.drain()


def open_call(patches, x, part, table, one, shards, units, hshards, hunits, ident):
    rows, width = x.shape
    count, hcount = len(shards), len(hshards)
    S = jax.ShapeDtypeStruct
    out = pl.pallas_call(
        partial(open_kernel, patches, units, count, hunits, hcount),
        out_shape=[S((rows, width), BF), S((patches, width), F32), S((patches, width), F32), S((3, patches, width), F32)]
        + gather_shapes(shards)
        + gather_shapes(hshards),
        in_specs=[IN_VMEM] * 4 + [IN_ANY] * (count + hcount),
        out_specs=[IN_VMEM] * 4 + [IN_ANY] * (count + hcount),
        scratch_shapes=[
            pltpu.VMEM((patches, width), F32),
            pltpu.VMEM(part.shape, F32), pltpu.VMEM(part.shape, F32), pltpu.VMEM(part.shape, F32),
            pltpu.VMEM((4,) + part.shape, F32), pltpu.VMEM((2,) + part.shape, F32),
        ]
        + gather_sems(units)
        + gather_sems(hunits)
        + [pltpu.SemaphoreType.DMA((6,)), pltpu.SemaphoreType.DMA((6,))],
        compiler_params=pltpu.CompilerParams(collective_id=ident, has_side_effects=True, vmem_limit_bytes=VMEM_LIMIT),
        name="open",
    )(x, part, table, one, *shards, *hshards)
    return out[:4], [g.reshape(2, -1, g.shape[-1]) for g in out[4 : 4 + count]], out[4 + count :]


def cross_kernel(
    patches, heads, units, n, resid_ref, residb_ref, mods_ref, used_ref, cm_ref, w2_ref, w3_ref, kv_ref, b3_ref, b4_ref, b5_ref, *refs
):
    shards, _, (wq_ref, wco_ref, q_ref, keys_ref, vals_ref, lse_ref, mixb_ref, rc_ref, nm_ref), fulls, refs = take(refs, n, n, 9, n)
    w2_buf, w3_buf, kv_buf, wq_buf, wco_buf, mix_buf, cmask, sems, g_send, g_recv = refs
    pos = Place()
    rows, width = resid_ref.shape
    frames = rows // patches
    half = width // 2
    loads = (
        pltpu.make_async_copy(kv_ref, kv_buf, sems.at[0]),
        pltpu.make_async_copy(w2_ref, w2_buf, sems.at[1]),
        pltpu.make_async_copy(w3_ref, w3_buf, sems.at[4]),
    )
    for c in loads:
        c.start()
    barrier(pos)
    tick = Ticker(tail_process(gather_units(pos, units, shards, fulls, g_send, g_recv), (4, 8)))
    tick()
    for i in range(3):
        cmask[i * patches : (i + 1) * patches, :] = cm_ref[...]
    mix_buf[...] = jnp.zeros(mix_buf.shape, F32)
    loads[0].wait()
    keys_ref[...] = dot(used_ref[...], kv_buf[0]).astype(BF)
    vals_ref[...] = (dot(used_ref[...], kv_buf[1]) + b4_ref[...]).astype(BF)
    loads[1].wait()
    loads[2].wait()
    for f in range(2):
        wq_buf[:, f * half : (f + 1) * half] = w2_buf[f]
        wco_buf[:, f * half : (f + 1) * half] = w3_buf[f]
    keep = (
        pltpu.make_async_copy(wq_buf, wq_ref, sems.at[2]),
        pltpu.make_async_copy(wco_buf, wco_ref, sems.at[3]),
    )
    for c in keep:
        c.start()
    q_ref[...] = (dot(residb_ref[...], wq_buf[...]) + b3_ref[...]).astype(BF)
    tick()
    for h in range(heads):
        cross_head(h, heads, rows // cmask.shape[0], q_ref, keys_ref, vals_ref, cmask, lse_ref, mix_buf)
        if h % 2:
            tick()
    mixb_ref[...] = mix_buf[...].astype(BF)
    rc_ref[...] = dot(mixb_ref[...], wco_buf[...]) + b5_ref[...]

    def frame(s):
        r = rows_at(s * patches, patches)
        rc = rc_ref[r, :] + resid_ref[r, :]
        rc_ref[r, :] = rc
        xhat, _ = normalise(rc)
        nm_ref[r, :] = (xhat * (1.0 + mods_ref[1]) + mods_ref[0]).astype(BF)

    each(frames, frame)
    for c in keep:
        c.wait()
    tick.drain()


def cross_call(patches, heads, resid, residb, mods, used, cm, w2, w3, kv, b3, b4, b5, shards, fulls, units, ident):
    rows, width = resid.shape
    caps = used.shape[0]
    S = jax.ShapeDtypeStruct
    n = len(shards)
    out = pl.pallas_call(
        partial(cross_kernel, patches, heads, units, n),
        out_shape=[
            S((width, width), BF), S((width, width), BF), S((rows, width), BF), S((caps, width), BF), S((caps, width), BF),
            S((rows, 128), F32), S((rows, width), BF), S((rows, width), F32), S((rows, width), BF),
        ]
        + gather_shapes(shards),
        in_specs=[IN_VMEM] * 5 + [IN_ANY] * 3 + [IN_VMEM] * 3 + [IN_ANY] * 2 * n,
        out_specs=[IN_ANY] * 2 + [IN_VMEM] * 7 + [IN_ANY] * n,
        input_output_aliases={11 + n + i: 9 + i for i in range(n)},
        scratch_shapes=[
            pltpu.VMEM(w2.shape, BF), pltpu.VMEM(w3.shape, BF), pltpu.VMEM(kv.shape, BF), pltpu.VMEM((width, width), BF), pltpu.VMEM((width, width), BF),
            pltpu.VMEM((rows, width), F32), pltpu.VMEM((3 * patches, caps), F32), pltpu.SemaphoreType.DMA((5,)),
        ]
        + gather_sems(units),
        compiler_params=pltpu.CompilerParams(collective_id=ident, has_side_effects=True, vmem_limit_bytes=VMEM_LIMIT),
        name="cross",
    )(resid, residb, mods, used, cm, w2, w3, kv, b3, b4, b5, *shards, *fulls)
    return out[:9], [g.reshape(2, -1, g.shape[-1]) for g in out[9:]]


def mlp_kernel(
    chunk, patches, plan, nm_ref, cot_ref, valid_ref, rc_ref, mods_ref, hb_ref, b6_ref, win_ref, wout_ref, *refs
):
    m = plan.n
    outs, r1s, r2s, keeps, refs = take(refs, 7, m, m, m)
    out_ref, grc_ref, hsum_ref, bsum_ref, gp_ref, dwin_ref, dwout_ref = outs
    (gm_ref, res_ref, win_b, wout_h, wout_b, act_b, gpre_b, din_s, dout_s, in_sem, out_sem), refs = refs[:11], refs[11:]
    pos = Place()
    rows, width = nm_ref.shape
    frames = rows // patches
    half = wout_ref.shape[2]
    per = win_ref.shape[2] // chunk
    total = 2 * per

    def places(j):
        f, u = lax.rem(j, 2), j // 2
        return f, f * per + u, pl.ds(pl.multiple_of(u * chunk, 128), chunk)

    def loads(j, slot):
        f, at, cols = places(j)
        rws = pl.ds(pl.multiple_of(at * chunk, 128), chunk)
        return (
            pltpu.make_async_copy(win_ref.at[f, :, cols], win_b.at[slot], in_sem.at[slot, 0]),
            pltpu.make_async_copy(wout_ref.at[:, rws], wout_h.at[slot], in_sem.at[slot, 1]),
        )

    def stores(j):
        f, at, cols = places(j)
        rws = pl.ds(pl.multiple_of(at * chunk, 128), chunk)
        return (
            pltpu.make_async_copy(din_s, dwin_ref.at[f, :, :, :, :, cols], out_sem.at[0]),
            pltpu.make_async_copy(dout_s, dwout_ref.at[:, rws], out_sem.at[1]),
        )

    for c in loads(0, 0):
        c.start()
    barrier(pos)
    units = plan.head_bind(pos, [dwin_ref], r1s, r2s, keeps, refs)
    bsum_ref[...] = jnp.zeros(bsum_ref.shape, F32)
    gp_ref[...] = jnp.zeros(gp_ref.shape, F32)

    def prepare(s):
        r = rows_at(s * patches, patches)
        gf = jnp.where(valid_ref[r, :] > 0.5, cot_ref[r, :].astype(F32), 0.0)
        gm = (mods_ref[2] * gf).astype(BF)
        gm_ref[r, :] = gm
        bsum_ref[0:1, :] += jnp.sum(gm.astype(F32), axis=0, keepdims=True)

    each(frames, prepare)

    def reduce(j, late, step):
        for u in range(per - 1):

            @pl.when(j == 2 * u + 2 + late)
            def _():
                for unit in units[2 * u : 2 * u + 2]:
                    getattr(unit, step)()

    def step(j, carry):
        slot = lax.rem(j, 2)
        _, at, _ = places(j)
        for c in loads(j, slot):
            c.wait()

        @pl.when(j + 1 < total)
        def _():
            for c in loads(j + 1, 1 - slot):
                c.start()

        wout_b[...] = jnp.concatenate([wout_h[slot, 0], wout_h[slot, 1]], axis=1)
        pre = dot(nm_ref[...], win_b[slot]) + hb_ref[pl.ds(at, 1), :]
        act, slope = gelu_parts(pre)
        act_b[...] = act.astype(BF)
        gpre = (dot_nt(gm_ref[...], wout_b[...]) * slope).astype(BF)
        gpre_b[...] = gpre
        hsum_ref[pl.ds(at, 1), :] = jnp.sum(gpre.astype(F32), axis=0, keepdims=True)

        @pl.when(j >= 1)
        def _():
            for c in stores(j - 1):
                c.wait()

        reduce(j, 0, "send")
        part = dot(act_b[...], wout_b[...])

        @pl.when(j == 0)
        def _():
            res_ref[...] = part

        @pl.when(j > 0)
        def _():
            res_ref[...] += part

        reduce(j, 0, "load")
        back = dot_nt(gpre_b[...], win_b[slot])

        @pl.when(j == 0)
        def _():
            grc_ref[...] = back

        @pl.when(j > 0)
        def _():
            grc_ref[...] += back

        reduce(j, 0, "step1")
        din_s[...] = dot_tn(nm_ref[...], gpre_b[...]).reshape(din_s.shape).astype(BF)
        d = dot_tn(act_b[...], gm_ref[...]).astype(BF)
        dout_s[0] = d[:, :half]
        dout_s[1] = d[:, half:]
        for c in stores(j):
            c.start()
        reduce(j, 1, "step2")
        return carry

    lax.fori_loop(0, total, step, 0)

    def finish(s):
        r = rows_at(s * patches, patches)
        ok = valid_ref[r, :] > 0.5
        rc = rc_ref[r, :]
        res = res_ref[r, :] + b6_ref[...]
        gf = jnp.where(ok, cot_ref[r, :].astype(F32), 0.0)
        out_ref[r, :] = jnp.where(ok, rc + mods_ref[2] * res, 0.0).astype(BF)
        xhat, rstd = normalise(rc)
        g = grc_ref[r, :]
        gp_ref[0] += g
        gp_ref[1] += g * xhat
        gp_ref[2] += gf * res
        grc_ref[r, :] = gf + normalise_back(xhat, rstd, g, mods_ref[1])

    each(frames, finish)
    for c in stores(total - 1):
        c.wait()
    for unit in units:
        unit.finish()


def mlp_call(patches, nm, cot, valid, rc, mods, hb, b6, win, wout, shard, plan, ident):
    rows, width = nm.shape
    chunk = 768
    total = 2 * win.shape[2] // chunk
    half = wout.shape[2]
    m = plan.n
    comm_scratch = plan.head_scratch()
    S = jax.ShapeDtypeStruct
    out = pl.pallas_call(
        partial(mlp_kernel, chunk, patches, plan),
        out_shape=[
            S((rows, width), BF), S((rows, width), F32), S((total, chunk), F32), S((8, width), F32), S((3, patches, width), F32),
            S((2, 4, 2, 2) + shard, BF), S(wout.shape, BF),
        ]
        + plan.r1_shapes
        + plan.halves
        + plan.halves,
        in_specs=[IN_VMEM] * 7 + [IN_ANY] * 2,
        out_specs=[IN_VMEM] * 5 + [IN_ANY] * (2 + 3 * m),
        scratch_shapes=[
            pltpu.VMEM((rows, width), BF), pltpu.VMEM((rows, width), F32),
            pltpu.VMEM((2, width, chunk), BF), pltpu.VMEM((2, 2, chunk, half), BF), pltpu.VMEM((chunk, width), BF),
            pltpu.VMEM((rows, chunk), BF), pltpu.VMEM((rows, chunk), BF),
            pltpu.VMEM((4, 2, 2, width // 16, chunk), BF), pltpu.VMEM((2, chunk, half), BF),
            pltpu.SemaphoreType.DMA((2, 2)), pltpu.SemaphoreType.DMA((2,)),
        ]
        + comm_scratch,
        compiler_params=pltpu.CompilerParams(collective_id=ident, has_side_effects=True, vmem_limit_bytes=VMEM_LIMIT),
        name="mlp",
    )(nm, cot, valid, rc, mods, hb.reshape(total, chunk), b6, win, wout)
    return out[:7], out[7 + m : 7 + 2 * m], out[7 + 2 * m :]


def cross_back_kernel(
    patches, heads, tail, plan, extra, n, cuts, grc_ref, q_ref, keys_ref, vals_ref, lse_ref, cm_ref, gate_ref,
    mixb_ref, residb_ref, attn_ref, ao_ref, wco_ref, wq_ref, wo_ref, *refs
):
    m, mt = plan.n, tail.n
    parts, keeps_in, r2s_in, outs8, shards, r1s, r2s, keeps, tmp, refs = take(refs, n, mt, mt, 8, 1, m, m, m, 3)
    gra_ref, gai_ref, gkvb_ref, bsum_ref, gp_ref, dwo_ref, dwq_ref, dwco_ref = outs8
    (w_buf, a_buf, gcb, gmix, gkv, p_buf, ds_buf, cmask, dw_s, sems, out_sem), h_refs, t_refs, x_refs, _ = take(refs, 11, *cuts)
    pos = Place()
    rows, width = grc_ref.shape
    frames = rows // patches
    half = width // 2
    scale = (width // heads) ** (-0.5)
    gq = gra_ref
    loads = [pltpu.make_async_copy(src, w_buf, sems.at[i]) for i, src in enumerate((wco_ref, wq_ref, wo_ref))]
    acts = [
        pltpu.make_async_copy(src, a_buf.at[i % 2], sems.at[3 + i])
        for i, src in enumerate((mixb_ref, residb_ref, ao_ref, attn_ref))
    ]
    outs = [pltpu.make_async_copy(dw_s, dst, out_sem.at[i]) for i, dst in enumerate((dwco_ref, dwq_ref, dwo_ref))]
    loads[0].start()
    acts[0].start()
    acts[1].start()
    barrier(pos)
    tails = scatter_tail_process(tail.tail_bind(pos, keeps_in, r2s_in, shards, t_refs), tail.deep, 4)
    tick = Ticker(both_processes(scatter_head_process(plan.head_bind(pos, parts, r1s, r2s, keeps, h_refs), plan.deep), tails))
    tick()
    for i in range(3):
        cmask[i * patches : (i + 1) * patches, :] = cm_ref[...]
    bsum_ref[...] = jnp.zeros(bsum_ref.shape, F32)
    gp_ref[...] = jnp.zeros(gp_ref.shape, F32)
    gkv[...] = jnp.zeros(gkv.shape, F32)
    gq[...] = jnp.zeros(gq.shape, F32)

    def first(s):
        r = rows_at(s * patches, patches)
        g = grc_ref[r, :].astype(BF)
        gcb[r, :] = g
        bsum_ref[0:1, :] += jnp.sum(g.astype(F32), axis=0, keepdims=True)

    each(frames, first)
    loads[0].wait()
    gmix[...] = dot_nt(gcb[...], w_buf[...]).astype(BF)
    loads[1].start()

    def weight_grad(k, left, right):
        d = dot_tn(left, right).astype(BF)
        for f in range(2):
            dw_s[f] = d[:, f * half : (f + 1) * half]
        outs[k].start()

    acts[0].wait()
    weight_grad(0, a_buf[0], gcb[...])
    acts[2].start()
    tick()
    for h in range(heads):
        cross_head_back(
            h, heads, rows // cmask.shape[0], q_ref, keys_ref, vals_ref, cmask, lse_ref, gmix, gq, gkv, p_buf, ds_buf
        )
        if h % 2:
            tick()
    gkvb_ref[...] = gkv[...].reshape(gkvb_ref.shape).astype(BF)
    captions = Ticker(scatter_head_process(extra.head_bind(pos, [gkvb_ref], tmp[:1], tmp[1:2], tmp[2:3], x_refs)))
    captions()

    def second(s):
        r = rows_at(s * patches, patches)
        g = (gq[r, :] * scale).astype(BF)
        gcb[r, :] = g
        bsum_ref[1:2, :] += jnp.sum(g.astype(F32), axis=0, keepdims=True)

    each(frames, second)
    captions()
    acts[1].wait()
    outs[0].wait()
    weight_grad(1, a_buf[1], gcb[...])
    acts[3].start()
    tick()
    captions()
    loads[1].wait()
    gra_ref[...] = dot_nt(gcb[...], w_buf[...])
    loads[2].start()
    acts[2].wait()
    tick()
    captions()

    def third(s):
        r = rows_at(s * patches, patches)
        gra = gra_ref[r, :] + grc_ref[r, :]
        gra_ref[r, :] = gra
        gp_ref[...] += gra * a_buf[0, r, :].astype(F32)
        g = (gate_ref[...] * gra).astype(BF)
        gmix[r, :] = g
        bsum_ref[2:3, :] += jnp.sum(g.astype(F32), axis=0, keepdims=True)

    each(frames, third)
    loads[2].wait()
    tick()
    gai_ref[...] = dot_nt(gmix[...], w_buf[...]).astype(BF)
    tick()
    acts[3].wait()
    outs[1].wait()
    weight_grad(2, a_buf[1], gmix[...])
    tick.drain()
    captions.drain()
    outs[2].wait()


def cross_back_call(
    patches, heads, grc, mixb, q, keys, vals, lse, cm, residb, attn, ao, gate, wco, wq, wo, keeps, r2s, tail, tail_outs, parts, plan, ident
):
    rows, width = grc.shape
    caps = keys.shape[0]
    n = len(parts)
    m, mt = plan.n, tail.n
    kv_blocks = (caps // 16, width)
    extra = ScatterPlan([kv_blocks], SCATTER_KV)
    scratches = [plan.head_scratch(), tail.tail_scratch(), extra.head_scratch()]
    S = jax.ShapeDtypeStruct
    out = pl.pallas_call(
        partial(cross_back_kernel, patches, heads, tail, plan, extra, n, [len(s) for s in scratches]),
        out_shape=[
            S((rows, width), F32), S((rows, width), BF), S((2, 4, 2, 2) + kv_blocks, BF), S((8, width), F32), S((patches, width), F32),
        ]
        + [S((2, width, width // 2), BF)] * 3
        + [S(tail_outs, F32)]
        + plan.r1_shapes
        + plan.halves
        + plan.halves
        + extra.r1_shapes
        + extra.halves
        + extra.halves,
        in_specs=[IN_VMEM] * 7 + [IN_ANY] * (7 + n + 2 * mt),
        out_specs=[IN_VMEM] * 5 + [IN_ANY] * 3 + [IN_VMEM] + [IN_ANY] * (3 * m + 3),
        scratch_shapes=[
            pltpu.VMEM((width, width), BF), pltpu.VMEM((2, rows, width), BF), pltpu.VMEM((rows, width), BF), pltpu.VMEM((rows, width), BF),
            pltpu.VMEM((2, caps, width), F32),
            pltpu.VMEM((rows, caps), BF), pltpu.VMEM((rows, caps), BF), pltpu.VMEM((3 * patches, caps), F32),
            pltpu.VMEM((2, width, width // 2), BF),
            pltpu.SemaphoreType.DMA((7,)), pltpu.SemaphoreType.DMA((3,)),
        ]
        + sum(scratches, []),
        compiler_params=pltpu.CompilerParams(collective_id=ident, has_side_effects=True, vmem_limit_bytes=VMEM_LIMIT),
        name="cross_back",
    )(grc, q, keys, vals, lse, cm, gate, mixb, residb, attn, ao, wco, wq, wo, *parts, *keeps, *r2s)
    return out[:8], out[8], out[9 + m : 9 + 2 * m], out[9 + 2 * m : 9 + 3 * m], (out[11 + 3 * m], out[10 + 3 * m])


def attend_back_kernel(
    patches, heads, tail, head, extra, n, cuts, gai_ref, q_ref, kvx_ref, probs_ref, e_ref, et_ref, info_ref, nm_ref, *refs
):
    mt, mh = tail.n, head.n
    keeps_in, r2s_in, parts, kv_keep, kv_r2, outs5, shards, r1s, r2s, keeps, refs = take(refs, mt, mt, n, 1, 1, 5, 3, mh, mh, mh)
    gq_ref, gk_ref, gv_ref, bsum_ref, dw_ref = outs5
    (gkv, halo_out, halo_in, dw_s, a_buf, sems, send, recv), t_refs, h_refs, xt_refs, _ = take(refs, 8, *cuts)
    loads = (pltpu.make_async_copy(gai_ref, a_buf, sems.at[2]), pltpu.make_async_copy(nm_ref, a_buf, sems.at[3]))
    loads[0].start()
    pos = Place()
    rows, width = q_ref.shape
    frames = rows // patches
    half = width // 2
    count, y = info_ref[0], info_ref[1]
    barrier(pos)
    tails = scatter_tail_process(tail.tail_bind(pos, keeps_in, r2s_in, shards[:2], t_refs), tail.deep, 4)
    heads_ = scatter_head_process(head.head_bind(pos, parts, r1s, r2s, keeps, h_refs))
    captions = scatter_tail_process(extra.tail_bind(pos, kv_keep, kv_r2, shards[2:], xt_refs))
    tick = Ticker(both_processes(captions, tails, heads_))
    tick()
    gkv[...] = jnp.zeros(gkv.shape, F32)
    tick()
    scale = (width // heads) ** (-0.5)
    loads[0].wait()
    for t in range(frames // 3):
        attend_tile_back(t, 3, patches, scale, q_ref, kvx_ref, e_ref, et_ref, probs_ref, a_buf, gq_ref, gkv)
        tick()
    loads[1].start()
    place = jnp.where(y == 0, count, -1) + 1
    pick_slot(frames + 2, patches, place, gkv, halo_out)
    copy = remote(halo_out, halo_in, send, recv, 0, pos.dev(y=1 - pos.y))
    copy.start()
    bsum_ref[...] = jnp.zeros(bsum_ref.shape, F32)
    loads[1].wait()
    for low, high in ((0, 640), (640, width)):
        tick()
        dw_s[:, low:high] = dot_tn(a_buf[...], gq_ref[:, low:high]).astype(BF)
    tick()
    copy.wait()
    mine = jnp.where(y == 0, count - 1, 0) + 1

    def settle(s):
        r = rows_at((s + 1) * patches, patches)
        o = rows_at(s * patches, patches)
        shape = (patches, 2 * width)
        drop = jnp.full(shape, (s + 1 == place).astype(F32), F32)
        add = jnp.full(shape, (s + 1 == mine).astype(F32), F32)
        g = jnp.where(drop > 0.5, 0.0, gkv[r, :]) + jnp.where(add > 0.5, halo_in[...].astype(F32), 0.0)
        g = g.astype(BF)
        gk_ref[o, :] = g[:, :width]
        gv_ref[o, :] = g[:, width:]
        bsum_ref[0:1, :] += jnp.sum(gq_ref[o, :].astype(F32), axis=0, keepdims=True)
        bsum_ref[1:2, :] += jnp.sum(g[:, width:].astype(F32), axis=0, keepdims=True)

    each(frames, settle)
    tick()
    dw_s[:, width:] = dot_tn(a_buf[...], gk_ref[:, :half]).astype(BF)
    out = [pltpu.make_async_copy(dw_s, dw_ref.at[f], sems.at[f]) for f in range(2)]
    out[0].start()
    tick()
    out[0].wait()
    dw_s[:, :half] = dot_tn(a_buf[...], gk_ref[:, half:]).astype(BF)
    tick()
    for low, high in ((0, half), (half, width)):
        dw_s[:, half + low : half + high] = dot_tn(a_buf[...], gv_ref[:, low:high]).astype(BF)
    out[1].start()
    tick.drain()
    out[1].wait()


def attend_back_call(
    patches, heads, gai, q, kvx, probs, e, et, info, nm, keeps, r2s, tail, tail_outs, parts, shard_shapes, units, kv_keep, kv_r2, kv_blocks, ident
):
    rows, width = q.shape
    cols = 3 * width // 2
    head = ScatterPlan(shard_shapes, units)
    extra = ScatterPlan([kv_blocks], SCATTER_KV)
    n, mt, mh = len(parts), tail.n, head.n
    scratches = [tail.tail_scratch(), head.head_scratch(), extra.tail_scratch()]
    S = jax.ShapeDtypeStruct
    out = pl.pallas_call(
        partial(attend_back_kernel, patches, heads, tail, head, extra, n, [len(s) for s in scratches]),
        out_shape=[S((rows, width), BF)] * 3
        + [S((8, width), F32), S((2, width, cols), BF)]
        + [S(s, F32) for s in tail_outs]
        + [S(kv_blocks, BF)]
        + head.r1_shapes
        + head.halves
        + head.halves,
        in_specs=[IN_ANY] + [IN_VMEM] * 5 + [IN_SMEM] + [IN_ANY] * (3 + 2 * mt + n),
        out_specs=[IN_VMEM] * 4 + [IN_ANY] + [IN_VMEM] * 3 + [IN_ANY] * (3 * mh),
        scratch_shapes=[
            pltpu.VMEM(kvx.shape, F32), pltpu.VMEM((patches, 2 * width), BF), pltpu.VMEM((patches, 2 * width), BF),
            pltpu.VMEM((width, cols), BF), pltpu.VMEM((rows, width), BF),
            pltpu.SemaphoreType.DMA((4,)), pltpu.SemaphoreType.DMA((1,)), pltpu.SemaphoreType.DMA((1,)),
        ]
        + sum(scratches, []),
        compiler_params=pltpu.CompilerParams(collective_id=ident, has_side_effects=True, vmem_limit_bytes=VMEM_LIMIT),
        name="attend_back",
    )(gai, q, kvx, probs, e, et, info, nm, *keeps, *r2s, *parts, kv_keep, kv_r2)
    return out[:5], out[5:8], out[8 + mh : 8 + 2 * mh], out[8 + 2 * mh : 8 + 3 * mh]


def close_kernel(
    patches, tail, plan, gunits, cuts, gq_ref, gk_ref, gv_ref, x_ref, scale_ref, gpg_ref, gpm_ref,
    ba_ref, bc_ref, bm_ref, hsum_ref, one_ref, used_ref,
    gra_ref, wqkv_ref, wkv_ref, kvlow_ref, *refs
):
    mt, m = tail.n, plan.n
    keeps_in, r2s_in, parts, outs6, tshards, shards, r1s, r2s, keeps, refs = take(refs, mt, mt, 1, 6, 3, 1, m, m, m)
    ig_ref, sum_ref, last_ref, rows_ref, kvg_ref, kvfull_ref = outs6
    mine_refs, t_refs, h_refs, c_refs, _ = take(refs, 15, *cuts)
    w_buf, late, gp, kv_buf, lands, zland, lands2, zland2, sems, g_send, g_recv, s_send, s_recv, s_send2, s_recv2 = mine_refs
    pos = Place()
    rows, width = x_ref.shape
    frames = rows // patches
    clips = one_ref.shape[1]
    loads = (
        pltpu.make_async_copy(wqkv_ref, w_buf, sems.at[0]),
        pltpu.make_async_copy(gra_ref, late, sems.at[1]),
        pltpu.make_async_copy(wkv_ref.at[0], w_buf.at[:, pl.ds(0, width)], sems.at[2]),
        pltpu.make_async_copy(wkv_ref.at[1], w_buf.at[:, pl.ds(width, width)], sems.at[4]),
    )
    loads[0].start()
    loads[1].start()
    barrier(pos)
    tick = Ticker(
        scatter_chain_process(
            plan.head_bind(pos, parts, r1s, r2s, keeps, h_refs), plan.tail_bind(pos, keeps, r2s, shards, c_refs)
        )
    )
    tick()
    tails = tail.tail_bind(pos, keeps_in, r2s_in, tshards, t_refs)

    def all_tails(step):
        for u in tails:
            getattr(u, step)()

    all_tails("load")
    gather = Ticker(gather_process(gather_units(pos, gunits, [kvlow_ref], [kvfull_ref], g_send, g_recv)))
    gather()
    gp[...] = jnp.zeros(gp.shape, F32)
    tick()
    all_tails("step1")
    base = 4 * clips
    sum_ref[...] = jnp.zeros(sum_ref.shape, F32)
    sum_ref[base : base + 2, :] = ba_ref[0:2, :]
    sum_ref[base + 2 : base + 3, :] = bc_ref[2:3, :]
    sum_ref[base + 3 : base + 4, :] = bc_ref[1:2, :]
    sum_ref[base + 5 : base + 6, :] = bc_ref[0:1, :]
    sum_ref[base + 6 : base + 7, :] = bm_ref[0:1, :]
    sum_ref[base + 7 : base + 11, :] = hsum_ref[...]

    def clip_sums(ref, base, step, grads):
        for k, g in enumerate(grads):
            for c in range(clips):
                at = base + c * step + k
                ref[at : at + 1, :] = jnp.sum(one_ref[:, c : c + 1] * g, axis=0, keepdims=True)

    clip_sums(sum_ref, 0, 4, (gpg_ref[...], gpm_ref[0], gpm_ref[1], gpm_ref[2]))
    small = Ticker(sum_process(pos, sum_ref, [lands.at[i] for i in range(3)], zland, s_send, s_recv))
    small()
    loads[0].wait()
    tick()
    ig_ref[...] = dot_nt(gq_ref[...], w_buf[:, :width])
    tick()
    gather()
    ig_ref[...] += dot_nt(gk_ref[...], w_buf[:, width : 2 * width])
    tick()
    small()
    ig_ref[...] += dot_nt(gv_ref[...], w_buf[:, 2 * width :])
    loads[2].start()
    loads[3].start()
    loads[1].wait()
    gather()
    tick()
    small()

    def finish(s):
        r = rows_at(s * patches, patches)
        xhat, rstd = normalise(x_ref[r, :].astype(F32))
        g = ig_ref[r, :]
        gp[0] += g
        gp[1] += g * xhat
        ig_ref[r, :] = late[r, :] + normalise_back(xhat, rstd, g, scale_ref[...])

    each(frames, finish)
    clip_sums(last_ref, 0, 2, (gp[0], gp[1]))
    last = Ticker(sum_process(pos, last_ref, [lands2.at[i] for i in range(3)], zland2, s_send2, s_recv2))
    last()
    small()
    tick()
    all_tails("step2")
    gather()
    last()
    tick()
    small.drain()
    last()
    tick()
    gather.drain()
    full = pltpu.make_async_copy(kvfull_ref, kv_buf, sems.at[3])
    full.start()
    last()
    tick()
    loads[2].wait()
    loads[3].wait()
    full.wait()
    kv0 = kv_buf[0].reshape(used_ref.shape[0], width)
    kv1 = kv_buf[1].reshape(used_ref.shape[0], width)
    rows_ref[...] = dot_nt(kv0, w_buf[:, :width]) + dot_nt(kv1, w_buf[:, width : 2 * width])
    last.drain()
    tick()
    mine = kv_buf[pos.y].reshape(used_ref.shape[0], width)
    kvg_ref[...] = dot_tn(used_ref[...], mine)
    sum_ref[20:21, :] = sum_ref[20:21, :] + jnp.sum(kv1.astype(F32), axis=0, keepdims=True)
    tick.drain()
    all_tails("step3")


def scatter_chain_process(heads, tails, lags=(1, 3, 4, 5, 6, 8)):
    for u in heads:
        u.send()
    yield
    total = len(heads)
    order = (
        (5, tails, "step3"), (4, tails, "step2"), (3, tails, "step1"), (2, tails, "load"), (1, heads, "step2"), (0, heads, "step1"),
    )
    for t in range(total + lags[5]):
        for i, units, step in order:
            if 0 <= t - lags[i] < total:
                getattr(units[t - lags[i]], step)()
        if t < total:
            heads[t].load()
        yield
    for u in heads:
        u.finish()


def close_call(
    patches, gq, gk, gv, x, scale, gpg, gpm, ba, bc, bm, hsum, one, used, gra, wqkv, wkv, kvlow, keeps, r2s, tail, tail_outs, part, shard_shape,
    units, gunits, ident,
):
    rows, width = x.shape
    plan = ScatterPlan([shard_shape], units)
    mt, m = tail.n, plan.n
    scratches = [tail.tail_scratch(), plan.head_scratch(), plan.tail_scratch()]
    S = jax.ShapeDtypeStruct
    full = gather_shapes([kvlow])
    least = (8, width)
    most = (4 * one.shape[1] + 16, width)
    out = pl.pallas_call(
        partial(close_kernel, patches, tail, plan, gunits, [len(s) for s in scratches]),
        out_shape=[
            S((rows, width), F32), S(most, F32), S(least, F32), S((used.shape[0], width), F32), S((used.shape[1], width), F32),
        ]
        + full
        + [S(s, F32) for s in tail_outs]
        + [S(shard_shape, F32)]
        + plan.r1_shapes
        + plan.halves
        + plan.halves,
        in_specs=[IN_VMEM] * 13 + [IN_ANY] * (4 + 2 * mt + 1),
        out_specs=[IN_VMEM] * 5 + [IN_ANY] + [IN_VMEM] * 4 + [IN_ANY] * (3 * m),
        scratch_shapes=[
            pltpu.VMEM(wqkv.shape, BF), pltpu.VMEM((rows, width), F32), pltpu.VMEM((2, patches, width), F32),
            pltpu.VMEM(full[0].shape, BF), pltpu.VMEM((3,) + most, F32), pltpu.VMEM((4,) + most, F32),
            pltpu.VMEM((3,) + least, F32), pltpu.VMEM((4,) + least, F32),
            pltpu.SemaphoreType.DMA((5,)),
        ]
        + gather_sems(gunits)
        + [pltpu.SemaphoreType.DMA((6,))] * 4
        + sum(scratches, []),
        compiler_params=pltpu.CompilerParams(collective_id=ident, has_side_effects=True, vmem_limit_bytes=VMEM_LIMIT),
        name="close",
    )(gq, gk, gv, x, scale, gpg, gpm, ba, bc, bm, hsum, one, used, gra, wqkv, wkv, kvlow, *keeps, *r2s, part)
    return out[:5], out[6:9], out[9]


GATHER_OPEN = (
    (0, None, (0, 512), "zxy"),
    (0, None, (512, 512), "zyx"),
    (0, None, (1024, 256), "zxy"),
    (1, None, None, "zyx"),
    (0, None, (1280, 448), "zxy"),
)
GATHER_ATTEND = (
    (0, None, None, "zxy"),
    (1, None, None, "zyx"),
    (2, None, (0, 640), "zxy"),
    (2, None, (640, 512), "zyx"),
)
GATHER_CROSS = (
    (0, None, (0, 256), "xyz"),
    (0, None, (256, 384), "zxy"),
    (0, None, (640, 384), "zyx"),
    (0, None, (1024, 384), "zxy"),
    (0, None, (1408, 384), "zyx"),
    (1, (0, 64), None, "xyz"),
    (0, None, (1792, 256), "zxy"),
    (0, None, (2048, 256), "zyx"),
    (1, (64, 48), None, "zxy"),
    (1, (112, 48), None, "zyx"),
    (1, (160, 32), None, "zxy"),
    (1, (192, 32), None, "zyx"),
    (1, (224, 32), None, "zxy"),
    (1, (256, 32), None, "zyx"),
)
SCATTER_EARLY = tuple((0, None, (384 * i, 384), ("xyz", "yxz")[i % 2], 0) for i in range(4))
SCATTER_LATE = (
    (0, None, (1920, 384), "yxz", 0),
    (1, (0, 48), None, "yxz", 0),
    (1, (48, 48), None, "xyz", 0),
    (1, (96, 48), None, "yxz", 0),
    (0, None, (1536, 384), "xyz", 0),
    (1, (144, 48), None, "xyz", 0),
    (1, (192, 48), None, "yxz", 0),
    (1, (240, 48), None, "xyz", 0),
)
SCATTER_MID = (
    (2, None, None, "xyz", 0),
    (1, None, None, "yxz", 0),
    (0, None, (0, 256), "xyz", 0),
    (0, None, (256, 320), "yxz", 0),
)
SCATTER_CLOSE = tuple((0, None, (256 * i, 256 if i < 6 else 192), ("xyz", "yxz")[i % 2], 0) for i in range(7))
SCATTER_KV = ((0, None, None, "xyz", 0),)
GATHER_CLOSE = ((0, None, None, "zxy"),)


def fast_body(
    tokens, cotangent, caption, null_embed, timesteps, null_mask, bucket_sizes, patch_mask, frame_counts, table, time_proj,
    self_qkv, self_out, cross_q, cross_kv, cross_out, mlp_in, mlp_out, biases, hidden_bias,
):
    frames, patches, width = tokens.shape
    heads = HEADS
    head_dim = width // heads
    clips, cap_len, _ = caption.shape
    cap_pad = -(-cap_len // 128) * 128
    rows = frames * patches
    count = frame_counts[0]
    frame_index = lax.axis_index("frames")
    patch_index = lax.axis_index("patches")
    bias_f = biases.astype(F32)
    patch_ids = patch_index * patches + jnp.arange(patches, dtype=jnp.int32)
    bucket_ends = jnp.cumsum(bucket_sizes)
    clip_ids = jnp.sum((patch_ids[:, None] >= bucket_ends[None, :]).astype(jnp.int32), axis=1)
    onehot = (clip_ids[:, None] == jnp.arange(clips, dtype=jnp.int32)[None, :]).astype(F32)
    valid = (jnp.arange(frames, dtype=jnp.int32) < count)[:, None] & (patch_mask[None, :] == 1)
    valid = valid.reshape(rows, 1).astype(F32)
    time_rows, time_cols = time_proj.shape
    features = time_features(timesteps, time_rows * lax.axis_size("patches")).astype(BF)
    own_features = lax.dynamic_slice_in_dim(features, patch_index * time_rows, time_rows, 1)
    time_part = jnp.pad(forward_dot(own_features, time_proj), ((0, 8 - clips), (0, 0)))
    used = jnp.where(null_mask[:, None, None] == 1, null_embed[None], caption)
    used = jnp.pad(used, ((0, 0), (0, cap_pad - cap_len), (0, 0))).reshape(clips * cap_pad, width)
    key_ids = jnp.arange(clips * cap_pad, dtype=jnp.int32)
    open_key = (clip_ids[:, None] == (key_ids // cap_pad)[None, :]) & (key_ids % cap_pad < cap_len)[None, :]
    cmask = jnp.where(open_key, 0.0, NEG)
    lanes = jnp.arange(width, dtype=jnp.int32)[:, None] // head_dim
    e = (lanes == jnp.arange(128, dtype=jnp.int32)[None, :]).astype(BF)
    et = jnp.concatenate([e.T, e.T], axis=0)
    info = jnp.stack([count, frame_index]).astype(jnp.int32)
    qkv_bias = jnp.concatenate([bias_f[0], jnp.zeros((width,), F32), bias_f[1]])[None]

    x = tokens.reshape(rows, width)
    cot = cotangent.reshape(rows, width)
    (nm_a, scale_a, gate_a, mods_m), (w_qkv, w_out), begun = open_call(
        patches, x, time_part, table.astype(F32), onehot, [self_qkv, self_out], GATHER_OPEN,
        [cross_q, cross_out, cross_kv], GATHER_ATTEND, 0,
    )
    (wqkv, wo, q, kvx, probs, attn, ao, resid, residb), (w_q, w_co, w_kv), begun = attend_call(
        patches, heads, nm_a, x, gate_a, w_qkv, w_out, qkv_bias, bias_f[2:3], e, et, info,
        [cross_q, cross_out, cross_kv], begun, GATHER_ATTEND, [mlp_in, mlp_out], GATHER_CROSS, 1,
    )
    (wq, wco, cq, keys, vals, lse, mixb, rc, nm_m), (w_in, w_mo) = cross_call(
        patches, heads, resid, residb, mods_m, used, cmask, w_q, w_co, w_kv, bias_f[3:4], bias_f[4:5], bias_f[5:6],
        [mlp_in, mlp_out], begun, GATHER_CROSS, 2,
    )
    mlp_shapes = [mlp_in.shape, mlp_out.shape]
    early, late = ScatterPlan(mlp_shapes, SCATTER_EARLY, 4, 2), ScatterPlan(mlp_shapes, SCATTER_LATE, 4)
    (block_out, grc, hsum, bsum_m, gp_m, dw_in, dw_mo), landed, kept = mlp_call(
        patches, nm_m, cot, valid, rc, mods_m, hidden_bias.astype(F32), bias_f[6:7], w_in, w_mo, mlp_in.shape, early, 6
    )

    def blocks(part, shard):
        return part.reshape((2, 4, 2, 2) + shard.shape)

    (gra, gai, gkv, bsum_c, gp_g, dwo, dwq, dwco), in_first, landed, kept, (kv_keep, kv_r2) = cross_back_call(
        patches, heads, grc, mixb, cq, keys, vals, lse, cmask, residb, attn, ao, gate_a, wco, wq, wo,
        kept, landed, early, mlp_in.shape, [dw_in, blocks(dw_mo, mlp_out)], late, 3,
    )
    kv_rows = clips * cap_pad // 16
    mid_shapes = [self_out.shape, cross_q.shape, cross_out.shape]
    (gq, gk, gv, bsum_a, dwqkv), (in_rest, mo_shard, kv_low), landed, kept = attend_back_call(
        patches, heads, gai, q, kvx, probs, e, et, info, nm_a, kept, landed, ScatterPlan(mlp_shapes, SCATTER_LATE), mlp_shapes,
        [blocks(dwo, self_out), blocks(dwq, cross_q), blocks(dwco, cross_out)], mid_shapes, SCATTER_MID,
        kv_keep, kv_r2, (kv_rows, width), 4,
    )
    in_shard = jnp.concatenate([in_first[:, :1536], in_rest[:, 1536:]], axis=1)
    own_used = lax.dynamic_slice_in_dim(used, patch_index * cross_kv.shape[0], cross_kv.shape[0], 1)
    (input_grad, totals, last_totals, caption_rows, cross_kv_grad), (out_shard, q_shard, co_shard), qkv_shard = close_call(
        patches, gq, gk, gv, x, scale_a, gp_g, gp_m, bsum_a, bsum_c, bsum_m, hsum.reshape(-1, width), onehot, own_used, gra, wqkv, w_kv, kv_low,
        kept, landed, ScatterPlan(mid_shapes, SCATTER_MID, 4, 4), mid_shapes, blocks(dwqkv, self_qkv), self_qkv.shape,
        SCATTER_CLOSE, GATHER_CLOSE, 5,
    )
    mod_total = jnp.concatenate(
        [last_totals.reshape(clips, 2, width), totals[: 4 * clips].reshape(clips, 4, width)], axis=1
    )
    biases_grad = totals[4 * clips : 4 * clips + 7]
    hidden_total = totals[4 * clips + 7 : 4 * clips + 11].reshape(-1)
    caption_rows = caption_rows.reshape(clips, cap_pad, width)[:, :cap_len]
    dropped = (null_mask == 1)[:, None, None]
    caption_grad = jnp.where(dropped, 0.0, caption_rows)
    null_grad = jnp.sum(jnp.where(dropped, caption_rows, 0.0), axis=0)
    table_grad = jnp.sum(mod_total, axis=0)
    own_mod = lax.dynamic_slice_in_dim(mod_total.reshape(clips, 6 * width), frame_index * time_cols, time_cols, 1)
    time_proj_grad = jnp.dot(own_features.astype(F32).T, own_mod, precision=HIGH)

    return (
        block_out.reshape(tokens.shape),
        input_grad.reshape(tokens.shape),
        caption_grad,
        null_grad,
        table_grad,
        time_proj_grad,
        qkv_shard,
        out_shard,
        q_shard,
        cross_kv_grad,
        co_shard,
        in_shard,
        mo_shard,
        biases_grad,
        hidden_total,
    )


def body(*args):
    if lax.axis_size("frames") == 2 and lax.axis_size("patches") == 16:
        return fast_body(*args)
    return plain_body(*args)


def solution(mesh):
    return jax.shard_map(
        body,
        mesh=mesh,
        in_specs=(
            P("frames", "patches", None),
            P("frames", "patches", None),
            P(),
            P(),
            P(),
            P(),
            P(),
            P("patches"),
            P("frames"),
            P(),
            P("patches", "frames"),
            P("patches", "frames"),
            P("patches", "frames"),
            P("patches", "frames"),
            P("patches", "frames"),
            P("patches", "frames"),
            P("patches", "frames"),
            P("patches", "frames"),
            P(),
            P(),
        ),
        out_specs=(
            P("frames", "patches", None),
            P("frames", "patches", None),
            P(),
            P(),
            P(),
            P("patches", "frames"),
            P("patches", "frames"),
            P("patches", "frames"),
            P("patches", "frames"),
            P("patches", "frames"),
            P("patches", "frames"),
            P("patches", "frames"),
            P("patches", "frames"),
            P(),
            P(),
        ),
        check_vma=False,
    )
```
